32 devices in a mesh: seq: 8 (over z, y), mem: 4 (over x, core).
Axes of the slice: x: 2, y: 2, z: 4, core: 2. Of those that a mesh axis runs over, the one named last changes fastest.
Arguments:
- inputs: bfloat16 [2, 8192, 1024], P(None, ('seq', 'mem')), may hold values from -6 to 6
- memory: bfloat16 [2, 8, 588, 1024], P(None, 'seq', 'mem'), may hold values from -6 to 6
- page_ids: int32 [2, 8192], replicated, may hold values from 0 to 7, as said below
- memory_length: int32 [2, 8], replicated, may hold values from 147 to 588, as said below
- cotangent: bfloat16 [2, 8192, 1024], P(None, ('seq', 'mem')), may hold values from -6 to 6
- gain_self: bfloat16 [1024], P(('seq', 'mem')), may hold values from 0.25 to 1.75
- self_query: bfloat16 [1024, 1024], P(('seq', 'mem')), may hold values from -0.25 to 0.25
- self_key: bfloat16 [1024, 1024], P(('seq', 'mem')), may hold values from -0.1875 to 0.1875
- self_value: bfloat16 [1024, 1024], P(('seq', 'mem')), may hold values from -0.1875 to 0.1875
- self_out: bfloat16 [1024, 1024], P(('seq', 'mem')), may hold values from -1.5 to 1.5
- gain_cross: bfloat16 [1024], P(('seq', 'mem')), may hold values from 0.25 to 1.75
- cross_query: bfloat16 [1024, 1024], P(('seq', 'mem')), may hold values from -0.25 to 0.25
- cross_key: bfloat16 [1024, 1024], P(('seq', 'mem')), may hold values from -0.1875 to 0.1875
- cross_value: bfloat16 [1024, 1024], P(('seq', 'mem')), may hold values from -0.1875 to 0.1875
- cross_out: bfloat16 [1024, 1024], P(('seq', 'mem')), may hold values from -1.5 to 1.5
- gain_mlp: bfloat16 [1024], P(('seq', 'mem')), may hold values from 0.25 to 1.75
- mlp_in: bfloat16 [4096, 1024], P(('seq', 'mem')), may hold values from -0.1875 to 0.1875
- mlp_out: bfloat16 [4096, 1024], P(('seq', 'mem')), may hold values from -0.1875 to 0.1875
Outputs:
- output: bfloat16 [2, 8192, 1024], P(None, ('seq', 'mem'))
- grad_inputs: float32 [2, 8192, 1024], P(None, ('seq', 'mem'))
- grad_memory: float32 [2, 8, 588, 1024], P(None, 'seq', 'mem')
- grad_gain_self: float32 [1024], P(('seq', 'mem'))
- grad_self_query: float32 [1024, 1024], P(('seq', 'mem'))
- grad_self_key: float32 [1024, 1024], P(('seq', 'mem'))
- grad_self_value: float32 [1024, 1024], P(('seq', 'mem'))
- grad_self_out: float32 [1024, 1024], P(('seq', 'mem'))
- grad_gain_cross: float32 [1024], P(('seq', 'mem'))
- grad_cross_query: float32 [1024, 1024], P(('seq', 'mem'))
- grad_cross_key: float32 [1024, 1024], P(('seq', 'mem'))
- grad_cross_value: float32 [1024, 1024], P(('seq', 'mem'))
- grad_cross_out: float32 [1024, 1024], P(('seq', 'mem'))
- grad_gain_mlp: float32 [1024], P(('seq', 'mem'))
- grad_mlp_in: float32 [4096, 1024], P(('seq', 'mem'))
- grad_mlp_out: float32 [4096, 1024], P(('seq', 'mem'))
The draws below stay inside these ranges and needn't reach their ends.
Inputs may be any that keep to these rules, and one draw needn't show every extreme that they name: `page_ids`: in each micro-batch page numbers never fall along the tokens. Cut the tokens into blocks of 1024: block 0 holds only page 0; block g (g >= 1) begins with tokens of page g - 1 and holds the first token of page g, and all its later tokens belong to page g. Each value is 147 or 588; the rows of a page's memory from memory_length on are padding.
All inputs are finite; a program needn't handle non-finite values.
Results may differ from the reference program's by a relative error of at most 0.04.
Values may be sent and summed in bfloat16 or wider, within the bound.
No kernel may reach another device: no remote copies, remote signals or barrier semaphores. Data moves between devices by JAX's collectives and lax.ppermute only.
A program may use at most 320 MiB of HBM per device.

```python
import jax
import jax.numpy as jnp
from jax import lax

D = 1024
H = 16
HEAD = 64
FF = 4096
MEM_ROWS = 588
SMALL_ROWS = 147
TOK_DEV = 256
MICRO = 2
GROUP = 1024
TOKENS = 8192
PAGES = 8
N_MEM = 4


def draw_page_ids(key, part):
    key = jax.random.fold_in(key, 7)
    groups = TOKENS // GROUP
    spill = jax.random.randint(key, (MICRO, groups), GROUP // 4, 3 * GROUP // 4 + 1)
    spill = jnp.where(jnp.arange(groups)[None, :] == 0, 0, spill)
    offsets = jnp.arange(GROUP)[None, None, :]
    base_page = jnp.arange(groups)[None, :, None] - 1
    page_number = base_page + (offsets >= spill[:, :, None]).astype(jnp.int32)
    return page_number.reshape(MICRO, TOKENS).astype(jnp.int32)


def draw_memory_length(key, part):
    key = jax.random.fold_in(key, 5)
    first_key, second_key = jax.random.split(key)
    flags = jax.random.randint(first_key, (MICRO, PAGES), 0, 2)
    chosen = jax.random.randint(second_key, (MICRO,), 0, PAGES)
    columns = jnp.arange(PAGES)[None, :]
    flags = jnp.where(columns == chosen[:, None], 1, flags)
    flags = jnp.where(columns == (chosen[:, None] + 1) % PAGES, 0, flags)
    return jnp.where(flags == 1, SMALL_ROWS, MEM_ROWS).astype(jnp.int32)


def shard_levels(rng, extent, cuts, least, top_value):
    gain, own = 1.0, jax.random.fold_in(rng, 6)
    for dim, blocks in cuts:
        steps = jnp.exp(jax.random.uniform(jax.random.fold_in(own, dim), (blocks,), jnp.float32, least / len(cuts), top_value / len(cuts)))
        gain = gain * jnp.repeat(steps, extent[dim] // blocks).reshape([-1 if axis == dim else 1 for axis in range(len(extent))])
    return gain


def normal_values(own_key, dims, scale, limit, shards=(), kind=jnp.bfloat16):
    gain = shard_levels(own_key, dims, shards, -0.22, 0.18) if shards else 1.0
    entries = jax.random.normal(own_key, dims, jnp.float32) * scale * gain
    return jnp.minimum(jnp.maximum(entries, -limit), limit).astype(kind)


def setup_inputs(seed: int = 0) -> dict:
    seeds = jax.random.split(jax.random.key(seed), 19)
    inputs = normal_values(seeds[0], (MICRO, TOKENS, D), 1.0, 6.0, ((1, 32),))
    memory = normal_values(seeds[1], (MICRO, PAGES, MEM_ROWS, D), 1.0, 6.0, ((1, 8), (2, 4)))
    page_ids = draw_page_ids(jax.random.fold_in(seeds[18], 71), 0)
    memory_length = draw_memory_length(jax.random.fold_in(seeds[18], 71), 0)
    cotangent = normal_values(seeds[4], (MICRO, TOKENS, D), 1.0, 6.0, ((1, 32),))
    gain_self = jnp.clip(1.0 + 0.15 * jax.random.normal(seeds[5], (D,), jnp.float32), 0.25, 1.75).astype(jnp.bfloat16)
    self_query = normal_values(seeds[6], (D, D), (D // 2) ** -0.5, 0.25, ((0, 32),))
    self_key = normal_values(seeds[7], (D, D), D ** -0.5, 0.1875, ((0, 32),))
    self_value = normal_values(seeds[8], (D, D), D ** -0.5, 0.1875, ((0, 32),))
    self_out = normal_values(seeds[9], (D, D), (D // 64) ** -0.5, 1.5, ((0, 32),))
    gain_cross = jnp.clip(1.0 + 0.15 * jax.random.normal(seeds[10], (D,), jnp.float32), 0.25, 1.75).astype(jnp.bfloat16)
    cross_query = normal_values(seeds[11], (D, D), (D // 2) ** -0.5, 0.25, ((0, 32),))
    cross_key = normal_values(seeds[12], (D, D), D ** -0.5, 0.1875, ((0, 32),))
    cross_value = normal_values(seeds[13], (D, D), D ** -0.5, 0.1875, ((0, 32),))
    cross_out = normal_values(seeds[14], (D, D), (D // 64) ** -0.5, 1.5, ((0, 32),))
    gain_mlp = jnp.clip(1.0 + 0.15 * jax.random.normal(seeds[15], (D,), jnp.float32), 0.25, 1.75).astype(jnp.bfloat16)
    mlp_in = normal_values(seeds[16], (FF, D), D ** -0.5, 0.1875, ((0, 32),))
    mlp_out = normal_values(seeds[17], (FF, D), (FF // 4) ** -0.5, 0.1875, ((0, 32),))
    return {"inputs": inputs, "memory": memory, "page_ids": page_ids, "memory_length": memory_length, "cotangent": cotangent, "gain_self": gain_self, "self_query": self_query, "self_key": self_key, "self_value": self_value, "self_out": self_out, "gain_cross": gain_cross, "cross_query": cross_query, "cross_key": cross_key, "cross_value": cross_value, "cross_out": cross_out, "gain_mlp": gain_mlp, "mlp_in": mlp_in, "mlp_out": mlp_out}


@jax.custom_vjp
def low(v):
    return lax.optimization_barrier(v.astype(jnp.bfloat16)).astype(jnp.float32)

@jax.custom_vjp
def low_back(v):
    return v

def low_keep(v):
    return (low(v), None)

def low_pass(kept, grad):
    return (grad,)

def back_keep(v):
    return (v, None)

def back_low(kept, grad):
    return (low(grad),)
low.defvjp(low_keep, low_pass)
low_back.defvjp(back_keep, back_low)

def matmul(left, right):
    return jnp.dot(left, right, precision=lax.Precision.HIGHEST)

def layer_norm(tensor, scales):
    average = lax.optimization_barrier(jnp.mean(tensor, axis=-1, keepdims=True))
    centered = tensor - average
    variance = lax.optimization_barrier(jnp.mean(centered * centered, axis=-1, keepdims=True))
    return centered * lax.rsqrt(variance + 1e-05) * scales

def exact_gelu(tensor):
    return jax.nn.gelu(tensor, approximate=False)

def attend(queries, key_rows, values, allowed):
    row_count = queries.shape[0]
    key_count = key_rows.shape[0]
    query_heads = queries.reshape(row_count, H, HEAD)
    key_heads = key_rows.reshape(key_count, H, HEAD)
    value_heads = values.reshape(key_count, H, HEAD)
    scores = low_back(jnp.einsum('rhd,khd->hrk', query_heads, key_heads, precision=lax.Precision.HIGHEST) * 0.125)
    masked = jnp.where(allowed[None], scores, -1e+30)
    rowmax = lax.optimization_barrier(jnp.max(masked, axis=-1, keepdims=True))
    weights = jnp.where(allowed[None], jnp.exp(masked - rowmax), 0.0)
    totals = lax.optimization_barrier(jnp.sum(weights, axis=-1))
    summed = low_back(jnp.einsum('hrk,khd->rhd', low(weights), value_heads, precision=lax.Precision.HIGHEST))
    return (summed / totals.T[:, :, None]).reshape(row_count, H * HEAD)

def forward_micro(x_rows, memory_rows, page_row, length_row, params):
    gain_one, query_w, key_w, value_w, out_w, gain_two, cquery_w, ckey_w, cvalue_w, cout_w, gain_three, inner_w, outer_w = params
    group = TOK_DEV * N_MEM
    groups = TOKENS // group
    low_one = low(layer_norm(x_rows, gain_one))
    queries = low(low_back(matmul(low_one, query_w)))
    key_rows = low(low_back(matmul(low_one, key_w)))
    values = low(low_back(matmul(low_one, value_w)))
    key_padded = jnp.concatenate([jnp.zeros((group, D), jnp.float32), key_rows], axis=0)
    value_padded = jnp.concatenate([jnp.zeros((group, D), jnp.float32), values], axis=0)
    ids_padded = jnp.concatenate([-jnp.ones((group,), jnp.int32), page_row], axis=0)

    def self_block(group_index):
        row_start = (group_index * group).astype(jnp.int32)
        block_q = lax.dynamic_slice_in_dim(queries, row_start, group, 0)
        block_k = lax.dynamic_slice_in_dim(key_padded, row_start, 2 * group, 0)
        block_v = lax.dynamic_slice_in_dim(value_padded, row_start, 2 * group, 0)
        query_ids = lax.dynamic_slice_in_dim(page_row, row_start, group, 0)
        key_ids = lax.dynamic_slice_in_dim(ids_padded, row_start, 2 * group, 0)
        query_pos = row_start + jnp.arange(group, dtype=jnp.int32)
        key_pos = row_start - group + jnp.arange(2 * group, dtype=jnp.int32)
        allowed = (key_ids[None, :] == query_ids[:, None]) & (key_pos[None, :] <= query_pos[:, None])
        return attend(block_q, block_k, block_v, allowed)
    self_raw = lax.map(jax.checkpoint(self_block), jnp.arange(groups, dtype=jnp.int32)).reshape(TOKENS, D)
    self_low = low(low_back(self_raw))
    after_self = x_rows + low_back(matmul(self_low, out_w))
    low_two = low(layer_norm(after_self, gain_two))
    cross_q = low(low_back(matmul(low_two, cquery_w)))
    memory_flat = memory_rows.reshape(PAGES * MEM_ROWS, D)
    memory_key = low(low_back(matmul(memory_flat, ckey_w))).reshape(PAGES, MEM_ROWS, D)
    memory_value = low(low_back(matmul(memory_flat, cvalue_w))).reshape(PAGES, MEM_ROWS, D)
    mkey_padded = jnp.concatenate([jnp.zeros((1, MEM_ROWS, D), jnp.float32), memory_key], axis=0)
    mvalue_padded = jnp.concatenate([jnp.zeros((1, MEM_ROWS, D), jnp.float32), memory_value], axis=0)
    length_padded = jnp.concatenate([jnp.zeros((1,), jnp.int32), length_row], axis=0)

    def cross_block(group_index):
        row_start = (group_index * group).astype(jnp.int32)
        page_start = group_index.astype(jnp.int32)
        block_q = lax.dynamic_slice_in_dim(cross_q, row_start, group, 0)
        block_k = lax.dynamic_slice_in_dim(mkey_padded, page_start, 2, 0).reshape(2 * MEM_ROWS, D)
        block_v = lax.dynamic_slice_in_dim(mvalue_padded, page_start, 2, 0).reshape(2 * MEM_ROWS, D)
        page_lens = lax.dynamic_slice_in_dim(length_padded, page_start, 2, 0)
        key_page = page_start - 1 + jnp.repeat(jnp.arange(2, dtype=jnp.int32), MEM_ROWS)
        key_place = jnp.tile(jnp.arange(MEM_ROWS, dtype=jnp.int32), 2)
        key_live = key_place < jnp.repeat(page_lens, MEM_ROWS)
        query_ids = lax.dynamic_slice_in_dim(page_row, row_start, group, 0)
        allowed = (query_ids[:, None] == key_page[None, :]) & key_live[None, :]
        return attend(block_q, block_k, block_v, allowed)
    cross_raw = lax.map(jax.checkpoint(cross_block), jnp.arange(groups, dtype=jnp.int32)).reshape(TOKENS, D)
    cross_low = low(low_back(cross_raw))
    after_cross = after_self + low_back(matmul(cross_low, cout_w))
    low_three = low(layer_norm(after_cross, gain_three))
    hidden_pre = low_back(matmul(low_three, inner_w.T))
    activ = low(exact_gelu(hidden_pre))
    return after_cross + low_back(matmul(activ, outer_w))

def reference(inputs, memory, page_ids, memory_length, cotangent, gain_self, self_query, self_key, self_value, self_out, gain_cross, cross_query, cross_key, cross_value, cross_out, gain_mlp, mlp_in, mlp_out):
    params = tuple((weight.astype(jnp.float32) for weight in (gain_self, self_query, self_key, self_value, self_out, gain_cross, cross_query, cross_key, cross_value, cross_out, gain_mlp, mlp_in, mlp_out)))
    x_all = inputs.astype(jnp.float32)
    memory_all = memory.astype(jnp.float32)

    def forward(x_stack, memory_stack, weights):
        return jnp.stack([forward_micro(x_stack[micro_index], memory_stack[micro_index], page_ids[micro_index], memory_length[micro_index], weights) for micro_index in range(MICRO)])
    result, pullback = jax.vjp(forward, x_all, memory_all, params)
    grad_x, grad_mem, grad_params = pullback(cotangent.astype(jnp.float32))
    return (result.astype(jnp.bfloat16), grad_x, grad_mem, grad_params[0], grad_params[1], grad_params[2], grad_params[3], grad_params[4], grad_params[5], grad_params[6], grad_params[7], grad_params[8], grad_params[9], grad_params[10], grad_params[11], grad_params[12])
```

```python
import functools
import jax
import jax.numpy as jnp
import numpy as np
from jax import lax
from jax.experimental import pallas as pl
from jax.experimental.pallas import tpu as pltpu
from jax.sharding import PartitionSpec as P

HEAD = 64
BF = jnp.bfloat16
F32 = jnp.float32
LOWEST = -1e30


def head_lanes(rows, width):
    return lax.broadcasted_iota(jnp.int32, (rows, width), 1) // HEAD


def one_head(block, lanes, head):
    return jnp.where(lanes == head, block, jnp.zeros_like(block))


def dot_nt(left, right):
    return lax.dot_general(left, right, (((1,), (1,)), ((), ())), preferred_element_type=F32)


def dot_nn(left, right):
    return lax.dot_general(left, right, (((1,), (0,)), ((), ())), preferred_element_type=F32)


def dot_tn(left, right):
    return lax.dot_general(left, right, (((0,), (0,)), ((), ())), preferred_element_type=F32)


def self_range(p, rows, blocks, spill, prev_spill):
    first = jnp.where(p * rows < spill, prev_spill // rows, blocks + spill // rows)
    return first, blocks + p + 1


def self_allowed(query, key, extent, spill, prev_spill):
    first = jnp.where(query < spill, prev_spill, extent + spill)
    return (key >= first) & (key <= extent + query)


def cross_allowed(query, place, side, spill, length, me, padded, real):
    part = place // padded
    inner = place - part * padded
    row = (part ^ me) * real + inner
    return (inner < real) & (row < length) & ((query < spill) == (side == 0))


def self_forward_kernel(rows, blocks, heads, sc, qkv, kvp, o_ref, lse_ref, k_scr, v_scr, s_scr, mx, tot):
    width = heads * HEAD
    extent = rows * blocks
    me, spill, prev_spill = sc[0], sc[1], sc[2]
    lanes = head_lanes(rows, width)

    def place(b):
        return pl.multiple_of((b ^ me) * rows, rows)

    first_used, _ = self_range(0, rows, blocks, spill, prev_spill)

    @pl.loop(first_used, 2 * blocks)
    def _(kb):
        def fill(keys, values):
            k_scr[kb] = keys
            for h in range(heads):
                v_scr[kb, h * rows : (h + 1) * rows, :] = one_head(values, lanes, h)

        @pl.when(kb < blocks)
        def _():
            at = pl.ds(place(kb), rows)
            fill(kvp[at, 0:width], kvp[at, width : 2 * width])

        @pl.when(kb >= blocks)
        def _():
            at = pl.ds(place(kb - blocks), rows)
            fill(qkv[at, width : 2 * width], qkv[at, 2 * width : 3 * width])

    @pl.loop(0, blocks)
    def _(p):
        q = qkv[pl.ds(place(p), rows), 0:width] * jnp.asarray(0.125, BF)
        mx[...] = jnp.full(mx.shape, LOWEST, F32)
        tot[...] = jnp.zeros(tot.shape, F32)
        first, last = self_range(p, rows, blocks, spill, prev_spill)
        query = p * rows + lax.broadcasted_iota(jnp.int32, (rows, 1), 0)

        @pl.loop(first, last)
        def _(kb):
            key = kb * rows + lax.broadcasted_iota(jnp.int32, (1, rows), 1)
            allowed = self_allowed(query, key, extent, spill, prev_spill)
            k = k_scr[kb]
            for h in range(heads):
                s = dot_nt(one_head(q, lanes, h), k)
                s = jnp.where(allowed, s, LOWEST)
                s_scr[kb, h] = s
                mx[h] = jnp.maximum(mx[h], s)

        for h in range(heads):
            mx[h, :, 0:1] = jnp.max(mx[h], axis=1, keepdims=True)

        def weigh(kb, acc):
            parts = []
            for h in range(heads):
                e = jnp.exp(s_scr[kb, h] - mx[h, :, 0:1])
                tot[h] += e
                parts.append(e.astype(BF))
            return acc + dot_nn(jnp.concatenate(parts, axis=1), v_scr[kb])

        acc = lax.fori_loop(first, last, weigh, jnp.zeros((rows, width), F32))
        finish(p, place(p), rows, heads, acc, mx, tot, lanes, o_ref, lse_ref)


def finish(p, start, rows, heads, acc, mx, tot, lanes, o_ref, lse_ref):
    over = jnp.zeros((rows, 128), F32)
    inverse = jnp.zeros(acc.shape, F32)
    slim = lax.broadcasted_iota(jnp.int32, (rows, 128), 1)
    for h in range(heads):
        total = jnp.sum(tot[h], axis=1, keepdims=True)
        inverse = jnp.where(lanes == h, 1.0 / total, inverse)
        over = jnp.where(slim == h, mx[h, :, 0:1] + jnp.log(total), over)
    o_ref[pl.ds(start, rows), :] = (acc * inverse).astype(BF)
    lse_ref[:, pl.ds(pl.multiple_of(p * rows, rows), rows)] = over.T[0:8, :]


def cross_forward_kernel(rows, blocks, heads, padded, real, sc, q_ref, kv0, kv1, o_ref, lse_ref, v_scr, s_scr, mx, tot):
    width = heads * HEAD
    keys = kv0.shape[0]
    me, spill = sc[0], sc[1]
    lanes = head_lanes(rows, width)
    key_lanes = head_lanes(keys, width)
    kvs = (kv0, kv1)

    def place(b):
        return pl.multiple_of((b ^ me) * rows, rows)

    for side in range(2):
        values = kvs[side][:, width : 2 * width]
        for h in range(heads):
            v_scr[side, h * keys : (h + 1) * keys, :] = one_head(values, key_lanes, h)
    spot = lax.broadcasted_iota(jnp.int32, (1, keys), 1)

    @pl.loop(0, blocks)
    def _(p):
        q = q_ref[pl.ds(place(p), rows), :] * jnp.asarray(0.125, BF)
        mx[...] = jnp.full(mx.shape, LOWEST, F32)
        tot[...] = jnp.zeros(tot.shape, F32)
        query = p * rows + lax.broadcasted_iota(jnp.int32, (rows, 1), 0)
        reads = (p * rows < spill, (p + 1) * rows > spill)
        for side in range(2):

            @pl.when(reads[side])
            def _():
                allowed = cross_allowed(query, spot, side, spill, sc[2 + side], me, padded, real)
                k = kvs[side][:, 0:width]
                for h in range(heads):
                    s = dot_nt(one_head(q, lanes, h), k)
                    s = jnp.where(allowed, s, LOWEST)
                    s_scr[side, h] = s
                    mx[h] = jnp.maximum(mx[h], jnp.max(s, axis=1, keepdims=True))

        def weigh(side, acc):
            parts = []
            for h in range(heads):
                e = jnp.exp(s_scr[side, h] - mx[h, :, 0:1])
                tot[h] += e
                parts.append(e.astype(BF))
            return acc + dot_nn(jnp.concatenate(parts, axis=1), v_scr[side])

        first = jnp.where(reads[0], 0, 1)
        last = jnp.where(reads[1], 2, 1)
        acc = lax.fori_loop(first, last, weigh, jnp.zeros((rows, width), F32))
        finish(p, place(p), rows, heads, acc, mx, tot, lanes, o_ref, lse_ref)


def spread(p, at, rows, heads, q, g, o_ref, lse_ref, lanes, q_cat, g_cat, stat):
    weighted = (g.astype(F32) * o_ref[at, :].astype(F32)).T
    for h in range(heads):
        q_cat[h * rows : (h + 1) * rows, :] = one_head(q, lanes, h)
        g_cat[h * rows : (h + 1) * rows, :] = one_head(g, lanes, h)
        stat[heads + h : heads + h + 1, :] = jnp.sum(weighted[h * HEAD : (h + 1) * HEAD, :], axis=0, keepdims=True)
    stat[0:heads, :] = lse_ref[0:heads, pl.ds(pl.multiple_of(p * rows, rows), rows)]


def back_block(rows, heads, k, v, allowed, q_cat, g_cat, stat, w_scr, ds_wide, ds_tall):
    count = k.shape[0]
    for h in range(heads):
        span = slice(h * rows, (h + 1) * rows)
        s = dot_nt(k, q_cat[span, :])
        e = jnp.where(allowed, jnp.exp(s - stat[h : h + 1, :]), 0.0)
        de = dot_nt(v, g_cat[span, :])
        ds = (e * (de - stat[heads + h : heads + h + 1, :])).astype(BF)
        w_scr[:, span] = e.astype(BF)
        ds_wide[:, span] = ds
        ds_tall[h * count : (h + 1) * count, :] = ds


def self_backward_kernel(rows, blocks, heads, sc, qkv, kvp, o_ref, g_ref, lse_ref, dq_ref, dkv_ref, dprev_ref,
                         kv_scr, k_cat, dkv_scr, q_cat, g_cat, stat, w_scr, ds_wide, ds_tall):
    width = heads * HEAD
    extent = rows * blocks
    me, spill, prev_spill = sc[0], sc[1], sc[2]
    lanes = head_lanes(rows, width)

    def place(b):
        return pl.multiple_of((b ^ me) * rows, rows)

    first_used, _ = self_range(0, rows, blocks, spill, prev_spill)

    @pl.loop(0, 2 * blocks)
    def _(kb):
        dkv_scr[kb] = jnp.zeros(dkv_scr.shape[1:], F32)

    @pl.loop(first_used, 2 * blocks)
    def _(kb):
        def fill(pair):
            kv_scr[kb] = pair
            scaled = pair[:, 0:width] * jnp.asarray(0.125, BF)
            for h in range(heads):
                k_cat[kb, h * rows : (h + 1) * rows, :] = one_head(scaled, lanes, h)

        @pl.when(kb < blocks)
        def _():
            fill(kvp[pl.ds(place(kb), rows), :])

        @pl.when(kb >= blocks)
        def _():
            fill(qkv[pl.ds(place(kb - blocks), rows), width : 3 * width])

    @pl.loop(0, blocks)
    def _(p):
        at = pl.ds(place(p), rows)
        q = qkv[at, 0:width] * jnp.asarray(0.125, BF)
        g = g_ref[at, :]
        spread(p, at, rows, heads, q, g, o_ref, lse_ref, lanes, q_cat, g_cat, stat)
        first, last = self_range(p, rows, blocks, spill, prev_spill)
        query = p * rows + lax.broadcasted_iota(jnp.int32, (1, rows), 1)

        def step(kb, dq):
            key = kb * rows + lax.broadcasted_iota(jnp.int32, (rows, 1), 0)
            allowed = self_allowed(query, key, extent, spill, prev_spill)
            back_block(rows, heads, kv_scr[kb, :, 0:width], kv_scr[kb, :, width : 2 * width], allowed,
                       q_cat, g_cat, stat, w_scr, ds_wide, ds_tall)
            dkv_scr[kb, :, 0:width] += dot_nn(ds_wide[...], q_cat[...])
            dkv_scr[kb, :, width : 2 * width] += dot_nn(w_scr[...], g_cat[...])
            return dq + dot_tn(ds_tall[...], k_cat[kb])

        dq = lax.fori_loop(first, last, step, jnp.zeros((rows, width), F32))
        dq_ref[at, :] = dq.astype(BF)

    @pl.loop(0, blocks)
    def _(b):
        at = pl.ds(place(b), rows)
        dprev_ref[at, :] = dkv_scr[b].astype(BF)
        dkv_ref[at, :] = dkv_scr[blocks + b].astype(BF)


def cross_backward_kernel(rows, blocks, heads, padded, real, pieces, sc, q_ref, kv0, kv1, o_ref, g_ref, lse_ref,
                          dq_ref, dkv0_ref, dkv1_ref, k_cat, dkv_scr, q_cat, g_cat, stat, w_scr, ds_wide, ds_tall):
    width = heads * HEAD
    keys = kv0.shape[0]
    step_keys = keys // pieces
    me, spill = sc[0], sc[1]
    lanes = head_lanes(rows, width)
    key_lanes = head_lanes(step_keys, width)
    kvs = (kv0, kv1)

    def place(b):
        return pl.multiple_of((b ^ me) * rows, rows)

    dkv_scr[...] = jnp.zeros(dkv_scr.shape, F32)
    for side in range(2):
        for piece in range(pieces):
            scaled = kvs[side][piece * step_keys : (piece + 1) * step_keys, 0:width] * jnp.asarray(0.125, BF)
            for h in range(heads):
                k_cat[side * pieces + piece, h * step_keys : (h + 1) * step_keys, :] = one_head(scaled, key_lanes, h)

    @pl.loop(0, blocks)
    def _(p):
        at = pl.ds(place(p), rows)
        q = q_ref[at, :] * jnp.asarray(0.125, BF)
        spread(p, at, rows, heads, q, g_ref[at, :], o_ref, lse_ref, lanes, q_cat, g_cat, stat)
        query = p * rows + lax.broadcasted_iota(jnp.int32, (1, rows), 1)
        reads = (p * rows < spill, (p + 1) * rows > spill)
        first = jnp.where(reads[0], 0, pieces)
        last = jnp.where(reads[1], 2 * pieces, pieces)

        def step(kb, dq):
            side = kb // pieces
            at_key = pl.ds(pl.multiple_of((kb - side * pieces) * step_keys, step_keys), step_keys)
            spot = (kb - side * pieces) * step_keys + lax.broadcasted_iota(jnp.int32, (step_keys, 1), 0)
            length = jnp.where(side == 0, sc[2], sc[3])
            allowed = cross_allowed(query, spot, side, spill, length, me, padded, real)
            is_prev = side == 0
            pair = jnp.where(is_prev, kv0[at_key, :], kv1[at_key, :])
            back_block(rows, heads, pair[:, 0:width], pair[:, width : 2 * width], allowed,
                       q_cat, g_cat, stat, w_scr, ds_wide, ds_tall)
            dkv_scr[kb, :, 0:width] += dot_nn(ds_wide[...], q_cat[...])
            dkv_scr[kb, :, width : 2 * width] += dot_nn(w_scr[...], g_cat[...])
            return dq + dot_tn(ds_tall[...], k_cat[kb])

        dq = lax.fori_loop(first, last, step, jnp.zeros((rows, width), F32))
        dq_ref[at, :] = dq.astype(BF)

    for piece in range(pieces):
        span = slice(piece * step_keys, (piece + 1) * step_keys)
        dkv0_ref[span, :] = dkv_scr[piece].astype(BF)
        dkv1_ref[span, :] = dkv_scr[pieces + piece].astype(BF)


def call(kernel, scalars, arrays, outs, scratch, flops):
    moved = sum(a.size * a.dtype.itemsize for a in (*arrays, *jax.tree.leaves(outs)))
    vmem = pl.BlockSpec(memory_space=pltpu.VMEM)
    return pl.pallas_call(
        kernel,
        out_shape=outs,
        in_specs=[pl.BlockSpec(memory_space=pltpu.SMEM)] + [vmem] * len(arrays),
        out_specs=jax.tree.map(lambda _: vmem, outs),
        scratch_shapes=scratch,
        compiler_params=pltpu.CompilerParams(vmem_limit_bytes=48 * 2**20),
        cost_estimate=pl.CostEstimate(flops=flops, bytes_accessed=moved, transcendentals=flops // 256),
    )(scalars, *arrays)


def self_forward(scalars, qkv, kvp, blocks):
    extent = qkv.shape[0]
    rows = extent // blocks
    width = qkv.shape[1] // 3
    heads = width // HEAD
    return call(
        functools.partial(self_forward_kernel, rows, blocks, heads),
        scalars,
        (qkv, kvp),
        [jax.ShapeDtypeStruct((extent, width), BF), jax.ShapeDtypeStruct((8, extent), F32)],
        [
            pltpu.VMEM((2 * blocks, rows, width), BF),
            pltpu.VMEM((2 * blocks, heads * rows, width), BF),
            pltpu.VMEM((2 * blocks, heads, rows, rows), F32),
            pltpu.VMEM((heads, rows, rows), F32),
            pltpu.VMEM((heads, rows, rows), F32),
        ],
        extent * extent * heads * 16 * HEAD,
    )


def cross_forward(scalars, q, kv0, kv1, blocks, real):
    extent, width = q.shape
    rows = extent // blocks
    heads = width // HEAD
    keys = kv0.shape[0]
    return call(
        functools.partial(cross_forward_kernel, rows, blocks, heads, keys // blocks, real),
        scalars,
        (q, kv0, kv1),
        [jax.ShapeDtypeStruct((extent, width), BF), jax.ShapeDtypeStruct((8, extent), F32)],
        [
            pltpu.VMEM((2, heads * keys, width), BF),
            pltpu.VMEM((2, heads, rows, keys), F32),
            pltpu.VMEM((heads, rows, keys), F32),
            pltpu.VMEM((heads, rows, keys), F32),
        ],
        extent * keys * heads * 16 * HEAD,
    )


def back_scratch(rows, heads, width, keys):
    return [
        pltpu.VMEM((heads * rows, width), BF),
        pltpu.VMEM((heads * rows, width), BF),
        pltpu.VMEM((8, rows), F32),
        pltpu.VMEM((keys, heads * rows), BF),
        pltpu.VMEM((keys, heads * rows), BF),
        pltpu.VMEM((heads * keys, rows), BF),
    ]


def self_backward(scalars, qkv, kvp, o, g, lse, blocks):
    extent = qkv.shape[0]
    rows = extent // blocks
    width = qkv.shape[1] // 3
    heads = width // HEAD
    return call(
        functools.partial(self_backward_kernel, rows, blocks, heads),
        scalars,
        (qkv, kvp, o, g, lse),
        [
            jax.ShapeDtypeStruct((extent, width), BF),
            jax.ShapeDtypeStruct((extent, 2 * width), BF),
            jax.ShapeDtypeStruct((extent, 2 * width), BF),
        ],
        [
            pltpu.VMEM((2 * blocks, rows, 2 * width), BF),
            pltpu.VMEM((2 * blocks, heads * rows, width), BF),
            pltpu.VMEM((2 * blocks, rows, 2 * width), F32),
        ]
        + back_scratch(rows, heads, width, rows),
        extent * extent * heads * 40 * HEAD,
    )


def cross_backward(scalars, q, kv0, kv1, o, g, lse, blocks, real, pieces=2):
    extent, width = q.shape
    rows = extent // blocks
    heads = width // HEAD
    keys = kv0.shape[0]
    step_keys = keys // pieces
    return call(
        functools.partial(cross_backward_kernel, rows, blocks, heads, keys // blocks, real, pieces),
        scalars,
        (q, kv0, kv1, o, g, lse),
        [
            jax.ShapeDtypeStruct((extent, width), BF),
            jax.ShapeDtypeStruct((keys, 2 * width), BF),
            jax.ShapeDtypeStruct((keys, 2 * width), BF),
        ],
        [
            pltpu.VMEM((2 * pieces, heads * step_keys, width), BF),
            pltpu.VMEM((2 * pieces, step_keys, 2 * width), F32),
        ]
        + back_scratch(rows, heads, width, step_keys),
        extent * keys * heads * 40 * HEAD,
    )


D = 1024
MICRO = 2


def product(left, right):
    return dot_nn(left, right)


def product_t(left, right):
    return dot_nt(left, right)


def outer_sum(left, right):
    return dot_tn(left, right)


def flip(block, axis, bit):
    return lax.ppermute(block, axis, [(i, i ^ bit) for i in range(lax.axis_size(axis))])


def shifted(block, distance):
    devices = range(lax.axis_size("seq"))
    route = [(i - distance, i) for i in devices if i - distance in devices]
    return lax.ppermute(block, "seq", route)


def group_pieces(own):
    far = flip(own, "mem", 2)
    near = flip(own, "mem", 1)
    return [own, near, far, flip(far, "mem", 1)]


def group_rows(own):
    return jnp.concatenate(group_pieces(own), axis=0)


def group_near(part):
    rows = part.shape[0] // 4
    slots = [part[i * rows : (i + 1) * rows] for i in range(4)]
    far = slots[2].astype(F32) + flip(slots[3], "mem", 1).astype(F32)
    near = slots[0].astype(F32) + flip(slots[1], "mem", 1).astype(F32)
    return near, far.astype(BF)


def group_far(near, far):
    return near + flip(far, "mem", 2).astype(F32)


def to_heads(pieces):
    rows = pieces[0].shape[0]
    far = flip(jnp.concatenate([pieces[2], pieces[3]], axis=0), "mem", 2)
    near = flip(pieces[1], "mem", 1)
    last = flip(far[rows:], "mem", 1)
    return [pieces[0], near, far[:rows], last]


def to_tokens(part):
    rows = part.shape[0] // 4
    far = flip(part[2 * rows :], "mem", 2)
    near = flip(part[rows : 2 * rows], "mem", 1)
    last = flip(far[rows:], "mem", 1)
    return [part[:rows], near, far[:rows], last]


def split_columns(tensor, me):
    width = tensor.shape[1] // 4
    return [lax.dynamic_slice_in_dim(tensor, (me ^ k) * width, width, 1) for k in range(4)]


def join_pieces(pieces, me, axis):
    odd = (me & 1) == 1
    high = (me & 2) == 2
    low_pair = [jnp.where(odd, pieces[1 - i], pieces[i]) for i in range(2)]
    high_pair = [jnp.where(odd, pieces[3 - i], pieces[2 + i]) for i in range(2)]
    ordered = [jnp.where(high, high_pair[i], low_pair[i]) for i in range(2)]
    ordered += [jnp.where(high, low_pair[i], high_pair[i]) for i in range(2)]
    return jnp.concatenate(ordered, axis=axis)


def seq_bits():
    count = lax.axis_size("seq")
    return [1 << i for i in reversed(range(count.bit_length() - 1))]


def seq_offsets(bits):
    offsets = [0]
    for bit in bits:
        offsets = offsets + [o ^ bit for o in offsets]
    return offsets


def seq_stage(blocks, bit):
    return blocks + [flip(b, "seq", bit) for b in blocks]


def seq_slots(block, bits):
    blocks = [block]
    for bit in bits:
        blocks = seq_stage(blocks, bit)
    return blocks


def assemble_kernel(rows, offsets, at, *refs):
    out = refs[len(offsets)]
    for ref, offset in zip(refs, offsets):
        out[pl.ds(pl.multiple_of((at[0] ^ offset) * rows, rows), rows), :] = ref[...]


def assemble(blocks, seq, bits):
    offsets = seq_offsets(bits)
    rows, columns = blocks[0].shape
    size = len(blocks) * rows
    out = jax.ShapeDtypeStruct((size, columns), blocks[0].dtype)
    return call(functools.partial(assemble_kernel, rows, offsets), seq.reshape(1), blocks, out, [], 0)


def reorder_kernel(rows, offsets, at, grad, out):
    for i, offset in enumerate(offsets):
        start = pl.multiple_of((at[0] ^ offset) * rows, rows)
        out[i * rows : (i + 1) * rows, :] = grad[pl.ds(start, rows), :].astype(BF)


def reorder(grad, seq, bits):
    offsets = seq_offsets(bits)
    rows = grad.shape[0] // len(offsets)
    out = jax.ShapeDtypeStruct(grad.shape, BF)
    return call(functools.partial(reorder_kernel, rows, offsets), seq.reshape(1), (grad,), out, [], 0)


def seq_reduce(tensor, bits):
    for bit in reversed(bits):
        cut = tensor.shape[0] // 2
        theirs = flip(tensor[cut:].astype(BF), "seq", bit)
        tensor = tensor[:cut].astype(F32) + theirs.astype(F32)
    return tensor


def normal_parts(tensor):
    average = jnp.mean(tensor, axis=-1, keepdims=True)
    centered = tensor - average
    scale = lax.rsqrt(jnp.mean(centered * centered, axis=-1, keepdims=True) + 1e-05)
    return centered * scale, scale


def normal_back(plain, scale, grad):
    inner = jnp.mean(grad * plain, axis=-1, keepdims=True)
    return scale * (grad - jnp.mean(grad, axis=-1, keepdims=True) - plain * inner)


def gelu_parts(pre):
    size = jnp.abs(pre)
    t = 1.0 / (1.0 + (0.3275911 * 0.7071067811865476) * size)
    poly = ((((1.061405429 * t - 1.453152027) * t + 1.421413741) * t - 0.284496736) * t + 0.254829592) * t
    bell = jnp.exp(-0.5 * pre * pre)
    tail = 0.5 * poly * bell
    cdf = jnp.where(pre < 0.0, tail, 1.0 - tail)
    return cdf, bell


def gelu(pre):
    cdf, _ = gelu_parts(pre)
    return pre * cdf


def gelu_slope(pre):
    cdf, bell = gelu_parts(pre)
    return cdf + pre * bell * 0.3989422804014327


def interleave(streams, aside):
    held = [next(s) for s in streams]
    results = [None] * len(streams)
    turn = 0
    ticks = 0
    while True:
        mark = None
        try:
            mark = streams[turn].send(held[turn])
        except StopIteration as end:
            results[turn] = end.value
        other = (turn + 1) % len(streams)
        if mark is not None:
            ticks += 1
            if results[other] is None:
                held[other], mark = lax.optimization_barrier((held[other], mark))
            if ticks in aside:
                mark = aside[ticks](mark)
            held[turn] = streams[turn].send(mark)
        if results[other] is None:
            turn = other
        elif results[turn] is not None:
            return results


def shards(
    inputs,
    memory,
    page_ids,
    memory_length,
    cotangent,
    gain_self,
    self_query,
    self_key,
    self_value,
    self_out,
    gain_cross,
    cross_query,
    cross_key,
    cross_value,
    cross_out,
    gain_mlp,
    mlp_in,
    mlp_out,
):
    seq = lax.axis_index("seq")
    me = lax.axis_index("mem")
    odd = me & 1
    blocks = lax.axis_size("mem")
    tok = inputs.shape[1]
    group = tok * blocks
    real = memory.shape[2]
    padded = -(-real // 16) * 16
    wrows = self_query.shape[0]
    bits = seq_bits()
    turned = bits[:-2] + [bits[-1], bits[-2]]
    half = D // 2

    def gain_rows(gain, weight):
        return (weight.astype(F32) * gain.astype(F32)[:, None]).astype(BF)

    def head_weights(parts):
        split = [split_columns(part, me) for part in parts]
        pieces = [jnp.concatenate([s[k] for s in split], axis=1) for k in range(4)]
        return join_pieces(to_heads(pieces), me, 0)

    def halves(tensor):
        return [lax.dynamic_slice_in_dim(tensor, (odd ^ k) * half, half, 1) for k in range(2)]

    def join_halves(own, other):
        return jnp.concatenate([jnp.where(odd == 0, own, other), jnp.where(odd == 0, other, own)], axis=1)

    norm_ones = [normal_parts(inputs[i].astype(F32)) for i in range(MICRO)]
    qkv_part = head_weights([gain_rows(gain_self, w) for w in (self_query, self_key, self_value)])
    low_pairs = []
    for i in range(MICRO):
        low = norm_ones[i][0].astype(BF)
        low_pairs.append(group_pieces(jnp.concatenate([low, shifted(low, 1)], axis=0)))

    extra = jnp.pad(gain_mlp[:, None], ((0, 0), (0, 127)))
    split = [halves(w) for w in (self_out, gain_rows(gain_cross, cross_query), cross_out)]
    own_half, other_half = [jnp.concatenate([s[k] for s in split] + [extra], axis=1) for k in range(2)]
    near_half = flip(other_half, "mem", 1)
    far_half = flip(jnp.concatenate([own_half, near_half], axis=0), "mem", 2)
    wide = join_pieces([own_half, near_half, far_half[:wrows], far_half[wrows:]], me, 0)
    ckv_part = head_weights([cross_key, cross_value])

    state = {}
    stages = seq_stage([qkv_part], bits[0])
    for bit in bits[1:-1]:
        stages = seq_stage(stages, bit)
    first_wide = seq_stage([wide[:, : 2 * half]], bits[0])
    for bit in bits[1:-2]:
        first_wide = seq_stage(first_wide, bit)
    stages, first_wide = lax.optimization_barrier((stages, first_wide))
    first_wide = seq_stage(first_wide, bits[-2])
    qkv_full = assemble(seq_stage(stages, bits[-1]), seq, bits)
    width = qkv_full.shape[1] // 3
    last_wide = jnp.concatenate([wide[:, 2 * half :], ckv_part], axis=1)
    hidden = mlp_in.shape[0]

    def before_self(mark):
        rows = jnp.pad(memory.reshape(MICRO, real, D), ((0, 0), (0, padded - real), (0, 0)))
        mark, first, last, rows = lax.optimization_barrier((mark, first_wide, last_wide, rows))
        state["first"] = seq_stage(first, bits[-1])
        last = seq_stage([last], bits[0])
        for bit in bits[1:-2]:
            last = seq_stage(last, bit)
        state["last"] = last
        state["rows"] = group_pieces(rows.reshape(MICRO * padded, D))
        return mark

    def after_self_one(mark):
        mark, last = lax.optimization_barrier((mark, state["last"]))
        state["last"] = seq_stage(last, bits[-2])
        return mark

    def after_self_two(mark):
        hidden_part = jnp.concatenate([mlp_in, mlp_out], axis=0)
        mark, first, last, hidden_part = lax.optimization_barrier((mark, state["first"], state["last"], hidden_part))
        state["last"] = seq_stage(last, bits[-1])
        own = assemble(first, seq, bits)
        state["first"] = own, flip(own, "mem", 1)
        state["hidden"] = seq_stage([hidden_part], turned[0])
        return mark

    def after_first_out(mark):
        mark, slots, rows, last = lax.optimization_barrier((mark, state["hidden"], state["rows"], state["last"]))
        for bit in turned[1:-1]:
            slots = seq_stage(slots, bit)
        state["hidden"] = slots
        own = assemble(last, seq, bits)
        state["ckv"] = own[:, half + 128 :]
        state["gain"] = own[:, half].astype(F32)[None, :]
        state["last"] = own[:, :half], flip(own[:, :half], "mem", 1)
        state["rows"] = [
            jnp.concatenate([r[i * padded : (i + 1) * padded] for r in rows], axis=0) for i in range(MICRO)
        ]
        state["mem_kv"] = [product(r, state["ckv"]).astype(BF) for r in state["rows"]]
        state["mem_prev"] = [shifted(kv, 1) for kv in state["mem_kv"]]
        return mark

    def after_cross_one(mark):
        mark, slots = lax.optimization_barrier((mark, state["hidden"]))
        state["hidden"] = seq_stage(slots, turned[-1])
        return mark

    def after_cross_out(mark):
        mark, slots = lax.optimization_barrier((mark, state["hidden"]))
        state["inner"] = jnp.concatenate([s[:hidden] for s in slots], axis=0)
        state["outer"] = jnp.concatenate([s[hidden:] for s in slots], axis=0)
        return mark

    def wide_weights(k):
        if k == 2:
            return state["last"]
        return [w[:, k * half : (k + 1) * half] for w in state["first"]]

    def wide_product(tensor, k):
        own, other = wide_weights(k)
        return join_halves(product(tensor, own), product(tensor, other))

    def wide_back(tensor, k):
        (left, right), (own, other) = halves(tensor), wide_weights(k)
        return product_t(left, own) + product_t(right, other)

    def wide_grads(left, right):
        own, other = halves(right)
        return outer_sum(left, own), outer_sum(left, other)

    def spill_of(micro, block):
        ids = lax.dynamic_slice_in_dim(page_ids[micro], jnp.maximum(block, 0) * group, group, 0)
        return jnp.sum((ids < block).astype(jnp.int32))

    def stream(i):
        x_rows = inputs[i].astype(F32)
        spill = spill_of(i, seq)
        self_at = jnp.stack([me, spill, spill_of(i, seq - 1)])
        before = memory_length[i][jnp.maximum(seq - 1, 0)]
        cross_at = jnp.stack([me, spill, before, memory_length[i][seq]])

        pieces = yield low_pairs[i]
        low_one = jnp.concatenate([p[:tok] for p in pieces], axis=0)
        low_before = jnp.concatenate([p[tok:] for p in pieces], axis=0)
        qkv = product(low_one, qkv_full).astype(BF)
        kv_prev = product(low_before, qkv_full[:, width:]).astype(BF)
        if i == 0:
            kv_prev = before_self(kv_prev)
        self_o, self_lse = self_forward(self_at, qkv, kv_prev, blocks)
        self_lse = yield self_lse

        pieces = yield to_tokens(self_o)
        self_low = join_pieces(pieces, me, 1)
        after_self = x_rows + wide_product(self_low, 0)
        plain_two, scale_two = normal_parts(after_self)
        low_two = plain_two.astype(BF)
        cross_q = split_columns(wide_product(low_two, 1).astype(BF), me)
        scale_two = yield scale_two

        pieces, top = yield to_heads(cross_q), group_pieces(cotangent[i])
        cross_q = jnp.concatenate(pieces, axis=0)
        mem_kv, mem_prev = state["mem_kv"][i], state["mem_prev"][i]
        cross_o, cross_lse = cross_forward(cross_at, cross_q, mem_prev, mem_kv, blocks, real)
        cross_lse = yield cross_lse

        pieces = yield to_tokens(cross_o)
        gain_three = state["gain"]
        cross_low = join_pieces(pieces, me, 1)
        after_cross = after_self + wide_product(cross_low, 2)
        plain_three, scale_three = normal_parts(after_cross)
        low_three = (plain_three * gain_three).astype(BF)
        scale_three = yield scale_three

        pieces = yield group_pieces(low_three)
        low_three = jnp.concatenate(pieces, axis=0)
        top = jnp.concatenate(top, axis=0)
        pre = product_t(low_three, state["inner"])
        pre_low = (product_t(top, state["outer"]) * gelu_slope(pre)).astype(BF)
        near, far = group_near(product(pre_low, state["inner"]).astype(BF))
        near = yield near

        grad_low_three = yield group_far(near, far)
        act = gelu(pre).astype(BF)
        grad_inner = outer_sum(pre_low, low_three)
        grad_outer = outer_sum(act, top)
        output = (after_cross + group_far(*group_near(product(act, state["outer"]).astype(BF)))).astype(BF)
        grad_gain_three = jnp.sum(grad_low_three * plain_three, axis=0)
        grad_after_cross = cotangent[i].astype(F32) + normal_back(
            plain_three, scale_three, grad_low_three * gain_three
        )
        cross_branch = grad_after_cross.astype(BF)
        pieces = split_columns(wide_back(cross_branch, 2).astype(BF), me)
        grad_gain_three = yield grad_gain_three

        pieces = yield to_heads(pieces)
        grad_cout = wide_grads(cross_low, cross_branch)
        cross_g = jnp.concatenate(pieces, axis=0)
        dcq, dmem_prev, dmem = cross_backward(
            cross_at, cross_q, mem_prev, mem_kv, cross_o, cross_g, cross_lse, blocks, real
        )
        dmem = yield dmem

        pieces = yield to_tokens(dcq)
        dmem = (dmem.astype(F32) + shifted(dmem_prev, -1).astype(F32)).astype(BF)
        grad_cq = join_pieces(pieces, me, 1)
        grad_after_self = grad_after_cross + normal_back(plain_two, scale_two, wide_back(grad_cq, 1))
        self_branch = grad_after_self.astype(BF)
        pieces = split_columns(wide_back(self_branch, 0).astype(BF), me)
        grad_after_self = yield grad_after_self

        pieces = yield to_heads(pieces)
        grad_cquery = wide_grads(low_two, grad_cq)
        grad_out = wide_grads(self_low, self_branch)
        self_g = jnp.concatenate(pieces, axis=0)
        dq, dkv, dkv_prev = self_backward(self_at, qkv, kv_prev, self_o, self_g, self_lse, blocks)
        dkv = yield dkv

        back = yield shifted(dkv_prev, -1)
        grad_qkv = outer_sum(low_one, jnp.concatenate([dq, dkv], axis=1))
        grad_prev = outer_sum(low_before, dkv_prev)
        dkv = (dkv.astype(F32) + back.astype(F32)).astype(BF)
        near, far = group_near(product_t(jnp.concatenate([dq, dkv], axis=1), qkv_full).astype(BF))
        near = yield near

        grad_plain = yield group_far(near, far)
        plain_one, scale_one = norm_ones[i]
        grad_x = grad_after_self + normal_back(plain_one, scale_one, grad_plain)
        grad_ckv = outer_sum(state["rows"][i], dmem)
        grad_mem = group_far(*group_near(product_t(dmem, state["ckv"]).astype(BF)))[:real].reshape(1, real, D)
        grad_qkv = grad_qkv + jnp.concatenate([jnp.zeros((D, width), F32), grad_prev], axis=1)
        return (output, grad_x, grad_mem, grad_gain_three, grad_inner, grad_outer, grad_qkv, grad_ckv,
                grad_out, grad_cquery, grad_cout)

    aside = {
        1: after_self_one,
        2: after_self_two,
        3: after_first_out,
        5: after_cross_one,
        8: after_cross_out,
    }
    done = interleave([stream(i) for i in range(MICRO)], aside)

    def total(k):
        return jax.tree.map(lambda a, b: a + b, done[0][k], done[1][k])

    def hidden_reduce(inner, outer):
        for bit in reversed(turned):
            cut = inner.shape[0] // 2
            theirs = flip(jnp.concatenate([inner[cut:], outer[cut:]], axis=0).astype(BF), "seq", bit).astype(F32)
            inner, outer = inner[:cut] + theirs[:cut], outer[:cut] + theirs[cut:]
        return inner, outer

    def wide_reduce(wide, extra_own, extra_other):
        own = jnp.concatenate([w[0].astype(BF) for w in wide] + extra_own, axis=1)
        other = jnp.concatenate([w[1].astype(BF) for w in wide] + extra_other, axis=1)
        return own.astype(F32) + flip(other, "mem", 1).astype(F32)

    def wide_finish(own):
        high = me >> 1
        rows_two = own.reshape(2, 2 * wrows, own.shape[1])
        theirs = lax.dynamic_index_in_dim(rows_two, 1 - high, 0, keepdims=False).astype(BF)
        own = lax.dynamic_index_in_dim(rows_two, high, 0, keepdims=False) + flip(theirs, "mem", 2).astype(F32)
        rows_two = own.reshape(2, wrows, own.shape[1])
        theirs = lax.dynamic_index_in_dim(rows_two, 1 - odd, 0, keepdims=False)
        own = lax.dynamic_index_in_dim(rows_two, odd, 0, keepdims=False)
        return own, flip(theirs.astype(BF), "mem", 1).astype(F32)

    def head_finish(summed, count):
        slots = summed.astype(BF).reshape(blocks, wrows, -1)
        ordered = [lax.dynamic_index_in_dim(slots, me ^ k, 0, keepdims=False) for k in range(4)]
        whole = join_pieces(to_tokens(jnp.concatenate(ordered, axis=0)), me, 1).astype(F32)
        whole = whole.reshape(wrows, blocks, count, -1)
        return [whole[:, :, k].reshape(wrows, D) for k in range(count)]

    def along_seq(tensor):
        return seq_reduce(reorder(tensor, seq, turned), turned)

    grad_inner, grad_outer = hidden_reduce(total(4), total(5))

    gain_terms = jnp.pad(total(3)[:, None], ((0, 0), (0, 127))).astype(BF)
    last = wide_reduce([total(10)], [gain_terms], [jnp.zeros_like(gain_terms)])
    last = along_seq(jnp.concatenate([last, total(7)], axis=1))
    own, near = wide_finish(last[:, : half + 128])
    grad_cout = join_halves(own[:, :half], near[:, :half])
    grad_gain_mlp = own[:, half] + near[:, half]
    grad_ckey, grad_cvalue = head_finish(last[:, half + 128 :], 2)

    own, near = wide_finish(along_seq(wide_reduce([total(8), total(9)], [], [])))
    grad_out, plain_cquery = [
        join_halves(own[:, k * half : (k + 1) * half], near[:, k * half : (k + 1) * half]) for k in range(2)
    ]
    plain_qkv = head_finish(along_seq(total(6)), 3)

    def gained(gain, weights, plains):
        scale = gain.astype(F32)[:, None]
        grad_gain = sum(jnp.sum(w.astype(F32) * p, axis=1) for w, p in zip(weights, plains))
        return grad_gain, [p * scale for p in plains]

    grad_gain_self, (grad_query, grad_key, grad_value) = gained(
        gain_self, (self_query, self_key, self_value), plain_qkv
    )
    grad_gain_cross, (grad_cquery,) = gained(gain_cross, (cross_query,), (plain_cquery,))
    return (
        jnp.stack([d[0] for d in done]),
        jnp.stack([d[1] for d in done]),
        jnp.stack([d[2] for d in done]),
        grad_gain_self,
        grad_query,
        grad_key,
        grad_value,
        grad_out,
        grad_gain_cross,
        grad_cquery,
        grad_ckey,
        grad_cvalue,
        grad_cout,
        grad_gain_mlp,
        grad_inner,
        grad_outer,
    )


def solution(mesh):
    rows = P(("seq", "mem"), None)
    tokens = P(None, ("seq", "mem"), None)
    pages = P(None, "seq", "mem", None)
    gains = P(("seq", "mem"))
    return jax.shard_map(
        shards,
        mesh=mesh,
        in_specs=(tokens, pages, P(), P(), tokens, gains, rows, rows, rows, rows, gains, rows, rows, rows, rows,
                  gains, rows, rows),
        out_specs=(tokens, tokens, pages, gains, rows, rows, rows, rows, gains, rows, rows, rows, rows, gains,
                   rows, rows),
        check_vma=False,
    )
```

```python
import functools
import jax
import jax.numpy as jnp
import numpy as np
from jax import lax
from jax.experimental import pallas as pl
from jax.experimental.pallas import tpu as pltpu
from jax.sharding import PartitionSpec as P

HEAD = 64
BF = jnp.bfloat16
F32 = jnp.float32
LOWEST = -1e30


def head_lanes(rows, width):
    return lax.broadcasted_iota(jnp.int32, (rows, width), 1) // HEAD


def one_head(block, lanes, head):
    return jnp.where(lanes == head, block, jnp.zeros_like(block))


def dot_nt(left, right):
    return lax.dot_general(left, right, (((1,), (1,)), ((), ())), preferred_element_type=F32)


def dot_nn(left, right):
    return lax.dot_general(left, right, (((1,), (0,)), ((), ())), preferred_element_type=F32)


def dot_tn(left, right):
    return lax.dot_general(left, right, (((0,), (0,)), ((), ())), preferred_element_type=F32)


def self_range(p, rows, blocks, spill, prev_spill):
    first = jnp.where(p * rows < spill, prev_spill // rows, blocks + spill // rows)
    return first, blocks + p + 1


def self_allowed(query, key, extent, spill, prev_spill):
    first = jnp.where(query < spill, prev_spill, extent + spill)
    return (key >= first) & (key <= extent + query)


def cross_allowed(query, place, side, spill, length, me, padded, real):
    part = place // padded
    inner = place - part * padded
    row = (part ^ me) * real + inner
    return (inner < real) & (row < length) & ((query < spill) == (side == 0))


def self_forward_kernel(rows, blocks, heads, sc, qkv, kvp, o_ref, lse_ref, k_scr, v_scr, s_scr, mx, tot):
    width = heads * HEAD
    extent = rows * blocks
    me, spill, prev_spill = sc[0], sc[1], sc[2]
    lanes = head_lanes(rows, width)

    def place(b):
        return pl.multiple_of((b ^ me) * rows, rows)

    first_used, _ = self_range(0, rows, blocks, spill, prev_spill)

    @pl.loop(first_used, 2 * blocks)
    def _(kb):
        def fill(keys, values):
            k_scr[kb] = keys
            for h in range(heads):
                v_scr[kb, h * rows : (h + 1) * rows, :] = one_head(values, lanes, h)

        @pl.when(kb < blocks)
        def _():
            at = pl.ds(place(kb), rows)
            fill(kvp[at, 0:width], kvp[at, width : 2 * width])

        @pl.when(kb >= blocks)
        def _():
            at = pl.ds(place(kb - blocks), rows)
            fill(qkv[at, width : 2 * width], qkv[at, 2 * width : 3 * width])

    @pl.loop(0, blocks)
    def _(p):
        q = qkv[pl.ds(place(p), rows), 0:width] * jnp.asarray(0.125, BF)
        mx[...] = jnp.full(mx.shape, LOWEST, F32)
        tot[...] = jnp.zeros(tot.shape, F32)
        first, last = self_range(p, rows, blocks, spill, prev_spill)
        query = p * rows + lax.broadcasted_iota(jnp.int32, (rows, 1), 0)

        @pl.loop(first, last)
        def _(kb):
            key = kb * rows + lax.broadcasted_iota(jnp.int32, (1, rows), 1)
            allowed = self_allowed(query, key, extent, spill, prev_spill)
            k = k_scr[kb]
            for h in range(heads):
                s = dot_nt(one_head(q, lanes, h), k)
                s = jnp.where(allowed, s, LOWEST)
                s_scr[kb, h] = s
                mx[h] = jnp.maximum(mx[h], s)

        for h in range(heads):
            mx[h, :, 0:1] = jnp.max(mx[h], axis=1, keepdims=True)

        def weigh(kb, acc):
            parts = []
            for h in range(heads):
                e = jnp.exp(s_scr[kb, h] - mx[h, :, 0:1])
                tot[h] += e
                parts.append(e.astype(BF))
            return acc + dot_nn(jnp.concatenate(parts, axis=1), v_scr[kb])

        acc = lax.fori_loop(first, last, weigh, jnp.zeros((rows, width), F32))
        finish(p, place(p), rows, heads, acc, mx, tot, lanes, o_ref, lse_ref)


def finish(p, start, rows, heads, acc, mx, tot, lanes, o_ref, lse_ref):
    over = jnp.zeros((rows, 128), F32)
    inverse = jnp.zeros(acc.shape, F32)
    slim = lax.broadcasted_iota(jnp.int32, (rows, 128), 1)
    for h in range(heads):
        total = jnp.sum(tot[h], axis=1, keepdims=True)
        inverse = jnp.where(lanes == h, 1.0 / total, inverse)
        over = jnp.where(slim == h, mx[h, :, 0:1] + jnp.log(total), over)
    o_ref[pl.ds(start, rows), :] = (acc * inverse).astype(BF)
    lse_ref[:, pl.ds(pl.multiple_of(p * rows, rows), rows)] = over.T[0:8, :]


def lay(out, own, near, far):
    rows = own.shape[0]
    out[0:rows, :] = own[...]
    out[rows : 2 * rows, :] = near[0:rows, :]
    out[2 * rows : 3 * rows, :] = far[0:rows, :]
    out[3 * rows :, :] = near[rows:, :]


def cross_forward_kernel(rows, blocks, heads, padded, real, sc, own, near, far, kv0, kv1, o_ref, lse_ref, q_ref,
                         v_scr, s_scr, mx, tot):
    lay(q_ref, own, near, far)
    width = heads * HEAD
    keys = kv0.shape[0]
    me, spill = sc[0], sc[1]
    lanes = head_lanes(rows, width)
    key_lanes = head_lanes(keys, width)
    kvs = (kv0, kv1)

    def place(b):
        return pl.multiple_of((b ^ me) * rows, rows)

    for side in range(2):
        values = kvs[side][:, width : 2 * width]
        for h in range(heads):
            v_scr[side, h * keys : (h + 1) * keys, :] = one_head(values, key_lanes, h)
    spot = lax.broadcasted_iota(jnp.int32, (1, keys), 1)

    @pl.loop(0, blocks)
    def _(p):
        q = q_ref[pl.ds(place(p), rows), :] * jnp.asarray(0.125, BF)
        mx[...] = jnp.full(mx.shape, LOWEST, F32)
        tot[...] = jnp.zeros(tot.shape, F32)
        query = p * rows + lax.broadcasted_iota(jnp.int32, (rows, 1), 0)
        reads = (p * rows < spill, (p + 1) * rows > spill)
        for side in range(2):

            @pl.when(reads[side])
            def _():
                allowed = cross_allowed(query, spot, side, spill, sc[2 + side], me, padded, real)
                k = kvs[side][:, 0:width]
                for h in range(heads):
                    s = dot_nt(one_head(q, lanes, h), k)
                    s = jnp.where(allowed, s, LOWEST)
                    s_scr[side, h] = s
                    mx[h] = jnp.maximum(mx[h], jnp.max(s, axis=1, keepdims=True))

        def weigh(side, acc):
            parts = []
            for h in range(heads):
                e = jnp.exp(s_scr[side, h] - mx[h, :, 0:1])
                tot[h] += e
                parts.append(e.astype(BF))
            return acc + dot_nn(jnp.concatenate(parts, axis=1), v_scr[side])

        first = jnp.where(reads[0], 0, 1)
        last = jnp.where(reads[1], 2, 1)
        acc = lax.fori_loop(first, last, weigh, jnp.zeros((rows, width), F32))
        finish(p, place(p), rows, heads, acc, mx, tot, lanes, o_ref, lse_ref)


def spread(p, at, rows, heads, q, g, o_ref, lse_ref, lanes, q_cat, g_cat, stat):
    weighted = (g.astype(F32) * o_ref[at, :].astype(F32)).T
    for h in range(heads):
        q_cat[h * rows : (h + 1) * rows, :] = one_head(q, lanes, h)
        g_cat[h * rows : (h + 1) * rows, :] = one_head(g, lanes, h)
        stat[heads + h : heads + h + 1, :] = jnp.sum(weighted[h * HEAD : (h + 1) * HEAD, :], axis=0, keepdims=True)
    stat[0:heads, :] = lse_ref[0:heads, pl.ds(pl.multiple_of(p * rows, rows), rows)]


def back_block(rows, heads, k, v, allowed, q_cat, g_cat, stat, w_scr, ds_wide, ds_tall):
    count = k.shape[0]
    for h in range(heads):
        span = slice(h * rows, (h + 1) * rows)
        s = dot_nt(k, q_cat[span, :])
        e = jnp.where(allowed, jnp.exp(s - stat[h : h + 1, :]), 0.0)
        de = dot_nt(v, g_cat[span, :])
        ds = (e * (de - stat[heads + h : heads + h + 1, :])).astype(BF)
        w_scr[:, span] = e.astype(BF)
        ds_wide[:, span] = ds
        ds_tall[h * count : (h + 1) * count, :] = ds


def self_backward_kernel(rows, blocks, heads, sc, qkv, kvp, o_ref, own, near, far, lse_ref, dq_ref, dkv_ref,
                         dprev_ref, g_ref, kv_scr, k_cat, dkv_scr, q_cat, g_cat, stat, w_scr, ds_wide, ds_tall):
    lay(g_ref, own, near, far)
    width = heads * HEAD
    extent = rows * blocks
    me, spill, prev_spill = sc[0], sc[1], sc[2]
    lanes = head_lanes(rows, width)

    def place(b):
        return pl.multiple_of((b ^ me) * rows, rows)

    first_used, _ = self_range(0, rows, blocks, spill, prev_spill)

    @pl.loop(0, 2 * blocks)
    def _(kb):
        dkv_scr[kb] = jnp.zeros(dkv_scr.shape[1:], F32)

    @pl.loop(first_used, 2 * blocks)
    def _(kb):
        def fill(pair):
            kv_scr[kb] = pair
            scaled = pair[:, 0:width] * jnp.asarray(0.125, BF)
            for h in range(heads):
                k_cat[kb, h * rows : (h + 1) * rows, :] = one_head(scaled, lanes, h)

        @pl.when(kb < blocks)
        def _():
            fill(kvp[pl.ds(place(kb), rows), :])

        @pl.when(kb >= blocks)
        def _():
            fill(qkv[pl.ds(place(kb - blocks), rows), width : 3 * width])

    @pl.loop(0, blocks)
    def _(p):
        at = pl.ds(place(p), rows)
        q = qkv[at, 0:width] * jnp.asarray(0.125, BF)
        g = g_ref[at, :]
        spread(p, at, rows, heads, q, g, o_ref, lse_ref, lanes, q_cat, g_cat, stat)
        first, last = self_range(p, rows, blocks, spill, prev_spill)
        query = p * rows + lax.broadcasted_iota(jnp.int32, (1, rows), 1)

        def step(kb, dq):
            key = kb * rows + lax.broadcasted_iota(jnp.int32, (rows, 1), 0)
            allowed = self_allowed(query, key, extent, spill, prev_spill)
            back_block(rows, heads, kv_scr[kb, :, 0:width], kv_scr[kb, :, width : 2 * width], allowed,
                       q_cat, g_cat, stat, w_scr, ds_wide, ds_tall)
            dkv_scr[kb, :, 0:width] += dot_nn(ds_wide[...], q_cat[...])
            dkv_scr[kb, :, width : 2 * width] += dot_nn(w_scr[...], g_cat[...])
            return dq + dot_tn(ds_tall[...], k_cat[kb])

        dq = lax.fori_loop(first, last, step, jnp.zeros((rows, width), F32))
        dq_ref[at, :] = dq.astype(BF)

    @pl.loop(0, blocks)
    def _(b):
        at = pl.ds(place(b), rows)
        dprev_ref[at, :] = dkv_scr[b].astype(BF)
        dkv_ref[at, :] = dkv_scr[blocks + b].astype(BF)


def cross_backward_kernel(rows, blocks, heads, padded, real, pieces, sc, q_ref, kv0, kv1, o_ref, own, near, far,
                          lse_ref, dq_ref, dkv0_ref, dkv1_ref, g_ref, k_cat, dkv_scr, q_cat, g_cat, stat, w_scr, ds_wide, ds_tall):
    lay(g_ref, own, near, far)
    width = heads * HEAD
    keys = kv0.shape[0]
    step_keys = keys // pieces
    me, spill = sc[0], sc[1]
    lanes = head_lanes(rows, width)
    key_lanes = head_lanes(step_keys, width)
    kvs = (kv0, kv1)

    def place(b):
        return pl.multiple_of((b ^ me) * rows, rows)

    dkv_scr[...] = jnp.zeros(dkv_scr.shape, F32)
    for side in range(2):
        for piece in range(pieces):
            scaled = kvs[side][piece * step_keys : (piece + 1) * step_keys, 0:width] * jnp.asarray(0.125, BF)
            for h in range(heads):
                k_cat[side * pieces + piece, h * step_keys : (h + 1) * step_keys, :] = one_head(scaled, key_lanes, h)

    @pl.loop(0, blocks)
    def _(p):
        at = pl.ds(place(p), rows)
        q = q_ref[at, :] * jnp.asarray(0.125, BF)
        spread(p, at, rows, heads, q, g_ref[at, :], o_ref, lse_ref, lanes, q_cat, g_cat, stat)
        query = p * rows + lax.broadcasted_iota(jnp.int32, (1, rows), 1)
        reads = (p * rows < spill, (p + 1) * rows > spill)
        first = jnp.where(reads[0], 0, pieces)
        last = jnp.where(reads[1], 2 * pieces, pieces)

        def step(kb, dq):
            side = kb // pieces
            at_key = pl.ds(pl.multiple_of((kb - side * pieces) * step_keys, step_keys), step_keys)
            spot = (kb - side * pieces) * step_keys + lax.broadcasted_iota(jnp.int32, (step_keys, 1), 0)
            length = jnp.where(side == 0, sc[2], sc[3])
            allowed = cross_allowed(query, spot, side, spill, length, me, padded, real)
            is_prev = side == 0
            pair = jnp.where(is_prev, kv0[at_key, :], kv1[at_key, :])
            back_block(rows, heads, pair[:, 0:width], pair[:, width : 2 * width], allowed,
                       q_cat, g_cat, stat, w_scr, ds_wide, ds_tall)
            dkv_scr[kb, :, 0:width] += dot_nn(ds_wide[...], q_cat[...])
            dkv_scr[kb, :, width : 2 * width] += dot_nn(w_scr[...], g_cat[...])
            return dq + dot_tn(ds_tall[...], k_cat[kb])

        dq = lax.fori_loop(first, last, step, jnp.zeros((rows, width), F32))
        dq_ref[at, :] = dq.astype(BF)

    for piece in range(pieces):
        span = slice(piece * step_keys, (piece + 1) * step_keys)
        dkv0_ref[span, :] = dkv_scr[piece].astype(BF)
        dkv1_ref[span, :] = dkv_scr[pieces + piece].astype(BF)


def call(kernel, scalars, arrays, outs, scratch=()):
    vmem = pl.BlockSpec(memory_space=pltpu.VMEM)
    return pl.pallas_call(
        kernel,
        out_shape=outs,
        in_specs=[pl.BlockSpec(memory_space=pltpu.SMEM)] + [vmem] * len(arrays),
        out_specs=jax.tree.map(lambda _: vmem, outs),
        scratch_shapes=scratch,
        compiler_params=pltpu.CompilerParams(vmem_limit_bytes=48 * 2**20),
        cost_estimate=pl.CostEstimate(flops=1024, bytes_accessed=1024, transcendentals=0),
    )(scalars, *arrays)


def self_forward(scalars, qkv, kvp, blocks):
    extent = qkv.shape[0]
    rows = extent // blocks
    width = qkv.shape[1] // 3
    heads = width // HEAD
    return call(
        functools.partial(self_forward_kernel, rows, blocks, heads),
        scalars,
        (qkv, kvp),
        [jax.ShapeDtypeStruct((extent, width), BF), jax.ShapeDtypeStruct((8, extent), F32)],
        [
            pltpu.VMEM((2 * blocks, rows, width), BF),
            pltpu.VMEM((2 * blocks, heads * rows, width), BF),
            pltpu.VMEM((2 * blocks, heads, rows, rows), F32),
            pltpu.VMEM((heads, rows, rows), F32),
            pltpu.VMEM((heads, rows, rows), F32),
        ],
    )


def cross_forward(scalars, pieces, kv0, kv1, blocks, real):
    rows, width = pieces[0].shape
    extent = rows * blocks
    heads = width // HEAD
    keys = kv0.shape[0]
    return call(
        functools.partial(cross_forward_kernel, rows, blocks, heads, keys // blocks, real),
        scalars,
        (*pieces, kv0, kv1),
        [
            jax.ShapeDtypeStruct((extent, width), BF),
            jax.ShapeDtypeStruct((8, extent), F32),
            jax.ShapeDtypeStruct((extent, width), BF),
        ],
        [
            pltpu.VMEM((2, heads * keys, width), BF),
            pltpu.VMEM((2, heads, rows, keys), F32),
            pltpu.VMEM((heads, rows, keys), F32),
            pltpu.VMEM((heads, rows, keys), F32),
        ],
    )


def back_scratch(rows, heads, width, keys):
    return [
        pltpu.VMEM((heads * rows, width), BF),
        pltpu.VMEM((heads * rows, width), BF),
        pltpu.VMEM((8, rows), F32),
        pltpu.VMEM((keys, heads * rows), BF),
        pltpu.VMEM((keys, heads * rows), BF),
        pltpu.VMEM((heads * keys, rows), BF),
    ]


def self_backward(scalars, qkv, kvp, o, g, lse, blocks):
    extent = qkv.shape[0]
    rows = extent // blocks
    width = qkv.shape[1] // 3
    heads = width // HEAD
    return call(
        functools.partial(self_backward_kernel, rows, blocks, heads),
        scalars,
        (qkv, kvp, o, *g, lse),
        [
            jax.ShapeDtypeStruct((extent, width), BF),
            jax.ShapeDtypeStruct((extent, 2 * width), BF),
            jax.ShapeDtypeStruct((extent, 2 * width), BF),
        ],
        [
            pltpu.VMEM((extent, width), BF),
            pltpu.VMEM((2 * blocks, rows, 2 * width), BF),
            pltpu.VMEM((2 * blocks, heads * rows, width), BF),
            pltpu.VMEM((2 * blocks, rows, 2 * width), F32),
        ]
        + back_scratch(rows, heads, width, rows),
    )


def cross_backward(scalars, q, kv0, kv1, o, g, lse, blocks, real, pieces=2):
    extent, width = q.shape
    rows = extent // blocks
    heads = width // HEAD
    keys = kv0.shape[0]
    step_keys = keys // pieces
    return call(
        functools.partial(cross_backward_kernel, rows, blocks, heads, keys // blocks, real, pieces),
        scalars,
        (q, kv0, kv1, o, *g, lse),
        [
            jax.ShapeDtypeStruct((extent, width), BF),
            jax.ShapeDtypeStruct((keys, 2 * width), BF),
            jax.ShapeDtypeStruct((keys, 2 * width), BF),
        ],
        [
            pltpu.VMEM((extent, width), BF),
            pltpu.VMEM((2 * pieces, heads * step_keys, width), BF),
            pltpu.VMEM((2 * pieces, step_keys, 2 * width), F32),
        ]
        + back_scratch(rows, heads, width, step_keys),
    )


def ordered_pieces(pieces, me):
    odd = (me & 1) == 1
    high = (me & 2) == 2
    low_pair = [jnp.where(odd, pieces[1 - i], pieces[i]) for i in range(2)]
    high_pair = [jnp.where(odd, pieces[3 - i], pieces[2 + i]) for i in range(2)]
    ordered = [jnp.where(high, high_pair[i], low_pair[i]) for i in range(2)]
    return ordered + [jnp.where(high, low_pair[i], high_pair[i]) for i in range(2)]


def join_pieces(pieces, me, axis):
    return jnp.concatenate(ordered_pieces(pieces, me), axis=axis)


def received(own, near, far, me):
    rows = own.shape[0]
    return join_pieces([own[...], near[0:rows, :], far[0:rows, :], near[rows:, :]], me, 1)


def send_pieces(tensor, me, first, second, rest):
    width = tensor.shape[1] // 4
    rows = tensor.shape[0]
    pieces = ordered_pieces([tensor[:, k * width : (k + 1) * width] for k in range(4)], me)
    first[...] = pieces[0]
    second[...] = pieces[1]
    rest[0:rows, :] = pieces[2]
    rest[rows:, :] = pieces[3]


def half_product(tensor, own, other, me, first):
    span = slice(first, first + own.shape[0] // 2)
    left, right = dot_nn(tensor, own[:, span]), dot_nn(tensor, other[:, span])
    odd = (me & 1) == 1
    return jnp.concatenate([jnp.where(odd, right, left), jnp.where(odd, left, right)], axis=1)


def two_halves(tensor, me):
    half = tensor.shape[1] // 2
    odd = (me & 1) == 1
    left, right = tensor[:, 0:half], tensor[:, half:]
    return jnp.where(odd, right, left), jnp.where(odd, left, right)


def half_back(mine, others, own, other, first):
    span = slice(first, first + own.shape[0] // 2)
    return dot_nt(mine, own[:, span]) + dot_nt(others, other[:, span])


def normal_parts(tensor):
    average = jnp.mean(tensor, axis=-1, keepdims=True)
    centered = tensor - average
    scale = lax.rsqrt(jnp.mean(centered * centered, axis=-1, keepdims=True) + 1e-05)
    return centered * scale, scale


def normal_back(plain, scale, grad):
    inner = jnp.mean(grad * plain, axis=-1, keepdims=True)
    return scale * (grad - jnp.mean(grad, axis=-1, keepdims=True) - plain * inner)


def gelu_parts(pre):
    size = jnp.abs(pre)
    t = 1.0 / (1.0 + (0.3275911 * 0.7071067811865476) * size)
    poly = ((((1.061405429 * t - 1.453152027) * t + 1.421413741) * t - 0.284496736) * t + 0.254829592) * t
    bell = jnp.exp(-0.5 * pre * pre)
    tail = 0.5 * poly * bell
    cdf = jnp.where(pre < 0.0, tail, 1.0 - tail)
    return pre * cdf, cdf + pre * bell * 0.3989422804014327


def qkv_kernel(at, low, far_low, near_low, ahead, far_ahead, near_ahead, weight, qkv, kvp, low_one, low_before):
    rows = low.shape[0]
    width = weight.shape[1] // 3
    for out, own, far, near in ((low_one, low, far_low, near_low), (low_before, ahead, far_ahead, near_ahead)):
        out[0:rows, :] = own[...]
        out[rows : 2 * rows, :] = near[0:rows, :]
        out[2 * rows : 3 * rows, :] = far[...]
        out[3 * rows :, :] = near[rows:, :]

    @pl.loop(0, 4)
    def _(b):
        block = pl.ds(pl.multiple_of(b * rows, rows), rows)
        qkv[block, :] = dot_nn(low_one[block, :], weight[...]).astype(BF)
        kvp[block, :] = dot_nn(low_before[block, :], weight[:, width:]).astype(BF)


def self_out_kernel(at, own, near, far, x, wide_own, wide_other,
                    low, after, plain, low_next, scale, first, second, rest):
    me = at[0]
    joined = received(own, near, far, me)
    low[...] = joined
    total = x[...].astype(F32) + half_product(joined, wide_own, wide_other, me, 0)
    after[...] = total
    normed, scaled = normal_parts(total)
    plain[...] = normed
    scale[...] = scaled
    rounded = normed.astype(BF)
    low_next[...] = rounded
    send_pieces(half_product(rounded, wide_own, wide_other, me, wide_own.shape[0] // 2).astype(BF), me, first, second, rest)


def cross_out_kernel(at, own, near, far, before, out_own, out_other, gain, low, after, plain, scale, low_next):
    me = at[0]
    joined = received(own, near, far, me)
    low[...] = joined
    total = before[...] + half_product(joined, out_own, out_other, me, 0)
    after[...] = total
    normed, scaled = normal_parts(total)
    plain[...] = normed
    scale[...] = scaled
    low_next[...] = (normed * gain[...]).astype(BF)


def mlp_kernel(at, low, near_low, far_low, top, near_top, far_top, inner, outer,
               low_all, top_all, act, pre_low, grad_keep, grad_send, out_keep, out_send):
    rows = low.shape[0]
    for out, own, near, far in ((low_all, low, near_low, far_low), (top_all, top, near_top, far_top)):
        out[0:rows, :] = own[...]
        out[rows : 2 * rows, :] = near[0:rows, :]
        out[2 * rows : 3 * rows, :] = far[...]
        out[3 * rows :, :] = near[rows:, :]
    for parity, grad, out in ((1, grad_send, out_send), (0, grad_keep, out_keep)):

        @pl.loop(0, 2)
        def _(b):
            block = pl.ds(pl.multiple_of((2 * b + parity) * rows, rows), rows)
            place = pl.ds(pl.multiple_of(b * rows, rows), rows)
            value, slope = gelu_parts(dot_nt(low_all[block, :], inner[...]))
            act_block = value.astype(BF)
            act[block, :] = act_block
            pre_block = (dot_nt(top_all[block, :], outer[...]) * slope).astype(BF)
            pre_low[block, :] = pre_block
            grad[place, :] = dot_nn(pre_block, inner[...]).astype(BF)
            out[place, :] = dot_nn(act_block, outer[...]).astype(BF)


def cross_back_kernel(at, near, far, plain, scale, gain, top, out_own, out_other,
                      grad_after, branch_own, branch_other, grad_gain, first, second, rest):
    me = at[0]
    grad = near[...] + far[...].astype(F32)
    normed = plain[...]
    grad_gain[...] = jnp.sum(grad * normed, axis=0, keepdims=True)
    total = top[...].astype(F32) + normal_back(normed, scale[...], grad * gain[...])
    grad_after[...] = total
    mine, others = two_halves(total.astype(BF), me)
    branch_own[...] = mine
    branch_other[...] = others
    send_pieces(half_back(mine, others, out_own, out_other, 0).astype(BF), me, first, second, rest)


def self_back_kernel(at, own, near, far, plain, scale, before, wide_own, wide_other,
                     grad_after, query_mine, query_others, branch_own, branch_other, first, second, rest):
    me = at[0]
    mine, others = two_halves(received(own, near, far, me), me)
    query_mine[...] = mine
    query_others[...] = others
    total = before[...] + normal_back(plain[...], scale[...], half_back(mine, others, wide_own, wide_other, wide_own.shape[0] // 2))
    grad_after[...] = total
    mine, others = two_halves(total.astype(BF), me)
    branch_own[...] = mine
    branch_other[...] = others
    send_pieces(half_back(mine, others, wide_own, wide_other, 0).astype(BF), me, first, second, rest)


def half_grads_kernel(names, at, *refs):
    own, other = refs[-2:]
    half = own.shape[1] // names
    for n in range(names):
        low_a, low_b, mine_a, mine_b, others_a, others_b = (ref[...] for ref in refs[6 * n : 6 * n + 6])
        span = slice(n * half, (n + 1) * half)
        other[:, span] = (dot_tn(low_a, others_a) + dot_tn(low_b, others_b)).astype(BF)
        own[:, span] = dot_tn(low_a, mine_a) + dot_tn(low_b, mine_b)


def qkv_back_kernel(at, dq, dkv, back, weight, keep, send):
    rows = dq.shape[0] // 4
    width = dq.shape[1]
    for parity, out in ((1, send), (0, keep)):

        @pl.loop(0, 2)
        def _(b):
            block = pl.ds(pl.multiple_of((2 * b + parity) * rows, rows), rows)
            place = pl.ds(pl.multiple_of(b * rows, rows), rows)
            kv = (dkv[block, :].astype(F32) + back[block, :].astype(F32)).astype(BF)
            grad = dot_nt(dq[block, :], weight[:, 0:width]) + dot_nt(kv, weight[:, width:])
            out[place, :] = grad.astype(BF)


def qkv_grads_kernel(at, low, before, dq, dkv, dkv_prev, out):
    width = dq.shape[1]
    out[:, 0:width] = dot_tn(low[...], dq[...])
    out[:, width:] = dot_tn(low[...], dkv[...]) + dot_tn(before[...], dkv_prev[...])


def shape(rows, columns, dtype=BF):
    return jax.ShapeDtypeStruct((rows, columns), dtype)


D = 1024
MICRO = 2


def flip(block, axis, bit):
    return lax.ppermute(block, axis, [(i, i ^ bit) for i in range(lax.axis_size(axis))])


def shifted(block, distance):
    devices = range(lax.axis_size("seq"))
    route = [(i - distance, i) for i in devices if i - distance in devices]
    return lax.ppermute(block, "seq", route)


def near_rows(own, far):
    return flip(jnp.concatenate([own, far], axis=0), "mem", 1)


def far_slots(part):
    rows = part.shape[0] // 4
    return part[:rows], part[rows : 2 * rows], flip(part[2 * rows :], "mem", 2)


def near_slots(own, side, far):
    rows = own.shape[0]
    return own, flip(jnp.concatenate([side, far[rows:]], axis=0), "mem", 1), far


def lay_slots(own, near, far):
    rows = own.shape[0]
    return jnp.concatenate([own, near[:rows], far[:rows], near[rows:]], axis=0)


def near_sum(keep, send):
    rows = keep.shape[0] // 2
    total = keep.astype(F32) + flip(send, "mem", 1).astype(F32)
    return total[:rows], total[rows:].astype(BF)


def seq_bits():
    count = lax.axis_size("seq")
    return [1 << i for i in reversed(range(count.bit_length() - 1))]


def seq_offsets(bits):
    offsets = [0]
    for bit in bits:
        offsets = offsets + [o ^ bit for o in offsets]
    return offsets


def seq_stage(block, bit):
    return jnp.concatenate([block, flip(block, "seq", bit)], axis=0)


def assemble_kernel(rows, offsets, at, first, second, *outs):
    half = len(offsets) // 2
    for i, offset in enumerate(offsets):
        ref = first if i < half else second
        start = pl.multiple_of((at[0] ^ offset) * rows, rows)
        column = 0
        for out in outs:
            columns = out.shape[1]
            place = slice((i % half) * rows, (i % half + 1) * rows)
            out[pl.ds(start, rows), :] = ref[place, column : column + columns]
            column += columns


def assemble(first, second, seq, bits, split):
    offsets = seq_offsets(bits)
    size = 2 * first.shape[0]
    outs = [shape(size, columns) for columns in split]
    return call(functools.partial(assemble_kernel, size // len(offsets), offsets), seq.reshape(1), (first, second), outs)


def reorder_kernel(rows, offsets, groups, at, *refs):
    out = refs[-1]
    for i, offset in enumerate(offsets):
        start = pl.multiple_of((at[0] ^ offset) * rows, rows)
        for column, terms in groups:
            total = None
            for term, first, columns in terms:
                part = refs[term][pl.ds(start, rows), first : first + columns].astype(F32)
                total = part if total is None else total + part
            out[i * rows : (i + 1) * rows, column : column + columns] = total.astype(BF)


def reorder(arrays, groups, seq, bits):
    offsets = seq_offsets(bits)
    size = arrays[0].shape[0]
    placed, column = [], 0
    for terms in groups:
        placed.append((column, terms))
        column += terms[0][2]
    out = jax.ShapeDtypeStruct((size, column), BF)
    kernel = functools.partial(reorder_kernel, size // len(offsets), offsets, placed)
    return call(kernel, seq.reshape(1), arrays, out)


def pack_kernel(width, half, at, *refs):
    me = at[0]
    (gain_self, gain_cross, gain_mlp), weights, (kept, message) = refs[:3], refs[3:11], refs[11:]
    query, key, value, out_w, cross_q, cross_k, cross_v, cross_o = weights

    def scaled(weight, gain):
        return (weight.astype(F32) * gain[...].astype(F32)).astype(BF)

    def piece(k):
        at_k = pl.ds(pl.multiple_of((me ^ k) * width, width), width)
        gained = [scaled(w[:, at_k], gain_self) for w in (query, key, value)]
        return jnp.concatenate(gained + [w[:, at_k] for w in (cross_k, cross_v)], axis=1)

    def side(k):
        at_k = pl.ds(pl.multiple_of(((me & 1) ^ k) * half, half), half)
        rows = gain_mlp.shape[0]
        lanes = lax.broadcasted_iota(jnp.int32, (rows, 128), 1)
        extra = jnp.where(lanes == 0, gain_mlp[...].astype(F32), 0.0).astype(BF)
        return jnp.concatenate([out_w[:, at_k], scaled(cross_q[:, at_k], gain_cross), cross_o[:, at_k], extra], axis=1)

    kept[...] = jnp.concatenate([piece(0), piece(1)], axis=1)
    message[...] = jnp.concatenate([piece(2), piece(3), side(0), side(1)], axis=1)


def repack_kernel(narrow, broad, at, kept, message, far, out):
    sides = 2 * narrow + broad
    out[:, 0:narrow] = kept[:, narrow:]
    out[:, narrow : 2 * narrow] = far[:, narrow : 2 * narrow]
    out[:, 2 * narrow : 2 * narrow + broad] = message[:, sides:]
    out[:, 2 * narrow + broad :] = far[:, sides:]


def unpack_kernel(width, narrow, broad, at, kept, message, far, near, qkv, first, last):
    me = at[0]
    start = 2 * narrow
    heads = [kept[:, 0:narrow], near[:, 0:narrow], far[:, 0:narrow], near[:, narrow:start]]
    sides = [message, near, far, near]
    sides = [ref[:, at_k : at_k + broad] for ref, at_k in zip(sides, (start, start, start, start + broad))]
    heads = join_pieces(heads, me, 0)
    sides = join_pieces(sides, me, 0)
    pair = broad - 128 - (broad - 128) // 3
    qkv[...] = heads[:, 0 : 3 * width]
    first[...] = jnp.concatenate([sides[:, 0:pair], heads[:, 3 * width :]], axis=1)
    last[...] = sides[:, pair:]


class Stay:
    def __init__(self, value):
        self.value = value


def interleave(streams, sides):
    held = [next(s) for s in streams]
    results = [None] * len(streams)
    waiting = [(side, *next(side)) for side in sides]
    turn = 0
    ticks = 0

    def serve(arrays):
        nonlocal ticks, waiting
        ticks += 1
        due = [w for w in waiting if w[1] == ticks]
        waiting = [w for w in waiting if w[1] != ticks]
        arrays, taken = lax.optimization_barrier((arrays, [w[2]() for w in due]))
        for (side, _, _), got in zip(due, taken):
            try:
                waiting.append((side, *side.send(got)))
            except StopIteration:
                pass
        return arrays

    while True:
        other = (turn + 1) % len(streams)
        try:
            mark = streams[turn].send(held[turn])
            while isinstance(mark, Stay):
                mark = streams[turn].send(serve(mark.value))
            if results[other] is None:
                held[other], mark = serve((held[other], mark))
            else:
                mark = serve(mark)
            held[turn] = streams[turn].send(mark)
        except StopIteration as end:
            results[turn] = end.value
        if results[other] is None:
            turn = other
        elif results[turn] is not None:
            assert not waiting
            return results


def shards(
    inputs,
    memory,
    page_ids,
    memory_length,
    cotangent,
    gain_self,
    self_query,
    self_key,
    self_value,
    self_out,
    gain_cross,
    cross_query,
    cross_key,
    cross_value,
    cross_out,
    gain_mlp,
    mlp_in,
    mlp_out,
):
    seq = lax.axis_index("seq")
    me = lax.axis_index("mem")
    odd = me & 1
    blocks = lax.axis_size("mem")
    tok = inputs.shape[1]
    group = tok * blocks
    real = memory.shape[2]
    padded = -(-real // 16) * 16
    wrows = self_query.shape[0]
    bits = seq_bits()
    turned = bits[:-2] + [bits[-1], bits[-2]]
    half = D // 2

    def join_halves(own, other):
        return jnp.concatenate([jnp.where(odd == 0, own, other), jnp.where(odd == 0, other, own)], axis=1)

    width = self_query.shape[1] // blocks
    narrow, broad = 5 * width, 3 * half + 128
    place = me.reshape(1)
    weights = (self_query, self_key, self_value, self_out, cross_query, cross_key, cross_value, cross_out)
    gains = [g[:, None] for g in (gain_self, gain_cross, gain_mlp)]
    kept, message = call(
        functools.partial(pack_kernel, width, half), place, (*gains, *weights),
        [shape(wrows, 2 * narrow), shape(wrows, 2 * (narrow + broad))],
    )
    far = flip(message, "mem", 2)
    norm_ones = [normal_parts(inputs[i].astype(F32)) for i in range(MICRO)]
    lows = [parts[0].astype(BF) for parts in norm_ones]
    befores = [shifted(low, 1) for low in lows]
    far_lows = [flip(lows[0], "mem", 2)]
    near = call(
        functools.partial(repack_kernel, narrow, broad), place, (kept, message, far),
        shape(*message.shape),
    )
    near = flip(near, "mem", 1)
    qkv_part, first_part, last_part = call(
        functools.partial(unpack_kernel, width, narrow, broad), place, (kept, message, far, near),
        [shape(blocks * wrows, columns) for columns in (3 * width, 2 * half + 2 * width, half + 128)],
    )

    state = {}
    hidden = mlp_in.shape[0]
    memory_own = jnp.pad(memory.reshape(MICRO, real, D), ((0, 0), (0, padded - real), (0, 0)))
    memory_own = memory_own.reshape(MICRO * padded, D)
    stage = seq_stage(qkv_part, bits[0])
    stage, first_part, befores[0] = lax.optimization_barrier((stage, first_part, befores[0]))
    far_befores = [flip(befores[0], "mem", 2)]
    for bit in bits[1:-1]:
        stage = seq_stage(stage, bit)
    stage, first_part, lows[1], befores[1] = lax.optimization_barrier((stage, first_part, lows[1], befores[1]))
    far_lows.append(flip(lows[1], "mem", 2))
    far_befores.append(flip(befores[1], "mem", 2))
    first_stage = first_part
    for bit in bits[:-2]:
        first_stage = seq_stage(first_stage, bit)
    (qkv_full,) = assemble(stage, flip(stage, "seq", bits[-1]), seq, bits, [3 * width])

    def first_side():
        (first,) = yield 1, lambda: (first_stage,)
        first = seq_stage(first, bits[-2])
        (first,) = yield 2, lambda: (first,)
        first = first, flip(first, "seq", bits[-1])
        first = yield 3, lambda: first
        state["wide_own"], state["ckv"] = assemble(*first, seq, bits, [2 * half, 2 * width])
        state["wide_other"] = flip(state["wide_own"], "mem", 1)

    def last_side():
        (last,) = yield 2, lambda: (last_part,)
        for bit in bits[:-2]:
            last = seq_stage(last, bit)
        (last,) = yield 3, lambda: (last,)
        last = seq_stage(last, bits[-2])
        (last,) = yield 5, lambda: (last,)
        last = last, flip(last, "seq", bits[-1])
        last = yield 7, lambda: last
        state["cout_own"], gain = assemble(*last, seq, bits, [half, 128])
        state["cout_other"] = flip(state["cout_own"], "mem", 1)
        state["gain"] = gain[:, 0].astype(F32)[None, :]

    def memory_side():
        (rows,) = yield 1, lambda: (memory_own,)
        rows = rows, shifted(rows, 1)
        rows = yield 2, lambda: rows
        rows = jnp.concatenate(rows, axis=0)
        far = flip(rows, "mem", 2)
        rows, far = yield 4, lambda: (rows, far)
        pieces = rows, near_rows(rows, far), far
        pieces = yield 5, lambda: pieces
        size = MICRO * padded
        near = pieces[1][: 2 * size], pieces[1][2 * size :]
        slots = pieces[0], near[0], pieces[2], near[1]
        rows = [
            jnp.concatenate([p[i * padded : (i + 1) * padded] for p in slots], axis=0) for i in range(2 * MICRO)
        ]
        state["rows"] = rows[:MICRO]
        keys = [dot_nn(r, state["ckv"]).astype(BF) for r in rows]
        state["mem_kv"], state["mem_prev"] = keys[:MICRO], keys[MICRO:]

    def hidden_side():
        (part,) = yield 1, lambda: (jnp.concatenate([mlp_in, mlp_out], axis=0),)
        whole = lax.all_gather(part, "seq", axis=0, tiled=True)
        (whole,) = yield 9, lambda: (whole,)
        whole = whole.reshape(-1, 2, hidden, D)
        state["inner"] = whole[:, 0].reshape(-1, D)
        state["outer"] = whole[:, 1].reshape(-1, D)
        grads = yield 13, lambda: (state["grad_inner"], state["grad_outer"])
        both = [sum(g).astype(BF).reshape(-1, 1, hidden, D) for g in grads]
        both = jnp.concatenate(both, axis=1).reshape(-1, D)
        both = lax.psum_scatter(both, "seq", scatter_dimension=0, tiled=True)
        state["hidden_grads"] = both[:hidden].astype(F32), both[hidden:].astype(F32)

    order = turned[::-1]

    def seq_start(tensor, bit):
        cut = tensor.shape[0] // 2
        return tensor[:cut].astype(F32), flip(tensor[cut:].astype(BF), "seq", bit)

    def seq_next(kept, received, bit):
        return seq_start(kept + received.astype(F32), bit)

    def tree_side(name, arrays, groups, ticks):
        for bit, tick in zip(order, ticks):
            if bit == order[0]:
                arrays = yield tick, lambda: arrays
                pair = seq_start(reorder(arrays, groups, seq, turned), bit)
            else:
                pair = yield tick, lambda: pair
                pair = seq_next(*pair, bit)
        for bit in order[len(ticks) :]:
            pair = seq_next(*pair, bit)
        state[name] = pair

    def half_grads(names):
        arrays = [part for low, mine, others in names for part in (*low, *mine, *others)]
        outs = [shape(D, len(names) * half, F32), shape(D, len(names) * half)]
        return call(functools.partial(half_grads_kernel, len(names)), place, arrays, outs)

    def cout_side():
        names, gains = yield 15, lambda: (state["grad_cout"], state["grad_gain_three"])
        own, other = half_grads([list(zip(*names))])
        gains = jnp.pad((gains[0] + gains[1]).reshape(D, 1), ((0, 0), (0, 127)))
        groups = [[(0, 0, half), (1, 0, half)], [(2, 0, 128)]]
        yield from tree_side("cout", (own, flip(other, "mem", 1), gains), groups, (16, 18, 20))

    def wide_side():
        out, query, ckv = yield 17, lambda: (state["grad_out"], state["grad_cquery"], state["grad_ckv"])
        own, other = half_grads([list(zip(*out)), list(zip(*query))])
        groups = [[(0, 0, 2 * half), (1, 0, 2 * half)], [(2, 0, 2 * width), (3, 0, 2 * width)]]
        yield from tree_side("wide", (own, flip(other, "mem", 1), *ckv), groups, (18, 20, 21))

    def qkv_side():
        arrays = yield 19, lambda: state["grad_qkv"]
        groups = [[(0, 0, 3 * width), (1, 0, 3 * width)]]
        pair = seq_start(reorder(arrays, groups, seq, turned), order[0])
        pair = yield 21, lambda: pair
        state["qkv"] = seq_next(*pair, order[1])

    def spill_of(micro, block):
        ids = lax.dynamic_slice_in_dim(page_ids[micro], jnp.maximum(block, 0) * group, group, 0)
        return jnp.sum((ids < block).astype(jnp.int32))

    for name in ("inner", "outer", "gain_three", "cout", "out", "cquery", "ckv", "qkv"):
        state["grad_" + name] = []
    quarter = [shape(tok, width), shape(tok, width), shape(2 * tok, width)]
    rounded, exact, column = shape(tok, D), shape(tok, D, F32), shape(tok, 1, F32)
    half_rows = shape(tok, half)

    def stream(i):
        spill = spill_of(i, seq)
        self_at = jnp.stack([me, spill, spill_of(i, seq - 1)])
        before = memory_length[i][jnp.maximum(seq - 1, 0)]
        cross_at = jnp.stack([me, spill, before, memory_length[i][seq]])

        low, far_low, ahead, far_ahead = yield lows[i], far_lows[i], befores[i], far_befores[i]
        qkv, kv_prev, low_one, low_before = call(
            qkv_kernel, place, (low, far_low, near_rows(low, far_low), ahead, far_ahead, near_rows(ahead, far_ahead), qkv_full),
            [shape(group, 3 * width), shape(group, 2 * width), shape(group, D), shape(group, D)],
        )
        if i == 0:
            qkv, kv_prev = yield Stay((qkv, kv_prev))
        self_o, self_lse = self_forward(self_at, qkv, kv_prev, blocks)
        self_lse = yield self_lse

        pieces = yield far_slots(self_o)
        self_low, after_self, plain_two, low_two, scale_two, *pieces = call(
            self_out_kernel, place, (*near_slots(*pieces), inputs[i], state["wide_own"], state["wide_other"]),
            [rounded, exact, exact, rounded, column, *quarter],
        )
        scale_two = yield scale_two

        pieces, top = yield (pieces[0], pieces[1], flip(pieces[2], "mem", 2)), cotangent[i]
        far_top = flip(top, "mem", 2)
        mem_kv, mem_prev = state["mem_kv"][i], state["mem_prev"][i]
        cross_o, cross_lse, cross_q = cross_forward(cross_at, near_slots(*pieces), mem_prev, mem_kv, blocks, real)
        cross_lse = yield cross_lse

        pieces, far_top = yield far_slots(cross_o), far_top
        cross_low, after_cross, plain_three, scale_three, low_three = call(
            cross_out_kernel, place,
            (*near_slots(*pieces), after_self, state["cout_own"], state["cout_other"], state["gain"]),
            [rounded, exact, exact, column, rounded],
        )
        near_top = near_rows(top, far_top)
        scale_three = yield scale_three

        low_three, far_three = yield low_three, flip(low_three, "mem", 2)
        whole, pair = shape(group, D), shape(2 * tok, D)
        low_all, top_all, act, pre_low, grad_keep, grad_send, out_keep, out_send = call(
            mlp_kernel, place,
            (low_three, near_rows(low_three, far_three), far_three, top, near_top, far_top, state["inner"], state["outer"]),
            [whole, whole, whole, whole, pair, pair, pair, pair],
        )
        near, far = near_sum(grad_keep, grad_send)
        near = yield near

        far, act, out_send = yield flip(far, "mem", 2), act, out_send
        grad_after_cross, mine, others, gain_three, *pieces = call(
            cross_back_kernel, place,
            (near, far, plain_three, scale_three, state["gain"], cotangent[i], state["cout_own"], state["cout_other"]),
            [exact, half_rows, half_rows, shape(1, D, F32), *quarter],
        )
        state["grad_inner"].append(dot_tn(pre_low, low_all))
        state["grad_outer"].append(dot_tn(act, top_all))
        state["grad_gain_three"].append(gain_three)
        state["grad_cout"].append((cross_low, mine, others))
        out_near, out_far = near_sum(out_keep, out_send)
        grad_after_cross = yield grad_after_cross

        pieces, out_far = yield (pieces[0], pieces[1], flip(pieces[2], "mem", 2)), out_far
        dcq, dmem_prev, dmem = cross_backward(
            cross_at, cross_q, mem_prev, mem_kv, cross_o, near_slots(*pieces), cross_lse, blocks, real
        )
        dmem = yield dmem

        back = shifted(dmem_prev, -1)
        pieces, out_far = yield far_slots(dcq), out_far
        output = (after_cross + out_near + flip(out_far, "mem", 2).astype(F32)).astype(BF)
        grad_after_self, query_mine, query_others, mine, others, *pieces = call(
            self_back_kernel, place,
            (*near_slots(*pieces), plain_two, scale_two, grad_after_cross, state["wide_own"], state["wide_other"]),
            [exact, half_rows, half_rows, half_rows, half_rows, *quarter],
        )
        state["grad_cquery"].append((low_two, query_mine, query_others))
        state["grad_out"].append((self_low, mine, others))
        dmem = (dmem.astype(F32) + back.astype(F32)).astype(BF)
        state["grad_ckv"].append(dot_tn(state["rows"][i], dmem))
        grad_after_self = yield grad_after_self

        pieces, dmem = yield (pieces[0], pieces[1], flip(pieces[2], "mem", 2)), dmem
        dq, dkv, dkv_prev = self_backward(self_at, qkv, kv_prev, self_o, near_slots(*pieces), self_lse, blocks)
        state["grad_qkv"].append(
            call(qkv_grads_kernel, place, (low_one, low_before, dq, dkv, dkv_prev), shape(D, 3 * width, F32))
        )
        mem_part = dot_nt(dmem, state["ckv"]).astype(BF)
        dkv = yield dkv

        back, mem_part = yield shifted(dkv_prev, -1), mem_part
        keep, send = call(qkv_back_kernel, place, (dq, dkv, back, qkv_full), [pair, pair])
        near, far = near_sum(keep, send)
        slots = [mem_part[k * padded : (k + 1) * padded] for k in (0, 2, 1, 3)]
        mem_near, mem_far = near_sum(jnp.concatenate(slots[:2], axis=0), jnp.concatenate(slots[2:], axis=0))
        grad_mem = (mem_near + flip(mem_far, "mem", 2).astype(F32))[:real].reshape(1, real, D)
        near = yield near

        far = yield flip(far, "mem", 2)
        plain_one, scale_one = norm_ones[i]
        grad_x = grad_after_self + normal_back(plain_one, scale_one, near + far.astype(F32))
        return output, grad_x, grad_mem

    sides = [first_side(), last_side(), memory_side(), hidden_side(), cout_side(), wide_side(), qkv_side()]
    done = interleave([stream(i) for i in range(MICRO)], sides)

    def wide_finish(own):
        high = me >> 1
        rows_two = own.reshape(2, 2 * wrows, own.shape[1])
        theirs = lax.dynamic_index_in_dim(rows_two, 1 - high, 0, keepdims=False).astype(BF)
        own = lax.dynamic_index_in_dim(rows_two, high, 0, keepdims=False) + flip(theirs, "mem", 2).astype(F32)
        rows_two = own.reshape(2, wrows, own.shape[1])
        theirs = lax.dynamic_index_in_dim(rows_two, 1 - odd, 0, keepdims=False)
        own = lax.dynamic_index_in_dim(rows_two, odd, 0, keepdims=False)
        return own, flip(theirs.astype(BF), "mem", 1).astype(F32)

    def head_finish(summed, count):
        slots = summed.astype(BF).reshape(blocks, wrows, -1)
        first, second, *rest = [lax.dynamic_index_in_dim(slots, me ^ k, 0, keepdims=False) for k in range(4)]
        far = flip(jnp.concatenate(rest, axis=0), "mem", 2)
        own, near, far = near_slots(first, second, far)
        whole = join_pieces([own, near[:wrows], far[:wrows], near[wrows:]], me, 1).astype(F32)
        whole = whole.reshape(wrows, blocks, count, -1)
        return [whole[:, :, k].reshape(wrows, D) for k in range(count)]

    def seq_finish(pair, left):
        for bit in left:
            pair = seq_next(*pair, bit)
        return pair[0] + pair[1].astype(F32)

    grad_inner, grad_outer = state["hidden_grads"]
    own, near = wide_finish(seq_finish(state["cout"], []))
    grad_cout = join_halves(own[:, :half], near[:, :half])
    grad_gain_mlp = own[:, half] + near[:, half]

    last = seq_finish(state["wide"], [])
    grad_ckey, grad_cvalue = head_finish(last[:, 2 * half :], 2)
    own, near = wide_finish(last[:, : 2 * half])
    grad_out, plain_cquery = [
        join_halves(own[:, k * half : (k + 1) * half], near[:, k * half : (k + 1) * half]) for k in range(2)
    ]
    plain_qkv = head_finish(seq_finish(state["qkv"], order[2:]), 3)

    def gained(gain, weights, plains):
        scale = gain.astype(F32)[:, None]
        grad_gain = sum(jnp.sum(w.astype(F32) * p, axis=1) for w, p in zip(weights, plains))
        return grad_gain, [p * scale for p in plains]

    grad_gain_self, (grad_query, grad_key, grad_value) = gained(
        gain_self, (self_query, self_key, self_value), plain_qkv
    )
    grad_gain_cross, (grad_cquery,) = gained(gain_cross, (cross_query,), (plain_cquery,))
    return (
        jnp.stack([d[0] for d in done]),
        jnp.stack([d[1] for d in done]),
        jnp.stack([d[2] for d in done]),
        grad_gain_self,
        grad_query,
        grad_key,
        grad_value,
        grad_out,
        grad_gain_cross,
        grad_cquery,
        grad_ckey,
        grad_cvalue,
        grad_cout,
        grad_gain_mlp,
        grad_inner,
        grad_outer,
    )


def solution(mesh):
    rows = P(("seq", "mem"), None)
    tokens = P(None, ("seq", "mem"), None)
    pages = P(None, "seq", "mem", None)
    gains = P(("seq", "mem"))
    return jax.shard_map(
        shards,
        mesh=mesh,
        in_specs=(tokens, pages, P(), P(), tokens, gains, rows, rows, rows, rows, gains, rows, rows, rows, rows,
                  gains, rows, rows),
        out_specs=(tokens, tokens, pages, gains, rows, rows, rows, rows, gains, rows, rows, rows, rows, gains,
                   rows, rows),
        check_vma=False,
    )
```

```python
import functools
import jax
import jax.numpy as jnp
import numpy as np
from jax import lax
from jax.experimental import pallas as pl
from jax.experimental.pallas import tpu as pltpu
from jax.sharding import PartitionSpec as P

HEAD = 64
BF = jnp.bfloat16
F32 = jnp.float32
LOWEST = -1e30


def head_lanes(rows, width):
    return lax.broadcasted_iota(jnp.int32, (rows, width), 1) // HEAD


def one_head(block, lanes, head):
    return jnp.where(lanes == head, block, jnp.zeros_like(block))


def dot_nt(left, right):
    return lax.dot_general(left, right, (((1,), (1,)), ((), ())), preferred_element_type=F32)


def dot_nn(left, right):
    return lax.dot_general(left, right, (((1,), (0,)), ((), ())), preferred_element_type=F32)


def dot_tn(left, right):
    return lax.dot_general(left, right, (((0,), (0,)), ((), ())), preferred_element_type=F32)


def self_range(p, rows, blocks, spill, prev_spill):
    first = jnp.where(p * rows < spill, prev_spill // rows, blocks + spill // rows)
    return first, blocks + p + 1


def self_allowed(query, key, extent, spill, prev_spill):
    first = jnp.where(query < spill, prev_spill, extent + spill)
    return (key >= first) & (key <= extent + query)


def cross_allowed(query, place, side, spill, length, me, padded, real):
    part = place // padded
    inner = place - part * padded
    row = (part ^ me) * real + inner
    return (inner < real) & (row < length) & ((query < spill) == (side == 0))


def fold(block, combine):
    total = block[0:8]
    for r in range(8, block.shape[0], 8):
        total = combine(total, block[r : r + 8])
    return total


def lay_heads(out, block, lanes, heads):
    rows = block.shape[0]
    for h in range(heads):
        out[h * rows : (h + 1) * rows, :] = one_head(block, lanes, h)


def score_block(kb, k, allowed, q_cat, s_scr, tops):
    rows = s_scr.shape[3]
    found = []
    for h, top in enumerate(tops):
        s = jnp.where(allowed, dot_nt(k, q_cat[h * rows : (h + 1) * rows, :]), LOWEST)
        s_scr[kb, h] = s
        found.append(jnp.maximum(top, fold(s, jnp.maximum)))
    return tuple(found)


def weigh_block(kb, tops, totals, s_scr, p_scr, v_cat):
    count = s_scr.shape[2]
    summed = []
    for h, (top, total) in enumerate(zip(tops, totals)):
        e = jnp.exp(s_scr[kb, h] - top)
        p_scr[h * count : (h + 1) * count, :] = e.astype(BF)
        summed.append(total + fold(e, jnp.add))
    return tuple(summed), dot_tn(p_scr[...], v_cat)


def attend(first, last, heads, scores, values, s_scr, p_scr, width):
    rows = s_scr.shape[3]
    lowest = jnp.full((8, rows), LOWEST, F32)
    tops = lax.fori_loop(first, last, scores, (lowest,) * heads)
    tops = tuple(jnp.max(top, axis=0, keepdims=True) for top in tops)

    def step(kb, carry):
        totals, acc = carry
        totals, more = weigh_block(kb, tops, totals, s_scr, p_scr, values(kb))
        return totals, acc + more

    start = (jnp.zeros((8, rows), F32),) * heads, jnp.zeros((rows, width), F32)
    totals, acc = lax.fori_loop(first, last, step, start)
    return tops, tuple(jnp.sum(total, axis=0, keepdims=True) for total in totals), acc


def finish(p, start, tops, totals, acc, lanes, o_ref, lse_ref):
    rows = acc.shape[0]
    heads = len(tops)
    inverse = jnp.concatenate([1.0 / total for total in totals] + [jnp.zeros((8 - heads, rows), F32)], axis=0).T
    spread_out = jnp.zeros(acc.shape, F32)
    for h in range(heads):
        spread_out = jnp.where(lanes == h, inverse[:, h : h + 1], spread_out)
    o_ref[pl.ds(start, rows), :] = (acc * spread_out).astype(BF)
    place = pl.ds(pl.multiple_of(p * rows, rows), rows)
    for h in range(heads):
        lse_ref[h : h + 1, place] = tops[h] + jnp.log(totals[h])


def self_forward_kernel(rows, blocks, heads, sc, qkv, kvp, o_ref, lse_ref, k_scr, v_scr, s_scr, q_cat, p_scr):
    width = heads * HEAD
    extent = rows * blocks
    me, spill, prev_spill = sc[0], sc[1], sc[4]
    lanes = head_lanes(rows, width)

    def place(b):
        return pl.multiple_of((b ^ me) * rows, rows)

    first_used, _ = self_range(0, rows, blocks, spill, prev_spill)

    @pl.loop(first_used, 2 * blocks)
    def _(kb):
        def fill(keys, values):
            k_scr[kb] = keys
            lay_heads(v_scr.at[kb], values, lanes, heads)

        @pl.when(kb < blocks)
        def _():
            at = pl.ds(place(kb), rows)
            fill(kvp[at, 0:width], kvp[at, width : 2 * width])

        @pl.when(kb >= blocks)
        def _():
            at = pl.ds(place(kb - blocks), rows)
            fill(qkv[at, width : 2 * width], qkv[at, 2 * width : 3 * width])

    @pl.loop(0, blocks)
    def _(p):
        lay_heads(q_cat, qkv[pl.ds(place(p), rows), 0:width] * jnp.asarray(0.125, BF), lanes, heads)
        first, last = self_range(p, rows, blocks, spill, prev_spill)
        query = p * rows + lax.broadcasted_iota(jnp.int32, (1, rows), 1)

        def scores(kb, tops):
            key = kb * rows + lax.broadcasted_iota(jnp.int32, (rows, rows), 0)
            return score_block(kb, k_scr[kb], self_allowed(query, key, extent, spill, prev_spill), q_cat, s_scr, tops)

        tops, totals, acc = attend(first, last, heads, scores, lambda kb: v_scr[kb], s_scr, p_scr, width)
        finish(p, place(p), tops, totals, acc, lanes, o_ref, lse_ref)


def lay(out, own, near, far):
    rows = own.shape[0]
    out[0:rows, :] = own[...]
    out[rows : 2 * rows, :] = near[0:rows, :]
    out[2 * rows : 3 * rows, :] = far[0:rows, :]
    out[3 * rows :, :] = near[rows:, :]


def cross_forward_kernel(rows, blocks, heads, padded, real, sc, own, near, far, kv0, kv1, o_ref, lse_ref, q_ref,
                         v_scr, s_scr, q_cat, p_scr):
    lay(q_ref, own, near, far)
    width = heads * HEAD
    keys = kv0.shape[0]
    me, spill = sc[0], sc[1]
    lanes = head_lanes(rows, width)
    key_lanes = head_lanes(keys, width)
    kvs = (kv0, kv1)

    def place(b):
        return pl.multiple_of((b ^ me) * rows, rows)

    for side in range(2):
        lay_heads(v_scr.at[side], kvs[side][:, width : 2 * width], key_lanes, heads)

    @pl.loop(0, blocks)
    def _(p):
        lay_heads(q_cat, q_ref[pl.ds(place(p), rows), :] * jnp.asarray(0.125, BF), lanes, heads)
        query = p * rows + lax.broadcasted_iota(jnp.int32, (1, rows), 1)

        def scores(side, tops):
            spot = lax.broadcasted_iota(jnp.int32, (keys, 1), 0)
            length = jnp.where(side == 0, sc[2], sc[3])
            allowed = cross_allowed(query, spot, side, spill, length, me, padded, real)
            k = jnp.where(side == 0, kv0[:, 0:width], kv1[:, 0:width])
            return score_block(side, k, allowed, q_cat, s_scr, tops)

        first = jnp.where(p * rows < spill, 0, 1)
        last = jnp.where((p + 1) * rows > spill, 2, 1)
        tops, totals, acc = attend(first, last, heads, scores, lambda side: v_scr[side], s_scr, p_scr, width)
        finish(p, place(p), tops, totals, acc, lanes, o_ref, lse_ref)


def spread(p, at, rows, heads, q, g, o_ref, lse_ref, lanes, q_cat, g_cat, stat):
    weighted = (g.astype(F32) * o_ref[at, :].astype(F32)).T
    for h in range(heads):
        q_cat[h * rows : (h + 1) * rows, :] = one_head(q, lanes, h)
        g_cat[h * rows : (h + 1) * rows, :] = one_head(g, lanes, h)
        stat[heads + h : heads + h + 1, :] = jnp.sum(weighted[h * HEAD : (h + 1) * HEAD, :], axis=0, keepdims=True)
    stat[0:heads, :] = lse_ref[0:heads, pl.ds(pl.multiple_of(p * rows, rows), rows)]


def back_block(rows, heads, k, v, allowed, q_cat, g_cat, stat, w_scr, ds_wide, ds_tall):
    count = k.shape[0]
    for h in range(heads):
        span = slice(h * rows, (h + 1) * rows)
        s = dot_nt(k, q_cat[span, :])
        e = jnp.where(allowed, jnp.exp(s - stat[h : h + 1, :]), 0.0)
        de = dot_nt(v, g_cat[span, :])
        ds = (e * (de - stat[heads + h : heads + h + 1, :])).astype(BF)
        w_scr[:, span] = e.astype(BF)
        ds_wide[:, span] = ds
        ds_tall[h * count : (h + 1) * count, :] = ds


def self_backward_kernel(rows, blocks, heads, sc, qkv, kvp, o_ref, own, near, far, lse_ref, dq_ref, dkv_ref,
                         dprev_ref, g_ref, kv_scr, k_cat, dkv_scr, q_cat, g_cat, stat, w_scr, ds_wide, ds_tall):
    lay(g_ref, own, near, far)
    width = heads * HEAD
    extent = rows * blocks
    me, spill, prev_spill = sc[0], sc[1], sc[4]
    lanes = head_lanes(rows, width)

    def place(b):
        return pl.multiple_of((b ^ me) * rows, rows)

    first_used, _ = self_range(0, rows, blocks, spill, prev_spill)

    @pl.loop(0, 2 * blocks)
    def _(kb):
        dkv_scr[kb] = jnp.zeros(dkv_scr.shape[1:], F32)

    @pl.loop(first_used, 2 * blocks)
    def _(kb):
        def fill(pair):
            kv_scr[kb] = pair
            scaled = pair[:, 0:width] * jnp.asarray(0.125, BF)
            for h in range(heads):
                k_cat[kb, h * rows : (h + 1) * rows, :] = one_head(scaled, lanes, h)

        @pl.when(kb < blocks)
        def _():
            fill(kvp[pl.ds(place(kb), rows), :])

        @pl.when(kb >= blocks)
        def _():
            fill(qkv[pl.ds(place(kb - blocks), rows), width : 3 * width])

    @pl.loop(0, blocks)
    def _(p):
        at = pl.ds(place(p), rows)
        q = qkv[at, 0:width] * jnp.asarray(0.125, BF)
        g = g_ref[at, :]
        spread(p, at, rows, heads, q, g, o_ref, lse_ref, lanes, q_cat, g_cat, stat)
        first, last = self_range(p, rows, blocks, spill, prev_spill)
        query = p * rows + lax.broadcasted_iota(jnp.int32, (1, rows), 1)

        def step(kb, dq):
            key = kb * rows + lax.broadcasted_iota(jnp.int32, (rows, 1), 0)
            allowed = self_allowed(query, key, extent, spill, prev_spill)
            back_block(rows, heads, kv_scr[kb, :, 0:width], kv_scr[kb, :, width : 2 * width], allowed,
                       q_cat, g_cat, stat, w_scr, ds_wide, ds_tall)
            dkv_scr[kb, :, 0:width] += dot_nn(ds_wide[...], q_cat[...])
            dkv_scr[kb, :, width : 2 * width] += dot_nn(w_scr[...], g_cat[...])
            return dq + dot_tn(ds_tall[...], k_cat[kb])

        dq = lax.fori_loop(first, last, step, jnp.zeros((rows, width), F32))
        dq_ref[at, :] = dq.astype(BF)

    @pl.loop(0, blocks)
    def _(b):
        at = pl.ds(place(b), rows)
        dprev_ref[at, :] = dkv_scr[b].astype(BF)
        dkv_ref[at, :] = dkv_scr[blocks + b].astype(BF)


def cross_backward_kernel(rows, blocks, heads, padded, real, pieces, sc, q_ref, kv0, kv1, o_ref, own, near, far,
                          lse_ref, dq_ref, dkv0_ref, dkv1_ref, g_ref, k_cat, dkv_scr, q_cat, g_cat, stat, w_scr, ds_wide, ds_tall):
    lay(g_ref, own, near, far)
    width = heads * HEAD
    keys = kv0.shape[0]
    step_keys = keys // pieces
    me, spill = sc[0], sc[1]
    lanes = head_lanes(rows, width)
    key_lanes = head_lanes(step_keys, width)
    kvs = (kv0, kv1)

    def place(b):
        return pl.multiple_of((b ^ me) * rows, rows)

    dkv_scr[...] = jnp.zeros(dkv_scr.shape, F32)
    for side in range(2):
        for piece in range(pieces):
            scaled = kvs[side][piece * step_keys : (piece + 1) * step_keys, 0:width] * jnp.asarray(0.125, BF)
            for h in range(heads):
                k_cat[side * pieces + piece, h * step_keys : (h + 1) * step_keys, :] = one_head(scaled, key_lanes, h)

    @pl.loop(0, blocks)
    def _(p):
        at = pl.ds(place(p), rows)
        q = q_ref[at, :] * jnp.asarray(0.125, BF)
        spread(p, at, rows, heads, q, g_ref[at, :], o_ref, lse_ref, lanes, q_cat, g_cat, stat)
        query = p * rows + lax.broadcasted_iota(jnp.int32, (1, rows), 1)
        reads = (p * rows < spill, (p + 1) * rows > spill)
        first = jnp.where(reads[0], 0, pieces)
        last = jnp.where(reads[1], 2 * pieces, pieces)

        def step(kb, dq):
            side = kb // pieces
            at_key = pl.ds(pl.multiple_of((kb - side * pieces) * step_keys, step_keys), step_keys)
            spot = (kb - side * pieces) * step_keys + lax.broadcasted_iota(jnp.int32, (step_keys, 1), 0)
            length = jnp.where(side == 0, sc[2], sc[3])
            allowed = cross_allowed(query, spot, side, spill, length, me, padded, real)
            is_prev = side == 0
            pair = jnp.where(is_prev, kv0[at_key, :], kv1[at_key, :])
            back_block(rows, heads, pair[:, 0:width], pair[:, width : 2 * width], allowed,
                       q_cat, g_cat, stat, w_scr, ds_wide, ds_tall)
            dkv_scr[kb, :, 0:width] += dot_nn(ds_wide[...], q_cat[...])
            dkv_scr[kb, :, width : 2 * width] += dot_nn(w_scr[...], g_cat[...])
            return dq + dot_tn(ds_tall[...], k_cat[kb])

        dq = lax.fori_loop(first, last, step, jnp.zeros((rows, width), F32))
        dq_ref[at, :] = dq.astype(BF)

    for piece in range(pieces):
        span = slice(piece * step_keys, (piece + 1) * step_keys)
        dkv0_ref[span, :] = dkv_scr[piece].astype(BF)
        dkv1_ref[span, :] = dkv_scr[pieces + piece].astype(BF)


def call(kernel, scalars, arrays, outs, scratch=(), time=2):
    vmem = pl.BlockSpec(memory_space=pltpu.VMEM)
    return pl.pallas_call(
        kernel,
        out_shape=outs,
        in_specs=[pl.BlockSpec(memory_space=pltpu.SMEM)] + [vmem] * len(arrays),
        out_specs=jax.tree.map(lambda _: vmem, outs),
        scratch_shapes=scratch,
        compiler_params=pltpu.CompilerParams(vmem_limit_bytes=48 * 2**20),
        cost_estimate=pl.CostEstimate(flops=1024, bytes_accessed=int(time * 640000), transcendentals=0),
    )(scalars, *arrays)


def self_forward(scalars, qkv, kvp, blocks):
    extent = qkv.shape[0]
    rows = extent // blocks
    width = qkv.shape[1] // 3
    heads = width // HEAD
    return call(
        functools.partial(self_forward_kernel, rows, blocks, heads),
        scalars,
        (qkv, kvp),
        [jax.ShapeDtypeStruct((extent, width), BF), jax.ShapeDtypeStruct((8, extent), F32)],
        [
            pltpu.VMEM((2 * blocks, rows, width), BF),
            pltpu.VMEM((2 * blocks, heads * rows, width), BF),
            pltpu.VMEM((2 * blocks, heads, rows, rows), F32),
            pltpu.VMEM((heads * rows, width), BF),
            pltpu.VMEM((heads * rows, rows), BF),
        ],
        time=18,
    )


def cross_forward(scalars, pieces, kv0, kv1, blocks, real):
    rows, width = pieces[0].shape
    extent = rows * blocks
    heads = width // HEAD
    keys = kv0.shape[0]
    return call(
        functools.partial(cross_forward_kernel, rows, blocks, heads, keys // blocks, real),
        scalars,
        (*pieces, kv0, kv1),
        [
            jax.ShapeDtypeStruct((extent, width), BF),
            jax.ShapeDtypeStruct((8, extent), F32),
            jax.ShapeDtypeStruct((extent, width), BF),
        ],
        [
            pltpu.VMEM((2, heads * keys, width), BF),
            pltpu.VMEM((2, heads, keys, rows), F32),
            pltpu.VMEM((heads * rows, width), BF),
            pltpu.VMEM((heads * keys, rows), BF),
        ],
        time=9,
    )


def back_scratch(rows, heads, width, keys):
    return [
        pltpu.VMEM((heads * rows, width), BF),
        pltpu.VMEM((heads * rows, width), BF),
        pltpu.VMEM((8, rows), F32),
        pltpu.VMEM((keys, heads * rows), BF),
        pltpu.VMEM((keys, heads * rows), BF),
        pltpu.VMEM((heads * keys, rows), BF),
    ]


def self_backward(scalars, qkv, kvp, o, g, lse, blocks):
    extent = qkv.shape[0]
    rows = extent // blocks
    width = qkv.shape[1] // 3
    heads = width // HEAD
    return call(
        functools.partial(self_backward_kernel, rows, blocks, heads),
        scalars,
        (qkv, kvp, o, *g, lse),
        [
            jax.ShapeDtypeStruct((extent, width), BF),
            jax.ShapeDtypeStruct((extent, 2 * width), BF),
            jax.ShapeDtypeStruct((extent, 2 * width), BF),
        ],
        [
            pltpu.VMEM((extent, width), BF),
            pltpu.VMEM((2 * blocks, rows, 2 * width), BF),
            pltpu.VMEM((2 * blocks, heads * rows, width), BF),
            pltpu.VMEM((2 * blocks, rows, 2 * width), F32),
        ]
        + back_scratch(rows, heads, width, rows),
        time=22,
    )


def cross_backward(scalars, q, kv0, kv1, o, g, lse, blocks, real, pieces=1):
    extent, width = q.shape
    rows = extent // blocks
    heads = width // HEAD
    keys = kv0.shape[0]
    step_keys = keys // pieces
    return call(
        functools.partial(cross_backward_kernel, rows, blocks, heads, keys // blocks, real, pieces),
        scalars,
        (q, kv0, kv1, o, *g, lse),
        [
            jax.ShapeDtypeStruct((extent, width), BF),
            jax.ShapeDtypeStruct((keys, 2 * width), BF),
            jax.ShapeDtypeStruct((keys, 2 * width), BF),
        ],
        [
            pltpu.VMEM((extent, width), BF),
            pltpu.VMEM((2 * pieces, heads * step_keys, width), BF),
            pltpu.VMEM((2 * pieces, step_keys, 2 * width), F32),
        ]
        + back_scratch(rows, heads, width, step_keys),
        time=14,
    )


def ordered_pieces(pieces, me):
    odd = (me & 1) == 1
    high = (me & 2) == 2
    low_pair = [jnp.where(odd, pieces[1 - i], pieces[i]) for i in range(2)]
    high_pair = [jnp.where(odd, pieces[3 - i], pieces[2 + i]) for i in range(2)]
    ordered = [jnp.where(high, high_pair[i], low_pair[i]) for i in range(2)]
    return ordered + [jnp.where(high, low_pair[i], high_pair[i]) for i in range(2)]


def join_pieces(pieces, me, axis):
    return jnp.concatenate(ordered_pieces(pieces, me), axis=axis)


def received(own, near, far, me):
    rows = own.shape[0]
    return join_pieces([own[...], near[0:rows, :], far[0:rows, :], near[rows:, :]], me, 1)


def send_pieces(tensor, me, first, second, rest):
    width = tensor.shape[1] // 4
    rows = tensor.shape[0]
    pieces = ordered_pieces([tensor[:, k * width : (k + 1) * width] for k in range(4)], me)
    first[...] = pieces[0]
    second[...] = pieces[1]
    rest[0:rows, :] = pieces[2]
    rest[rows:, :] = pieces[3]


def half_product(tensor, own, other, me, first):
    span = slice(first, first + own.shape[0] // 2)
    left, right = dot_nn(tensor, own[:, span]), dot_nn(tensor, other[:, span])
    odd = (me & 1) == 1
    return jnp.concatenate([jnp.where(odd, right, left), jnp.where(odd, left, right)], axis=1)


def two_halves(tensor, me):
    half = tensor.shape[1] // 2
    odd = (me & 1) == 1
    left, right = tensor[:, 0:half], tensor[:, half:]
    return jnp.where(odd, right, left), jnp.where(odd, left, right)


def half_back(mine, others, own, other, first):
    span = slice(first, first + own.shape[0] // 2)
    return dot_nt(mine, own[:, span]) + dot_nt(others, other[:, span])


def normal_parts(tensor):
    average = jnp.mean(tensor, axis=-1, keepdims=True)
    centered = tensor - average
    scale = lax.rsqrt(jnp.mean(centered * centered, axis=-1, keepdims=True) + 1e-05)
    return centered * scale, scale


def normal_back(plain, scale, grad):
    inner = jnp.mean(grad * plain, axis=-1, keepdims=True)
    return scale * (grad - jnp.mean(grad, axis=-1, keepdims=True) - plain * inner)


def gelu_parts(pre):
    size = jnp.abs(pre)
    t = 1.0 / (1.0 + (0.3275911 * 0.7071067811865476) * size)
    poly = ((((1.061405429 * t - 1.453152027) * t + 1.421413741) * t - 0.284496736) * t + 0.254829592) * t
    bell = jnp.exp(-0.5 * pre * pre)
    tail = 0.5 * poly * bell
    cdf = jnp.where(pre < 0.0, tail, 1.0 - tail)
    return pre * cdf, cdf + pre * bell * 0.3989422804014327


def place_kernel(group, at, lengths, ids, *outs):
    seq, me = at[0], at[1]
    before = jnp.maximum(seq - 1, 0)
    for i, out in enumerate(outs):
        out[0] = me
        out[2] = lengths[i, before]
        out[3] = lengths[i, seq]
        for slot, block, number in ((1, seq, seq), (4, before, seq - 1)):
            rows = group // 128
            part = ids[i, pl.ds(pl.multiple_of(block * rows, rows), rows), :]
            out[slot] = jnp.sum(jnp.where(part < number, 1.0, 0.0)).astype(jnp.int32)
        for slot in (5, 6, 7):
            out[slot] = 0


def norm_kernel(at, x, low):
    rows = 256
    for start in range(0, low.shape[0], rows):
        span = slice(start, min(start + rows, low.shape[0]))
        low[span, :] = normal_parts(x[span, :].astype(F32))[0].astype(BF)


def lay_four(out, own, near, far, last):
    rows = own.shape[0]
    for k, ref in enumerate((own, near, far, last)):
        out[k * rows : (k + 1) * rows, :] = ref[...]


def qkv_kernel(i, rows, at, *refs):
    weight, qkv, kvp = refs[8:]
    width = weight.shape[1] // 3
    own = slice(i * rows, (i + 1) * rows)
    for k in range(4):
        block = slice(k * rows, (k + 1) * rows)
        qkv[block, :] = dot_nn(refs[k][own, :], weight[...]).astype(BF)
        kvp[block, :] = dot_nn(refs[4 + k][own, :], weight[:, width:]).astype(BF)


def memory_kernel(size, at, own, near, far, last, weight, *outs):
    count = len(outs) // 2
    rows, keys = outs[:count], outs[count:]
    for i in range(count):
        span = slice(i * size, (i + 1) * size)
        block = jnp.concatenate([ref[span, :] for ref in (own, near, far, last)], axis=0)
        rows[i][...] = block
        keys[i][...] = dot_nn(block, weight[...]).astype(BF)


def hidden_kernel(rows, at, whole, inner, outer):
    slot = 2 * rows
    for i in range(inner.shape[0] // rows):
        inner[i * rows : (i + 1) * rows, :] = whole[i * slot : i * slot + rows, :]
        outer[i * rows : (i + 1) * rows, :] = whole[i * slot + rows : i * slot + 2 * rows, :]


def hidden_grads_kernel(rows, at, pre_low, low, act, top, *refs):
    before, out = (refs[0], refs[1]) if len(refs) == 2 else (None, refs[0])
    step, slot = 256, 2 * rows
    for i in range(pre_low.shape[1] // step):
        for k, (left, right) in enumerate(((pre_low, low), (act, top))):
            grad = dot_tn(left[:, i * step : (i + 1) * step], right[...])
            for part in range(step // rows):
                start = (i * step // rows + part) * slot + k * rows
                block = grad[part * rows : (part + 1) * rows]
                if before is not None:
                    block = block + before[start : start + rows, :].astype(F32)
                out[start : start + rows, :] = block.astype(BF)


def near_kernel(at, keep, received, near, far):
    rows = near.shape[0]
    near[...] = keep[0:rows, :].astype(F32) + received[0:rows, :].astype(F32)
    far[...] = (keep[rows:, :].astype(F32) + received[rows:, :].astype(F32)).astype(BF)


def tree_kernel(at, keep, received, kept, sent):
    rows = kept.shape[0]
    kept[...] = keep[0:rows, :] + received[0:rows, :].astype(F32)
    sent[...] = (keep[rows:, :] + received[rows:, :].astype(F32)).astype(BF)


def output_kernel(at, after, near, far, out):
    out[...] = (after[...] + near[...] + far[...].astype(F32)).astype(BF)


def grad_x_kernel(i, at, x, before, near, far, back, out):
    rows = out.shape[0]
    plain, scale = normal_parts(x[i * rows : (i + 1) * rows, :].astype(F32))
    grad = near[...] + far[...].astype(F32) + back[...].astype(F32)
    out[...] = before[...] + normal_back(plain, scale, grad)


def far_sum_kernel(at, near, far, out):
    out[...] = (near[...] + far[...].astype(F32)).astype(BF)


def memory_back_kernel(at, own, prev, rows_own, rows_prev, weight, grad, keep, send):
    grad[...] = dot_tn(rows_own[...], own[...]) + dot_tn(rows_prev[...], prev[...])
    rows = own.shape[0] // 4
    for k, part in enumerate((own, prev)):
        part = dot_nt(part[...], weight[...]).astype(BF)
        for slot, out, place in ((0, keep, 0), (1, send, 0), (2, keep, 2), (3, send, 2)):
            out[(place + k) * rows : (place + k + 1) * rows, :] = part[slot * rows : (slot + 1) * rows]


def self_out_kernel(i, at, own, near, far, x, wide_own, wide_other,
                    low, after, plain, low_next, scale, first, second, rest):
    me = at[0]
    joined = received(own, near, far, me)
    low[...] = joined
    rows = low.shape[0]
    total = x[i * rows : (i + 1) * rows, :].astype(F32) + half_product(joined, wide_own, wide_other, me, 0)
    after[...] = total
    normed, scaled = normal_parts(total)
    plain[...] = normed
    scale[...] = scaled
    rounded = normed.astype(BF)
    low_next[...] = rounded
    send_pieces(half_product(rounded, wide_own, wide_other, me, wide_own.shape[0] // 2).astype(BF), me, first, second, rest)


def cross_out_kernel(at, own, near, far, before, out_own, out_other, gain, low, after, plain, scale, low_next):
    me = at[0]
    joined = received(own, near, far, me)
    low[...] = joined
    total = before[...] + half_product(joined, out_own, out_other, me, 0)
    after[...] = total
    normed, scaled = normal_parts(total)
    plain[...] = normed
    scale[...] = scaled
    low_next[...] = (normed * gain[...]).astype(BF)


def mlp_kernel(i, at, low, near_low, far_low, last_low, top, near_top, far_top, last_top, inner, outer,
               low_all, top_all, act, pre_low, grad_keep, grad_send, out_keep, out_send):
    rows = low.shape[0]
    lay_four(low_all, low, near_low, far_low, last_low)
    lay_four(top_all, *(ref.at[i * rows : (i + 1) * rows, :] for ref in (top, near_top, far_top, last_top)))
    for parity, grad, out in ((1, grad_send, out_send), (0, grad_keep, out_keep)):

        @pl.loop(0, 2)
        def _(b):
            block = pl.ds(pl.multiple_of((2 * b + parity) * rows, rows), rows)
            place = pl.ds(pl.multiple_of(b * rows, rows), rows)
            value, slope = gelu_parts(dot_nt(low_all[block, :], inner[...]))
            act_block = value.astype(BF)
            act[block, :] = act_block
            pre_block = (dot_nt(top_all[block, :], outer[...]) * slope).astype(BF)
            pre_low[block, :] = pre_block
            grad[place, :] = dot_nn(pre_block, inner[...]).astype(BF)
            out[place, :] = dot_nn(act_block, outer[...]).astype(BF)


def cross_back_kernel(i, at, near, far, plain, scale, gain, top, out_own, out_other,
                      grad_after, branch_own, branch_other, grad_gain, first, second, rest):
    me = at[0]
    grad = near[...] + far[...].astype(F32)
    normed = plain[...]
    grad_gain[...] = jnp.sum(grad * normed, axis=0, keepdims=True)
    rows = near.shape[0]
    total = top[i * rows : (i + 1) * rows, :].astype(F32) + normal_back(normed, scale[...], grad * gain[...])
    grad_after[...] = total
    mine, others = two_halves(total.astype(BF), me)
    branch_own[...] = mine
    branch_other[...] = others
    send_pieces(half_back(mine, others, out_own, out_other, 0).astype(BF), me, first, second, rest)


def self_back_kernel(at, own, near, far, plain, scale, before, wide_own, wide_other,
                     grad_after, query_mine, query_others, branch_own, branch_other, first, second, rest):
    me = at[0]
    mine, others = two_halves(received(own, near, far, me), me)
    query_mine[...] = mine
    query_others[...] = others
    total = before[...] + normal_back(plain[...], scale[...], half_back(mine, others, wide_own, wide_other, wide_own.shape[0] // 2))
    grad_after[...] = total
    mine, others = two_halves(total.astype(BF), me)
    branch_own[...] = mine
    branch_other[...] = others
    send_pieces(half_back(mine, others, wide_own, wide_other, 0).astype(BF), me, first, second, rest)


def half_grads_kernel(names, at, *refs):
    own, other = refs[-2:]
    half = own.shape[1] // names
    for n in range(names):
        low_a, low_b, mine_a, mine_b, others_a, others_b = (ref[...] for ref in refs[6 * n : 6 * n + 6])
        span = slice(n * half, (n + 1) * half)
        other[:, span] = (dot_tn(low_a, others_a) + dot_tn(low_b, others_b)).astype(BF)
        own[:, span] = dot_tn(low_a, mine_a) + dot_tn(low_b, mine_b)


def qkv_back_kernel(at, dq, dkv, dkv_prev, weight, keep, send, keep_prev, send_prev):
    rows = dq.shape[0] // 4
    width = dq.shape[1]
    for parity, out, out_prev in ((1, send, send_prev), (0, keep, keep_prev)):
        for b in range(2):
            block = slice((2 * b + parity) * rows, (2 * b + parity + 1) * rows)
            place = slice(b * rows, (b + 1) * rows)
            grad = dot_nt(dq[block, :], weight[:, 0:width]) + dot_nt(dkv[block, :], weight[:, width:])
            out[place, :] = grad.astype(BF)
            out_prev[place, :] = dot_nt(dkv_prev[block, :], weight[:, width:]).astype(BF)


def qkv_grads(i, refs, dq, dkv, dkv_prev):
    rows = dq.shape[0] // 4
    own = slice(i * rows, (i + 1) * rows)
    queries, others = None, None
    for k in range(4):
        block = slice(k * rows, (k + 1) * rows)
        low, before = refs[k][own, :], refs[4 + k][own, :]
        query = dot_tn(low, dq[block, :])
        other = dot_tn(low, dkv[block, :]) + dot_tn(before, dkv_prev[block, :])
        queries, others = (query, other) if k == 0 else (queries + query, others + other)
    return queries, others


def qkv_grads_kernel(i, at, *refs):
    dq, dkv, dkv_prev, out = refs[8:]
    width = dq.shape[1]
    out[:, 0:width], out[:, width:] = qkv_grads(i, refs, dq, dkv, dkv_prev)


def last_qkv_grads_kernel(i, offsets, at, *refs):
    dq, dkv, dkv_prev, earlier, keep, send, total = refs[8:]
    width = dq.shape[1]
    queries, others = qkv_grads(i, refs, dq, dkv, dkv_prev)
    total[:, 0:width] = earlier[:, 0:width] + queries
    total[:, width:] = earlier[:, width:] + others
    half = len(offsets) // 2
    rows = total.shape[0] // len(offsets)
    for i, offset in enumerate(offsets):
        out = keep if i < half else send
        start = pl.multiple_of((at[0] ^ offset) * rows, rows)
        out[(i % half) * rows : (i % half + 1) * rows, :] = total[pl.ds(start, rows), :].astype(out.dtype)


def shape(rows, columns, dtype=BF):
    return jax.ShapeDtypeStruct((rows, columns), dtype)


D = 1024
MICRO = 2


def flip(block, axis, bit):
    return lax.ppermute(block, axis, [(i, i ^ bit) for i in range(lax.axis_size(axis))])


def shifted(block, distance):
    devices = range(lax.axis_size("seq"))
    route = [(i - distance, i) for i in devices if i - distance in devices]
    return lax.ppermute(block, "seq", route)


def far_slots(part):
    rows = part.shape[0] // 4
    return part[:rows], part[rows : 2 * rows], flip(part[2 * rows :], "mem", 2)


def near_slots(own, side, far):
    rows = own.shape[0]
    return own, flip(jnp.concatenate([side, far[rows:]], axis=0), "mem", 1), far


def near_sum(place, keep, send):
    rows, columns = keep.shape
    outs = [shape(rows // 2, columns, F32), shape(rows // 2, columns)]
    return call(near_kernel, place, (keep, flip(send, "mem", 1)), outs, time=1)


def seq_bits():
    count = lax.axis_size("seq")
    return [1 << i for i in reversed(range(count.bit_length() - 1))]


def seq_offsets(bits):
    offsets = [0]
    for bit in bits:
        offsets = offsets + [o ^ bit for o in offsets]
    return offsets


def seq_stage(block, bit):
    return jnp.concatenate([block, flip(block, "seq", bit)], axis=0)


def assemble_kernel(rows, offsets, at, first, second, *outs):
    half = len(offsets) // 2
    for i, offset in enumerate(offsets):
        ref = first if i < half else second
        start = pl.multiple_of((at[0] ^ offset) * rows, rows)
        column = 0
        for out in outs:
            columns = out.shape[1]
            place = slice((i % half) * rows, (i % half + 1) * rows)
            out[pl.ds(start, rows), :] = ref[place, column : column + columns]
            column += columns


def assemble(first, second, seq, bits, split):
    offsets = seq_offsets(bits)
    size = 2 * first.shape[0]
    outs = [shape(size, columns) for columns in split]
    return call(functools.partial(assemble_kernel, size // len(offsets), offsets), seq.reshape(1), (first, second), outs)


def reorder_kernel(rows, offsets, groups, at, *refs):
    keep, send = refs[-2:]
    half = len(offsets) // 2
    for i, offset in enumerate(offsets):
        start = pl.multiple_of((at[0] ^ offset) * rows, rows)
        out = keep if i < half else send
        place = slice((i % half) * rows, (i % half + 1) * rows)
        for column, terms in groups:
            total = None
            for term, first, columns in terms:
                part = refs[term][pl.ds(start, rows), first : first + columns].astype(F32)
                total = part if total is None else total + part
            out[place, column : column + columns] = total.astype(out.dtype)


def reorder(arrays, groups, seq, bits):
    offsets = seq_offsets(bits)
    size = arrays[0].shape[0]
    placed, column = [], 0
    for terms in groups:
        placed.append((column, terms))
        column += terms[0][2]
    kernel = functools.partial(reorder_kernel, size // len(offsets), offsets, placed)
    return call(kernel, seq.reshape(1), arrays, [shape(size // 2, column, F32), shape(size // 2, column)], time=column // 300)


def pack_kernel(width, half, at, *refs):
    me = at[0]
    (gain_self, gain_cross, gain_mlp), weights, (kept, message) = refs[:3], refs[3:11], refs[11:]
    query, key, value, out_w, cross_q, cross_k, cross_v, cross_o = weights

    def scaled(weight, gain):
        return (weight.astype(F32) * gain[...].astype(F32)).astype(BF)

    def piece(k):
        at_k = pl.ds(pl.multiple_of((me ^ k) * width, width), width)
        gained = [scaled(w[:, at_k], gain_self) for w in (query, key, value)]
        return jnp.concatenate(gained + [w[:, at_k] for w in (cross_k, cross_v)], axis=1)

    def side(k):
        at_k = pl.ds(pl.multiple_of(((me & 1) ^ k) * half, half), half)
        rows = gain_mlp.shape[0]
        lanes = lax.broadcasted_iota(jnp.int32, (rows, 128), 1)
        extra = jnp.where(lanes == 0, gain_mlp[...].astype(F32), 0.0).astype(BF)
        return jnp.concatenate([out_w[:, at_k], scaled(cross_q[:, at_k], gain_cross), cross_o[:, at_k], extra], axis=1)

    kept[...] = jnp.concatenate([piece(0), piece(1)], axis=1)
    message[...] = jnp.concatenate([piece(2), piece(3), side(0), side(1)], axis=1)


def repack_kernel(narrow, broad, at, kept, message, far, out):
    sides = 2 * narrow + broad
    out[:, 0:narrow] = kept[:, narrow:]
    out[:, narrow : 2 * narrow] = far[:, narrow : 2 * narrow]
    out[:, 2 * narrow : 2 * narrow + broad] = message[:, sides:]
    out[:, 2 * narrow + broad :] = far[:, sides:]


def unpack_kernel(width, narrow, broad, at, kept, message, far, near, qkv, first):
    me = at[0]
    start = 2 * narrow
    heads = [kept[:, 0:narrow], near[:, 0:narrow], far[:, 0:narrow], near[:, narrow:start]]
    sides = [message, near, far, near]
    sides = [ref[:, at_k : at_k + broad] for ref, at_k in zip(sides, (start, start, start, start + broad))]
    heads = join_pieces(heads, me, 0)
    sides = join_pieces(sides, me, 0)
    qkv[...] = heads[:, 0 : 3 * width]
    pair = broad - 128 - (broad - 128) // 3
    first[...] = jnp.concatenate([sides[:, 0:pair], heads[:, 3 * width :], sides[:, pair:]], axis=1)


class Stay:
    def __init__(self, value):
        self.value = value


def interleave(streams, sides):
    held = [next(s) for s in streams]
    results = [None] * len(streams)
    waiting = [(side, *next(side)) for side in sides]
    turn = 0
    ticks = 0

    def serve(arrays):
        nonlocal ticks, waiting
        ticks += 1
        due = [w for w in waiting if w[1] == ticks]
        waiting = [w for w in waiting if w[1] != ticks]
        arrays, taken = lax.optimization_barrier((arrays, [w[2]() for w in due]))
        for (side, _, _), got in zip(due, taken):
            try:
                waiting.append((side, *side.send(got)))
            except StopIteration:
                pass
        return arrays

    while True:
        other = (turn + 1) % len(streams)
        try:
            mark = streams[turn].send(held[turn])
            while isinstance(mark, Stay):
                mark = streams[turn].send(serve(mark.value))
            if results[other] is None:
                held[other], mark = serve((held[other], mark))
            else:
                mark = serve(mark)
            held[turn] = streams[turn].send(mark)
        except StopIteration as end:
            results[turn] = end.value
        if results[other] is None:
            turn = other
        elif results[turn] is not None:
            assert not waiting
            return results


def shards(
    inputs,
    memory,
    page_ids,
    memory_length,
    cotangent,
    gain_self,
    self_query,
    self_key,
    self_value,
    self_out,
    gain_cross,
    cross_query,
    cross_key,
    cross_value,
    cross_out,
    gain_mlp,
    mlp_in,
    mlp_out,
):
    seq = lax.axis_index("seq")
    me = lax.axis_index("mem")
    odd = me & 1
    blocks = lax.axis_size("mem")
    tok = inputs.shape[1]
    group = tok * blocks
    real = memory.shape[2]
    padded = -(-real // 16) * 16
    wrows = self_query.shape[0]
    bits = seq_bits()
    turned = bits[:-2] + [bits[-1], bits[-2]]
    half = D // 2

    def join_halves(own, other):
        return jnp.concatenate([jnp.where(odd == 0, own, other), jnp.where(odd == 0, other, own)], axis=1)

    width = self_query.shape[1] // blocks
    narrow, broad = 5 * width, 3 * half + 128
    place = me.reshape(1)
    weights = (self_query, self_key, self_value, self_out, cross_query, cross_key, cross_value, cross_out)
    gains = [g[:, None] for g in (gain_self, gain_cross, gain_mlp)]
    kept, message = call(
        functools.partial(pack_kernel, width, half), place, (*gains, *weights),
        [shape(wrows, 2 * narrow), shape(wrows, 2 * (narrow + broad))],
    )
    far = flip(message, "mem", 2)
    x_rows, tops = inputs.reshape(MICRO * tok, D), cotangent.reshape(MICRO * tok, D)
    lows = call(norm_kernel, place, (x_rows,), shape(MICRO * tok, D))
    far, lows = lax.optimization_barrier((far, lows))
    befores = shifted(lows, 1)
    far_lows, near_lows = flip(lows, "mem", 2), flip(lows, "mem", 1)
    memory_own = jnp.pad(memory.reshape(MICRO, real, D), ((0, 0), (0, padded - real), (0, 0)))
    memory_own = memory_own.reshape(MICRO * padded, D)
    smem = pl.BlockSpec(memory_space=pltpu.SMEM)
    ids = page_ids.reshape(MICRO, -1, 128)
    places = pl.pallas_call(
        functools.partial(place_kernel, group),
        out_shape=[jax.ShapeDtypeStruct((8,), jnp.int32)] * MICRO,
        in_specs=[smem, smem, pl.BlockSpec(memory_space=pltpu.VMEM)],
        out_specs=[smem] * MICRO,
    )(jnp.stack([seq, me]), memory_length, ids)
    near = call(
        functools.partial(repack_kernel, narrow, broad), place, (kept, message, far),
        shape(*message.shape),
    )
    near = flip(near, "mem", 1)
    qkv_part, first_part = call(
        functools.partial(unpack_kernel, width, narrow, broad), place, (kept, message, far, near),
        [shape(blocks * wrows, columns) for columns in (3 * width, 3 * half + 128 + 2 * width)],
    )

    state = {}
    hidden = mlp_in.shape[0]
    stage = seq_stage(qkv_part, bits[0])
    hidden_part = jnp.concatenate([mlp_in, mlp_out], axis=0)
    stage, memory_own, places, hidden_part = lax.optimization_barrier((stage, memory_own, places, hidden_part))
    memory_before = shifted(memory_own, 1)
    for bit in bits[1:-1]:
        stage = seq_stage(stage, bit)
    stage, first_part, befores, far_lows = lax.optimization_barrier((stage, first_part, befores, far_lows))
    last_lows = flip(far_lows, "mem", 1)
    far_befores, near_befores = flip(befores, "mem", 2), flip(befores, "mem", 1)
    first_stage = first_part
    for bit in bits[:-2]:
        first_stage = seq_stage(first_stage, bit)
    (qkv_full,) = assemble(stage, flip(stage, "seq", bits[-1]), seq, bits, [3 * width])
    gathered = [lows, near_lows, far_lows, last_lows, befores, near_befores, far_befores, flip(far_befores, "mem", 1)]

    def first_side():
        (first,) = yield 1, lambda: (first_stage,)
        first = seq_stage(first, bits[-2])
        (first,) = yield 2, lambda: (first,)
        cut = 2 * half + 2 * width
        first, last = first[:, :cut], first[:, cut:]
        first = first, flip(first, "seq", bits[-1])
        *first, last = yield 3, lambda: (*first, last)
        state["wide_own"], state["ckv"] = assemble(*first, seq, bits, [2 * half, 2 * width])
        state["wide_other"] = flip(state["wide_own"], "mem", 1)
        last = last, flip(last, "seq", bits[-1])
        last = yield 5, lambda: last
        state["cout_own"], gain = assemble(*last, seq, bits, [half, 128])
        state["gain"] = gain[:, 0].astype(F32)[None, :]
        (own,) = yield 6, lambda: (state["cout_own"],)
        state["cout_other"] = flip(own, "mem", 1)

    def memory_side():
        rows = yield 1, lambda: (memory_own, memory_before)
        rows = jnp.concatenate(rows, axis=0)
        far, near = flip(rows, "mem", 2), flip(rows, "mem", 1)
        rows, near, far = yield 3, lambda: (rows, near, far)
        pieces = rows, near, far, flip(far, "mem", 1)
        pieces = yield 4, lambda: pieces
        whole = blocks * padded
        outs = [shape(whole, D)] * (2 * MICRO) + [shape(whole, 2 * width)] * (2 * MICRO)
        got = call(functools.partial(memory_kernel, padded), place, (*pieces, state["ckv"]), outs, time=6)
        state["rows"], state["rows_prev"], state["mem_kv"], state["mem_prev"] = (
            got[k * MICRO : (k + 1) * MICRO] for k in range(4)
        )

    def top_side():
        (top,) = yield 2, lambda: (tops,)
        far, near = flip(top, "mem", 2), flip(top, "mem", 1)
        far, near = yield 4, lambda: (far, near)
        state["top"] = tops, near, far, flip(far, "mem", 1)

    def hidden_side():
        (part,) = yield 3, lambda: (hidden_part,)
        whole = lax.all_gather(part, "seq", axis=0, tiled=True)
        (whole,) = yield 9, lambda: (whole,)
        both = [shape(whole.shape[0] // 2, D)] * 2
        state["inner"], state["outer"] = call(functools.partial(hidden_kernel, hidden), place, (whole,), both)
        kernel = functools.partial(hidden_grads_kernel, hidden)
        arrays = yield 12, lambda: state["grad_hidden"][0]
        grads = call(kernel, place, arrays, shape(2 * D, D), time=9)
        arrays = yield 13, lambda: (*state["grad_hidden"][1], grads)
        grads = call(kernel, place, arrays, shape(2 * D, D), time=9)
        (grads,) = yield 14, lambda: (grads,)
        grads = lax.psum_scatter(grads, "seq", scatter_dimension=0, tiled=True)
        (grads,) = yield 18, lambda: (grads,)
        state["hidden_grads"] = grads[:hidden].astype(F32), grads[hidden:].astype(F32)

    order = turned[::-1]

    def seq_next(kept, received, bit):
        rows, columns = kept.shape[0] // 2, kept.shape[1]
        kept, sent = call(tree_kernel, place, (kept, received), [shape(rows, columns, F32), shape(rows, columns)])
        return kept, flip(sent, "seq", bit)

    def half_grads(names):
        arrays = [part for low, mine, others in names for part in (*low, *mine, *others)]
        outs = [shape(D, len(names) * half, F32), shape(D, len(names) * half)]
        return call(functools.partial(half_grads_kernel, len(names)), place, arrays, outs, time=2 * len(names))

    def tree_side(name, arrays, groups, ticks):
        arrays = yield ticks[0], lambda: arrays
        kept, sent = reorder(arrays, groups, seq, turned)
        pair = kept, flip(sent, "seq", order[0])
        for bit, tick in zip(order[1:], ticks[1:]):
            pair = yield tick, lambda: pair
            pair = seq_next(*pair, bit)
        for bit in order[len(ticks) :]:
            pair = seq_next(*pair, bit)
        state[name] = pair

    def cout_side():
        names, gains = yield 15, lambda: (state["grad_cout"], state["grad_gain_three"])
        own, other = half_grads([list(zip(*names))])
        gains = jnp.pad((gains[0] + gains[1]).reshape(D, 1), ((0, 0), (0, 127)))
        groups = [[(0, 0, half), (1, 0, half)], [(2, 0, 128)]]
        yield from tree_side("cout", (own, flip(other, "mem", 1), gains), groups, (16, 18, 19))

    def wide_side():
        out, query, ckv = yield 17, lambda: (state["grad_out"], state["grad_cquery"], state["grad_ckv"])
        own, other = half_grads([list(zip(*out)), list(zip(*query))])
        groups = [[(0, 0, 2 * half), (1, 0, 2 * half)], [(2, 0, 2 * width), (3, 0, 2 * width)]]
        yield from tree_side("wide", (own, flip(other, "mem", 1), *ckv), groups, (18, 19))

    def qkv_side():
        kept, sent = yield 19, lambda: state["grad_qkv"][-1]
        state["qkv"] = kept, flip(sent, "seq", order[0])

    for name in ("hidden", "gain_three", "cout", "out", "cquery", "ckv", "qkv"):
        state["grad_" + name] = []
    quarter = [shape(tok, width), shape(tok, width), shape(2 * tok, width)]
    rounded, exact, column = shape(tok, D), shape(tok, D, F32), shape(tok, 1, F32)
    half_rows, whole, pair_rows = shape(tok, half), shape(group, D), shape(2 * tok, D)

    def far_pieces(pieces):
        return pieces[0], pieces[1], flip(pieces[2], "mem", 2)

    def stream(i):
        at = places[i]
        pieces = yield gathered
        qkv, kv_prev = call(
            functools.partial(qkv_kernel, i, tok), place, (*pieces, qkv_full),
            [shape(group, 3 * width), shape(group, 2 * width)], time=5,
        )
        if i == 0:
            qkv, kv_prev = yield Stay((qkv, kv_prev))
        self_o, self_lse = self_forward(at, qkv, kv_prev, blocks)
        self_lse = yield self_lse

        pieces = yield far_slots(self_o)
        self_low, after_self, plain_two, low_two, scale_two, *pieces = call(
            functools.partial(self_out_kernel, i), place,
            (*near_slots(*pieces), x_rows, state["wide_own"], state["wide_other"]),
            [rounded, exact, exact, rounded, column, *quarter], time=4,
        )
        scale_two = yield scale_two

        pieces = yield far_pieces(pieces)
        mem_kv, mem_prev = state["mem_kv"][i], state["mem_prev"][i]
        cross_o, cross_lse, cross_q = cross_forward(at, near_slots(*pieces), mem_prev, mem_kv, blocks, real)
        cross_lse = yield cross_lse

        pieces = yield far_slots(cross_o)
        cross_low, after_cross, plain_three, scale_three, low_three = call(
            cross_out_kernel, place,
            (*near_slots(*pieces), after_self, state["cout_own"], state["cout_other"], state["gain"]),
            [rounded, exact, exact, column, rounded], time=3,
        )
        scale_three = yield scale_three

        low_three, near, far = yield low_three, flip(low_three, "mem", 1), flip(low_three, "mem", 2)
        low_all, top_all, act, pre_low, grad_keep, grad_send, out_keep, out_send = call(
            functools.partial(mlp_kernel, i), place,
            (low_three, near, far, flip(far, "mem", 1), *state["top"], state["inner"], state["outer"]),
            [whole, whole, whole, whole, pair_rows, pair_rows, pair_rows, pair_rows], time=15,
        )
        state["grad_hidden"].append((pre_low, low_all, act, top_all))
        grad_keep = yield grad_keep

        near, far = near_sum(place, grad_keep, grad_send)
        far, out_send = yield flip(far, "mem", 2), out_send
        grad_after_cross, mine, others, gain_three, *pieces = call(
            functools.partial(cross_back_kernel, i), place,
            (near, far, plain_three, scale_three, state["gain"], tops, state["cout_own"], state["cout_other"]),
            [exact, half_rows, half_rows, shape(1, D, F32), *quarter], time=3,
        )
        state["grad_gain_three"].append(gain_three)
        state["grad_cout"].append((cross_low, mine, others))
        grad_after_cross = yield grad_after_cross

        pieces, out_send = yield far_pieces(pieces), out_send
        dcq, dmem_prev, dmem = cross_backward(
            at, cross_q, mem_prev, mem_kv, cross_o, near_slots(*pieces), cross_lse, blocks, real
        )
        out_near, out_far = near_sum(place, out_keep, out_send)
        dmem = yield dmem

        pieces, out_far = yield far_slots(dcq), out_far
        out_far = flip(out_far, "mem", 2)
        grad_after_self, query_mine, query_others, mine, others, *pieces = call(
            self_back_kernel, place,
            (*near_slots(*pieces), plain_two, scale_two, grad_after_cross, state["wide_own"], state["wide_other"]),
            [exact, half_rows, half_rows, half_rows, half_rows, *quarter], time=4,
        )
        state["grad_cquery"].append((low_two, query_mine, query_others))
        state["grad_out"].append((self_low, mine, others))
        mem_rows = shape(4 * padded, D)
        grad_ckv, mem_keep, mem_send = call(
            memory_back_kernel, place, (dmem, dmem_prev, state["rows"][i], state["rows_prev"][i], state["ckv"]),
            [shape(D, 2 * width, F32), mem_rows, mem_rows], time=5,
        )
        state["grad_ckv"].append(grad_ckv)
        grad_after_self = yield grad_after_self

        pieces, out_far = yield far_pieces(pieces), out_far
        dq, dkv, dkv_prev = self_backward(at, qkv, kv_prev, self_o, near_slots(*pieces), self_lse, blocks)
        grads = (*gathered, dq, dkv, dkv_prev)
        if i == 0:
            grads = call(functools.partial(qkv_grads_kernel, i), place, grads, shape(D, 3 * width, F32), time=7)
        else:
            grads = call(
                functools.partial(last_qkv_grads_kernel, i, seq_offsets(turned)), seq.reshape(1),
                (*grads, state["grad_qkv"][0]), [shape(D // 2, 3 * width, F32), shape(D // 2, 3 * width)],
                [pltpu.VMEM((D, 3 * width), F32)], time=8,
            )
        state["grad_qkv"].append(grads)
        output = call(output_kernel, place, (after_cross, out_near, out_far), rounded)
        keep, send, keep_prev, send_prev = call(
            qkv_back_kernel, place, (dq, dkv, dkv_prev, qkv_full), [pair_rows] * 4, time=5
        )
        keep = yield keep

        near_prev, far_prev = near_sum(place, keep_prev, send_prev)
        near, far = near_sum(place, keep, send)
        far_prev, far, mem_send = yield flip(far_prev, "mem", 2), flip(far, "mem", 2), mem_send
        back = shifted(call(far_sum_kernel, place, (near_prev, far_prev), rounded), -1)
        mem_near, mem_far = near_sum(place, mem_keep, mem_send)
        mem_all = call(far_sum_kernel, place, (mem_near, flip(mem_far, "mem", 2)), shape(2 * padded, D))
        mem_back = shifted(mem_all[padded:], -1)
        grad_mem = (mem_all[:padded].astype(F32) + mem_back.astype(F32))[:real].reshape(1, real, D)
        grad_x = call(functools.partial(grad_x_kernel, i), place, (x_rows, grad_after_self, near, far, back), exact)
        return output, grad_x, grad_mem

    sides = [first_side(), memory_side(), top_side(), hidden_side(), cout_side(), wide_side(), qkv_side()]
    done = interleave([stream(i) for i in range(MICRO)], sides)

    def wide_finish(own):
        high = me >> 1
        rows_two = own.reshape(2, 2 * wrows, own.shape[1])
        theirs = lax.dynamic_index_in_dim(rows_two, 1 - high, 0, keepdims=False).astype(BF)
        own = lax.dynamic_index_in_dim(rows_two, high, 0, keepdims=False) + flip(theirs, "mem", 2).astype(F32)
        rows_two = own.reshape(2, wrows, own.shape[1])
        theirs = lax.dynamic_index_in_dim(rows_two, 1 - odd, 0, keepdims=False)
        own = lax.dynamic_index_in_dim(rows_two, odd, 0, keepdims=False)
        return own, flip(theirs.astype(BF), "mem", 1).astype(F32)

    def head_finish(summed, count):
        slots = summed.astype(BF).reshape(blocks, wrows, -1)
        first, second, *rest = [lax.dynamic_index_in_dim(slots, me ^ k, 0, keepdims=False) for k in range(4)]
        far = flip(jnp.concatenate(rest, axis=0), "mem", 2)
        own, near, far = near_slots(first, second, far)
        whole = join_pieces([own, near[:wrows], far[:wrows], near[wrows:]], me, 1).astype(F32)
        whole = whole.reshape(wrows, blocks, count, -1)
        return [whole[:, :, k].reshape(wrows, D) for k in range(count)]

    def seq_finish(pair, left):
        for bit in left:
            pair = seq_next(*pair, bit)
        return pair[0] + pair[1].astype(F32)

    grad_inner, grad_outer = state["hidden_grads"]
    own, near = wide_finish(seq_finish(state["cout"], []))
    grad_cout = join_halves(own[:, :half], near[:, :half])
    grad_gain_mlp = own[:, half] + near[:, half]

    last = seq_finish(state["wide"], [])
    grad_ckey, grad_cvalue = head_finish(last[:, 2 * half :], 2)
    own, near = wide_finish(last[:, : 2 * half])
    grad_out, plain_cquery = [
        join_halves(own[:, k * half : (k + 1) * half], near[:, k * half : (k + 1) * half]) for k in range(2)
    ]
    plain_qkv = head_finish(seq_finish(state["qkv"], order[1:]), 3)

    def gained(gain, weights, plains):
        scale = gain.astype(F32)[:, None]
        grad_gain = sum(jnp.sum(w.astype(F32) * p, axis=1) for w, p in zip(weights, plains))
        return grad_gain, [p * scale for p in plains]

    grad_gain_self, (grad_query, grad_key, grad_value) = gained(
        gain_self, (self_query, self_key, self_value), plain_qkv
    )
    grad_gain_cross, (grad_cquery,) = gained(gain_cross, (cross_query,), (plain_cquery,))
    return (
        jnp.stack([d[0] for d in done]),
        jnp.stack([d[1] for d in done]),
        jnp.stack([d[2] for d in done]),
        grad_gain_self,
        grad_query,
        grad_key,
        grad_value,
        grad_out,
        grad_gain_cross,
        grad_cquery,
        grad_ckey,
        grad_cvalue,
        grad_cout,
        grad_gain_mlp,
        grad_inner,
        grad_outer,
    )


def solution(mesh):
    rows = P(("seq", "mem"), None)
    tokens = P(None, ("seq", "mem"), None)
    pages = P(None, "seq", "mem", None)
    gains = P(("seq", "mem"))
    return jax.shard_map(
        shards,
        mesh=mesh,
        in_specs=(tokens, pages, P(), P(), tokens, gains, rows, rows, rows, rows, gains, rows, rows, rows, rows,
                  gains, rows, rows),
        out_specs=(tokens, tokens, pages, gains, rows, rows, rows, rows, gains, rows, rows, rows, rows, gains,
                   rows, rows),
        check_vma=False,
    )
```

```python
import functools
import math
import jax
import jax.numpy as jnp
import numpy as np
from jax import lax
from jax.experimental import pallas as pl
from jax.experimental.pallas import tpu as pltpu
from jax.sharding import PartitionSpec as P

HEAD = 64
BF = jnp.bfloat16
F32 = jnp.float32
LOWEST = -1e30


def head_lanes(rows, width):
    return lax.broadcasted_iota(jnp.int32, (rows, width), 1) // HEAD


def one_head(block, lanes, head):
    return jnp.where(lanes == head, block, jnp.zeros_like(block))


def dot_nt(left, right):
    return lax.dot_general(left, right, (((1,), (1,)), ((), ())), preferred_element_type=F32)


def dot_nn(left, right):
    return lax.dot_general(left, right, (((1,), (0,)), ((), ())), preferred_element_type=F32)


def dot_tn(left, right):
    return lax.dot_general(left, right, (((0,), (0,)), ((), ())), preferred_element_type=F32)


def self_range(p, rows, blocks, spill, prev_spill):
    first = jnp.where(p * rows < spill, prev_spill // rows, blocks + spill // rows)
    return first, blocks + p + 1


def self_allowed(query, key, extent, spill, prev_spill):
    first = jnp.where(query < spill, prev_spill, extent + spill)
    return (key >= first) & (key <= extent + query)


def cross_allowed(query, place, side, spill, length, me, padded, real):
    part = place // padded
    inner = place - part * padded
    row = (part ^ me) * real + inner
    return (inner < real) & (row < length) & ((query < spill) == (side == 0))


def fold(block, combine):
    total = block[0:8]
    for r in range(8, block.shape[0], 8):
        total = combine(total, block[r : r + 8])
    return total


def lay_heads(out, block, lanes, heads):
    rows = block.shape[0]
    for h in range(heads):
        out[h * rows : (h + 1) * rows, :] = one_head(block, lanes, h)


def score_block(kb, k, allowed, q_cat, s_scr, tops):
    rows = s_scr.shape[3]
    found = []
    for h, top in enumerate(tops):
        s = jnp.where(allowed, dot_nt(k, q_cat[h * rows : (h + 1) * rows, :]), LOWEST)
        s_scr[kb, h] = s
        found.append(jnp.maximum(top, fold(s, jnp.maximum)))
    return tuple(found)


def weigh_block(kb, tops, totals, s_scr, p_scr, v_cat):
    count = s_scr.shape[2]
    summed = []
    for h, (top, total) in enumerate(zip(tops, totals)):
        e = jnp.exp(s_scr[kb, h] - top)
        p_scr[h * count : (h + 1) * count, :] = e.astype(BF)
        summed.append(total + fold(e, jnp.add))
    return tuple(summed), dot_tn(p_scr[...], v_cat)


def attend(first, last, heads, scores, values, s_scr, p_scr, width):
    rows = s_scr.shape[3]
    lowest = jnp.full((8, rows), LOWEST, F32)
    tops = lax.fori_loop(first, last, scores, (lowest,) * heads)
    tops = tuple(jnp.max(top, axis=0, keepdims=True) for top in tops)

    def step(kb, carry):
        totals, acc = carry
        totals, more = weigh_block(kb, tops, totals, s_scr, p_scr, values(kb))
        return totals, acc + more

    start = (jnp.zeros((8, rows), F32),) * heads, jnp.zeros((rows, width), F32)
    totals, acc = lax.fori_loop(first, last, step, start)
    return tops, tuple(jnp.sum(total, axis=0, keepdims=True) for total in totals), acc


def finish(p, start, tops, totals, acc, lanes, o_ref, lse_ref):
    rows = acc.shape[0]
    heads = len(tops)
    inverse = jnp.concatenate([1.0 / total for total in totals] + [jnp.zeros((8 - heads, rows), F32)], axis=0).T
    spread_out = jnp.zeros(acc.shape, F32)
    for h in range(heads):
        spread_out = jnp.where(lanes == h, inverse[:, h : h + 1], spread_out)
    o_ref[pl.ds(start, rows), :] = (acc * spread_out).astype(BF)
    place = pl.ds(pl.multiple_of(p * rows, rows), rows)
    for h in range(heads):
        lse_ref[h : h + 1, place] = tops[h] + jnp.log(totals[h])


def self_forward_kernel(rows, blocks, heads, sc, qkv, kvp, o_ref, lse_ref, k_scr, v_scr, s_scr, q_cat, p_scr):
    width = heads * HEAD
    extent = rows * blocks
    me, spill, prev_spill = sc[0], sc[1], sc[4]
    lanes = head_lanes(rows, width)

    def place(b):
        return pl.multiple_of((b ^ me) * rows, rows)

    first_used, _ = self_range(0, rows, blocks, spill, prev_spill)

    @pl.loop(first_used, 2 * blocks)
    def _(kb):
        def fill(keys, values):
            k_scr[kb] = keys
            lay_heads(v_scr.at[kb], values, lanes, heads)

        @pl.when(kb < blocks)
        def _():
            at = pl.ds(place(kb), rows)
            fill(kvp[at, 0:width], kvp[at, width : 2 * width])

        @pl.when(kb >= blocks)
        def _():
            at = pl.ds(place(kb - blocks), rows)
            fill(qkv[at, width : 2 * width], qkv[at, 2 * width : 3 * width])

    @pl.loop(0, blocks)
    def _(p):
        lay_heads(q_cat, qkv[pl.ds(place(p), rows), 0:width] * jnp.asarray(0.125, BF), lanes, heads)
        first, last = self_range(p, rows, blocks, spill, prev_spill)
        query = p * rows + lax.broadcasted_iota(jnp.int32, (1, rows), 1)

        def scores(kb, tops):
            key = kb * rows + lax.broadcasted_iota(jnp.int32, (rows, rows), 0)
            return score_block(kb, k_scr[kb], self_allowed(query, key, extent, spill, prev_spill), q_cat, s_scr, tops)

        tops, totals, acc = attend(first, last, heads, scores, lambda kb: v_scr[kb], s_scr, p_scr, width)
        finish(p, place(p), tops, totals, acc, lanes, o_ref, lse_ref)


def lay(out, own, near, far):
    rows = own.shape[0]
    out[0:rows, :] = own[...]
    out[rows : 2 * rows, :] = near[0:rows, :]
    out[2 * rows : 3 * rows, :] = far[0:rows, :]
    out[3 * rows :, :] = near[rows:, :]


def cross_forward_kernel(rows, blocks, heads, padded, real, sc, own, near, far, kv0, kv1, o_ref, lse_ref, q_ref,
                         v_scr, s_scr, q_cat, p_scr):
    lay(q_ref, own, near, far)
    width = heads * HEAD
    keys = kv0.shape[0]
    me, spill = sc[0], sc[1]
    lanes = head_lanes(rows, width)
    key_lanes = head_lanes(keys, width)
    kvs = (kv0, kv1)

    def place(b):
        return pl.multiple_of((b ^ me) * rows, rows)

    for side in range(2):
        lay_heads(v_scr.at[side], kvs[side][:, width : 2 * width], key_lanes, heads)

    @pl.loop(0, blocks)
    def _(p):
        lay_heads(q_cat, q_ref[pl.ds(place(p), rows), :] * jnp.asarray(0.125, BF), lanes, heads)
        query = p * rows + lax.broadcasted_iota(jnp.int32, (1, rows), 1)

        def scores(side, tops):
            spot = lax.broadcasted_iota(jnp.int32, (keys, 1), 0)
            length = jnp.where(side == 0, sc[2], sc[3])
            allowed = cross_allowed(query, spot, side, spill, length, me, padded, real)
            k = jnp.where(side == 0, kv0[:, 0:width], kv1[:, 0:width])
            return score_block(side, k, allowed, q_cat, s_scr, tops)

        first = jnp.where(p * rows < spill, 0, 1)
        last = jnp.where((p + 1) * rows > spill, 2, 1)
        tops, totals, acc = attend(first, last, heads, scores, lambda side: v_scr[side], s_scr, p_scr, width)
        finish(p, place(p), tops, totals, acc, lanes, o_ref, lse_ref)


def spread(p, at, rows, heads, q, g, o_ref, lse_ref, lanes, q_cat, g_cat, stat):
    weighted = (g.astype(F32) * o_ref[at, :].astype(F32)).T
    for h in range(heads):
        q_cat[h * rows : (h + 1) * rows, :] = one_head(q, lanes, h)
        g_cat[h * rows : (h + 1) * rows, :] = one_head(g, lanes, h)
        stat[heads + h : heads + h + 1, :] = jnp.sum(weighted[h * HEAD : (h + 1) * HEAD, :], axis=0, keepdims=True)
    stat[0:heads, :] = lse_ref[0:heads, pl.ds(pl.multiple_of(p * rows, rows), rows)]


def back_block(rows, heads, k, v, allowed, q_cat, g_cat, stat, w_scr, ds_wide, ds_tall):
    count = k.shape[0]
    for h in range(heads):
        span = slice(h * rows, (h + 1) * rows)
        s = dot_nt(k, q_cat[span, :])
        e = jnp.where(allowed, jnp.exp(s - stat[h : h + 1, :]), 0.0)
        de = dot_nt(v, g_cat[span, :])
        ds = (e * (de - stat[heads + h : heads + h + 1, :])).astype(BF)
        w_scr[:, span] = e.astype(BF)
        ds_wide[:, span] = ds
        ds_tall[h * count : (h + 1) * count, :] = ds


def self_backward_kernel(rows, blocks, heads, sc, qkv, kvp, o_ref, own, near, far, lse_ref, dq_ref, dkv_ref,
                         dprev_ref, g_ref, kv_scr, k_cat, dkv_scr, q_cat, g_cat, stat, w_scr, ds_wide, ds_tall):
    lay(g_ref, own, near, far)
    width = heads * HEAD
    extent = rows * blocks
    me, spill, prev_spill = sc[0], sc[1], sc[4]
    lanes = head_lanes(rows, width)

    def place(b):
        return pl.multiple_of((b ^ me) * rows, rows)

    first_used, _ = self_range(0, rows, blocks, spill, prev_spill)

    @pl.loop(0, 2 * blocks)
    def _(kb):
        dkv_scr[kb] = jnp.zeros(dkv_scr.shape[1:], F32)

    @pl.loop(first_used, 2 * blocks)
    def _(kb):
        def fill(pair):
            kv_scr[kb] = pair
            scaled = pair[:, 0:width] * jnp.asarray(0.125, BF)
            for h in range(heads):
                k_cat[kb, h * rows : (h + 1) * rows, :] = one_head(scaled, lanes, h)

        @pl.when(kb < blocks)
        def _():
            fill(kvp[pl.ds(place(kb), rows), :])

        @pl.when(kb >= blocks)
        def _():
            fill(qkv[pl.ds(place(kb - blocks), rows), width : 3 * width])

    @pl.loop(0, blocks)
    def _(p):
        at = pl.ds(place(p), rows)
        q = qkv[at, 0:width] * jnp.asarray(0.125, BF)
        g = g_ref[at, :]
        spread(p, at, rows, heads, q, g, o_ref, lse_ref, lanes, q_cat, g_cat, stat)
        first, last = self_range(p, rows, blocks, spill, prev_spill)
        query = p * rows + lax.broadcasted_iota(jnp.int32, (1, rows), 1)

        def step(kb, dq):
            key = kb * rows + lax.broadcasted_iota(jnp.int32, (rows, 1), 0)
            allowed = self_allowed(query, key, extent, spill, prev_spill)
            back_block(rows, heads, kv_scr[kb, :, 0:width], kv_scr[kb, :, width : 2 * width], allowed,
                       q_cat, g_cat, stat, w_scr, ds_wide, ds_tall)
            dkv_scr[kb, :, 0:width] += dot_nn(ds_wide[...], q_cat[...])
            dkv_scr[kb, :, width : 2 * width] += dot_nn(w_scr[...], g_cat[...])
            return dq + dot_tn(ds_tall[...], k_cat[kb])

        dq = lax.fori_loop(first, last, step, jnp.zeros((rows, width), F32))
        dq_ref[at, :] = dq.astype(BF)

    @pl.loop(0, blocks)
    def _(b):
        at = pl.ds(place(b), rows)
        dprev_ref[at, :] = dkv_scr[b].astype(BF)
        dkv_ref[at, :] = dkv_scr[blocks + b].astype(BF)


def cross_backward_kernel(rows, blocks, heads, padded, real, pieces, sc, q_ref, kv0, kv1, o_ref, own, near, far,
                          lse_ref, dq_ref, dkv0_ref, dkv1_ref, g_ref, k_cat, dkv_scr, q_cat, g_cat, stat, w_scr, ds_wide, ds_tall):
    lay(g_ref, own, near, far)
    width = heads * HEAD
    keys = kv0.shape[0]
    step_keys = keys // pieces
    me, spill = sc[0], sc[1]
    lanes = head_lanes(rows, width)
    key_lanes = head_lanes(step_keys, width)
    kvs = (kv0, kv1)

    def place(b):
        return pl.multiple_of((b ^ me) * rows, rows)

    dkv_scr[...] = jnp.zeros(dkv_scr.shape, F32)
    for side in range(2):
        for piece in range(pieces):
            scaled = kvs[side][piece * step_keys : (piece + 1) * step_keys, 0:width] * jnp.asarray(0.125, BF)
            for h in range(heads):
                k_cat[side * pieces + piece, h * step_keys : (h + 1) * step_keys, :] = one_head(scaled, key_lanes, h)

    @pl.loop(0, blocks)
    def _(p):
        at = pl.ds(place(p), rows)
        q = q_ref[at, :] * jnp.asarray(0.125, BF)
        spread(p, at, rows, heads, q, g_ref[at, :], o_ref, lse_ref, lanes, q_cat, g_cat, stat)
        query = p * rows + lax.broadcasted_iota(jnp.int32, (1, rows), 1)
        reads = (p * rows < spill, (p + 1) * rows > spill)
        first = jnp.where(reads[0], 0, pieces)
        last = jnp.where(reads[1], 2 * pieces, pieces)

        def step(kb, dq):
            side = kb // pieces
            at_key = pl.ds(pl.multiple_of((kb - side * pieces) * step_keys, step_keys), step_keys)
            spot = (kb - side * pieces) * step_keys + lax.broadcasted_iota(jnp.int32, (step_keys, 1), 0)
            length = jnp.where(side == 0, sc[2], sc[3])
            allowed = cross_allowed(query, spot, side, spill, length, me, padded, real)
            is_prev = side == 0
            pair = jnp.where(is_prev, kv0[at_key, :], kv1[at_key, :])
            back_block(rows, heads, pair[:, 0:width], pair[:, width : 2 * width], allowed,
                       q_cat, g_cat, stat, w_scr, ds_wide, ds_tall)
            dkv_scr[kb, :, 0:width] += dot_nn(ds_wide[...], q_cat[...])
            dkv_scr[kb, :, width : 2 * width] += dot_nn(w_scr[...], g_cat[...])
            return dq + dot_tn(ds_tall[...], k_cat[kb])

        dq = lax.fori_loop(first, last, step, jnp.zeros((rows, width), F32))
        dq_ref[at, :] = dq.astype(BF)

    for piece in range(pieces):
        span = slice(piece * step_keys, (piece + 1) * step_keys)
        dkv0_ref[span, :] = dkv_scr[piece].astype(BF)
        dkv1_ref[span, :] = dkv_scr[pieces + piece].astype(BF)


def call(kernel, scalars, arrays, outs, scratch=(), time=2):
    vmem = pl.BlockSpec(memory_space=pltpu.VMEM)
    held = (*arrays, *jax.tree.leaves(outs), *scratch)
    room = sum(math.prod(a.shape) * jnp.dtype(a.dtype).itemsize for a in held) + 12 * 2**20
    return pl.pallas_call(
        kernel,
        out_shape=outs,
        in_specs=[pl.BlockSpec(memory_space=pltpu.SMEM)] + [vmem] * len(arrays),
        out_specs=jax.tree.map(lambda _: vmem, outs),
        scratch_shapes=scratch,
        compiler_params=pltpu.CompilerParams(vmem_limit_bytes=min(room, 48 * 2**20)),
        cost_estimate=pl.CostEstimate(flops=1024, bytes_accessed=int(time * 640000), transcendentals=0),
    )(scalars, *arrays)


def self_forward(scalars, qkv, kvp, blocks):
    extent = qkv.shape[0]
    rows = extent // blocks
    width = qkv.shape[1] // 3
    heads = width // HEAD
    return call(
        functools.partial(self_forward_kernel, rows, blocks, heads),
        scalars,
        (qkv, kvp),
        [jax.ShapeDtypeStruct((extent, width), BF), jax.ShapeDtypeStruct((8, extent), F32)],
        [
            pltpu.VMEM((2 * blocks, rows, width), BF),
            pltpu.VMEM((2 * blocks, heads * rows, width), BF),
            pltpu.VMEM((2 * blocks, heads, rows, rows), F32),
            pltpu.VMEM((heads * rows, width), BF),
            pltpu.VMEM((heads * rows, rows), BF),
        ],
        time=18,
    )


def cross_forward(scalars, pieces, kv0, kv1, blocks, real):
    rows, width = pieces[0].shape
    extent = rows * blocks
    heads = width // HEAD
    keys = kv0.shape[0]
    return call(
        functools.partial(cross_forward_kernel, rows, blocks, heads, keys // blocks, real),
        scalars,
        (*pieces, kv0, kv1),
        [
            jax.ShapeDtypeStruct((extent, width), BF),
            jax.ShapeDtypeStruct((8, extent), F32),
            jax.ShapeDtypeStruct((extent, width), BF),
        ],
        [
            pltpu.VMEM((2, heads * keys, width), BF),
            pltpu.VMEM((2, heads, keys, rows), F32),
            pltpu.VMEM((heads * rows, width), BF),
            pltpu.VMEM((heads * keys, rows), BF),
        ],
        time=9,
    )


def back_scratch(rows, heads, width, keys):
    return [
        pltpu.VMEM((heads * rows, width), BF),
        pltpu.VMEM((heads * rows, width), BF),
        pltpu.VMEM((8, rows), F32),
        pltpu.VMEM((keys, heads * rows), BF),
        pltpu.VMEM((keys, heads * rows), BF),
        pltpu.VMEM((heads * keys, rows), BF),
    ]


def self_backward(scalars, qkv, kvp, o, g, lse, blocks):
    extent = qkv.shape[0]
    rows = extent // blocks
    width = qkv.shape[1] // 3
    heads = width // HEAD
    return call(
        functools.partial(self_backward_kernel, rows, blocks, heads),
        scalars,
        (qkv, kvp, o, *g, lse),
        [
            jax.ShapeDtypeStruct((extent, width), BF),
            jax.ShapeDtypeStruct((extent, 2 * width), BF),
            jax.ShapeDtypeStruct((extent, 2 * width), BF),
        ],
        [
            pltpu.VMEM((extent, width), BF),
            pltpu.VMEM((2 * blocks, rows, 2 * width), BF),
            pltpu.VMEM((2 * blocks, heads * rows, width), BF),
            pltpu.VMEM((2 * blocks, rows, 2 * width), F32),
        ]
        + back_scratch(rows, heads, width, rows),
        time=22,
    )


def cross_backward(scalars, q, kv0, kv1, o, g, lse, blocks, real, pieces=1):
    extent, width = q.shape
    rows = extent // blocks
    heads = width // HEAD
    keys = kv0.shape[0]
    step_keys = keys // pieces
    return call(
        functools.partial(cross_backward_kernel, rows, blocks, heads, keys // blocks, real, pieces),
        scalars,
        (q, kv0, kv1, o, *g, lse),
        [
            jax.ShapeDtypeStruct((extent, width), BF),
            jax.ShapeDtypeStruct((keys, 2 * width), BF),
            jax.ShapeDtypeStruct((keys, 2 * width), BF),
        ],
        [
            pltpu.VMEM((extent, width), BF),
            pltpu.VMEM((2 * pieces, heads * step_keys, width), BF),
            pltpu.VMEM((2 * pieces, step_keys, 2 * width), F32),
        ]
        + back_scratch(rows, heads, width, step_keys),
        time=14,
    )


def ordered_pieces(pieces, me):
    odd = (me & 1) == 1
    high = (me & 2) == 2
    low_pair = [jnp.where(odd, pieces[1 - i], pieces[i]) for i in range(2)]
    high_pair = [jnp.where(odd, pieces[3 - i], pieces[2 + i]) for i in range(2)]
    ordered = [jnp.where(high, high_pair[i], low_pair[i]) for i in range(2)]
    return ordered + [jnp.where(high, low_pair[i], high_pair[i]) for i in range(2)]


def join_pieces(pieces, me, axis):
    return jnp.concatenate(ordered_pieces(pieces, me), axis=axis)


def received(own, near, far, me):
    rows = own.shape[0]
    return join_pieces([own[...], near[0:rows, :], far[0:rows, :], near[rows:, :]], me, 1)


def send_pieces(tensor, me, first, second, rest):
    width = tensor.shape[1] // 4
    rows = tensor.shape[0]
    pieces = ordered_pieces([tensor[:, k * width : (k + 1) * width] for k in range(4)], me)
    first[...] = pieces[0]
    second[...] = pieces[1]
    rest[0:rows, :] = pieces[2]
    rest[rows:, :] = pieces[3]


def half_product(tensor, own, other, me, first):
    span = slice(first, first + own.shape[0] // 2)
    left, right = dot_nn(tensor, own[:, span]), dot_nn(tensor, other[:, span])
    odd = (me & 1) == 1
    return jnp.concatenate([jnp.where(odd, right, left), jnp.where(odd, left, right)], axis=1)


def two_halves(tensor, me):
    half = tensor.shape[1] // 2
    odd = (me & 1) == 1
    left, right = tensor[:, 0:half], tensor[:, half:]
    return jnp.where(odd, right, left), jnp.where(odd, left, right)


def half_back(mine, others, own, other, first):
    span = slice(first, first + own.shape[0] // 2)
    return dot_nt(mine, own[:, span]) + dot_nt(others, other[:, span])


def normal_parts(tensor):
    average = jnp.mean(tensor, axis=-1, keepdims=True)
    centered = tensor - average
    scale = lax.rsqrt(jnp.mean(centered * centered, axis=-1, keepdims=True) + 1e-05)
    return centered * scale, scale


def normal_back(plain, scale, grad):
    inner = jnp.mean(grad * plain, axis=-1, keepdims=True)
    return scale * (grad - jnp.mean(grad, axis=-1, keepdims=True) - plain * inner)


def gelu_parts(pre):
    size = jnp.abs(pre)
    t = 1.0 / (1.0 + (0.3275911 * 0.7071067811865476) * size)
    poly = ((((1.061405429 * t - 1.453152027) * t + 1.421413741) * t - 0.284496736) * t + 0.254829592) * t
    bell = jnp.exp(-0.5 * pre * pre)
    tail = 0.5 * poly * bell
    cdf = jnp.where(pre < 0.0, tail, 1.0 - tail)
    return pre * cdf, cdf + pre * bell * 0.3989422804014327


def place_kernel(group, at, lengths, ids, *outs):
    seq, me = at[0], at[1]
    before = jnp.maximum(seq - 1, 0)
    for i, out in enumerate(outs):
        out[0] = me
        out[2] = lengths[i, before]
        out[3] = lengths[i, seq]
        for slot, block, number in ((1, seq, seq), (4, before, seq - 1)):
            rows = group // 128
            part = ids[i, pl.ds(pl.multiple_of(block * rows, rows), rows), :]
            out[slot] = jnp.sum(jnp.where(part < number, 1.0, 0.0)).astype(jnp.int32)
        for slot in (5, 6, 7):
            out[slot] = 0


def norm_kernel(at, x, low):
    rows = 256
    for start in range(0, low.shape[0], rows):
        span = slice(start, min(start + rows, low.shape[0]))
        low[span, :] = normal_parts(x[span, :].astype(F32))[0].astype(BF)


def lay_four(out, own, near, far, last):
    rows = own.shape[0]
    for k, ref in enumerate((own, near, far, last)):
        out[k * rows : (k + 1) * rows, :] = ref[...]


def qkv_kernel(i, rows, at, *refs):
    weight, qkv, kvp = refs[8:]
    width = weight.shape[1] // 3
    own = slice(i * rows, (i + 1) * rows)
    for k in range(4):
        block = slice(k * rows, (k + 1) * rows)
        qkv[block, :] = dot_nn(refs[k][own, :], weight[...]).astype(BF)
        kvp[block, :] = dot_nn(refs[4 + k][own, :], weight[:, width:]).astype(BF)


def memory_kernel(size, at, *refs):
    weight, outs = refs[8], refs[9:]
    count = len(outs) // 2
    rows, keys = outs[:count], outs[count:]
    for i in range(count):
        span = slice((i % (count // 2)) * size, (i % (count // 2) + 1) * size)
        pieces = refs[0:4] if i < count // 2 else refs[4:8]
        block = jnp.concatenate([ref[span, :] for ref in pieces], axis=0)
        rows[i][...] = block
        keys[i][...] = dot_nn(block, weight[...]).astype(BF)


def hidden_kernel(rows, at, whole, inner, outer):
    slot = 2 * rows
    for i in range(inner.shape[0] // rows):
        inner[i * rows : (i + 1) * rows, :] = whole[i * slot : i * slot + rows, :]
        outer[i * rows : (i + 1) * rows, :] = whole[i * slot + rows : i * slot + 2 * rows, :]


def hidden_grads_kernel(rows, at, pre_low, low, act, top, *refs):
    before, out = (refs[0], refs[1]) if len(refs) == 2 else (None, refs[0])
    step, slot = 256, 2 * rows
    for i in range(pre_low.shape[1] // step):
        for k, (left, right) in enumerate(((pre_low, low), (act, top))):
            grad = dot_tn(left[:, i * step : (i + 1) * step], right[...])
            for part in range(step // rows):
                start = (i * step // rows + part) * slot + k * rows
                block = grad[part * rows : (part + 1) * rows]
                if before is not None:
                    block = block + before[start : start + rows, :].astype(F32)
                out[start : start + rows, :] = block.astype(BF)


def near_kernel(at, keep, received, near, far):
    rows = near.shape[0]
    near[...] = keep[0:rows, :].astype(F32) + received[0:rows, :].astype(F32)
    far[...] = (keep[rows:, :].astype(F32) + received[rows:, :].astype(F32)).astype(BF)


def tree_kernel(at, keep, received, kept, sent):
    rows = kept.shape[0]
    kept[...] = keep[0:rows, :] + received[0:rows, :].astype(F32)
    sent[...] = (keep[rows:, :] + received[rows:, :].astype(F32)).astype(BF)


def output_kernel(at, after, near, far, out):
    out[...] = (after[...] + near[...] + far[...].astype(F32)).astype(BF)


def grad_x_kernel(i, at, x, before, near, far, back, out):
    rows = out.shape[0]
    plain, scale = normal_parts(x[i * rows : (i + 1) * rows, :].astype(F32))
    grad = near[...] + far[...].astype(F32) + back[...].astype(F32)
    out[...] = before[...] + normal_back(plain, scale, grad)


def far_sum_kernel(at, near, far, out):
    out[...] = (near[...] + far[...].astype(F32)).astype(BF)


def memory_back_kernel(at, own_a, own_b, prev_a, prev_b, rows_a, rows_b, rows_prev_a, rows_prev_b, weight,
                       grad, keep, send):
    rows = own_a.shape[0] // 4
    total = None
    grads, places = (own_a, own_b, prev_a, prev_b), (rows_a, rows_b, rows_prev_a, rows_prev_b)
    for k, (part, memory) in enumerate(zip(grads, places)):
        term = dot_tn(memory[...], part[...])
        total = term if total is None else total + term
        part = dot_nt(part[...], weight[...]).astype(BF)
        for slot, out, place in ((0, keep, 0), (1, send, 0), (2, keep, 4), (3, send, 4)):
            out[(place + k) * rows : (place + k + 1) * rows, :] = part[slot * rows : (slot + 1) * rows]
    grad[...] = total


def self_out_kernel(i, at, own, near, far, x, wide_own, wide_other,
                    low, after, plain, low_next, scale, first, second, rest):
    me = at[0]
    joined = received(own, near, far, me)
    low[...] = joined
    rows = low.shape[0]
    total = x[i * rows : (i + 1) * rows, :].astype(F32) + half_product(joined, wide_own, wide_other, me, 0)
    after[...] = total
    normed, scaled = normal_parts(total)
    plain[...] = normed
    scale[...] = scaled
    rounded = normed.astype(BF)
    low_next[...] = rounded
    send_pieces(half_product(rounded, wide_own, wide_other, me, wide_own.shape[0] // 2).astype(BF), me, first, second, rest)


def cross_out_kernel(at, own, near, far, before, out_own, out_other, gain, low, after, plain, scale, low_next):
    me = at[0]
    joined = received(own, near, far, me)
    low[...] = joined
    total = before[...] + half_product(joined, out_own, out_other, me, 0)
    after[...] = total
    normed, scaled = normal_parts(total)
    plain[...] = normed
    scale[...] = scaled
    low_next[...] = (normed * gain[...]).astype(BF)


def mlp_kernel(i, at, low, near_low, far_low, last_low, top, near_top, far_top, last_top, inner, outer,
               low_all, top_all, act, pre_low, grad_keep, grad_send, out_keep, out_send):
    rows = low.shape[0]
    lay_four(low_all, low, near_low, far_low, last_low)
    lay_four(top_all, *(ref.at[i * rows : (i + 1) * rows, :] for ref in (top, near_top, far_top, last_top)))
    for parity, grad, out in ((1, grad_send, out_send), (0, grad_keep, out_keep)):

        @pl.loop(0, 2)
        def _(b):
            block = pl.ds(pl.multiple_of((2 * b + parity) * rows, rows), rows)
            place = pl.ds(pl.multiple_of(b * rows, rows), rows)
            value, slope = gelu_parts(dot_nt(low_all[block, :], inner[...]))
            act_block = value.astype(BF)
            act[block, :] = act_block
            pre_block = (dot_nt(top_all[block, :], outer[...]) * slope).astype(BF)
            pre_low[block, :] = pre_block
            grad[place, :] = dot_nn(pre_block, inner[...]).astype(BF)
            out[place, :] = dot_nn(act_block, outer[...]).astype(BF)


def cross_back_kernel(i, at, near, far, plain, scale, gain, top, out_own, out_other,
                      grad_after, branch_own, branch_other, grad_gain, first, second, rest):
    me = at[0]
    grad = near[...] + far[...].astype(F32)
    normed = plain[...]
    grad_gain[...] = jnp.sum(grad * normed, axis=0, keepdims=True)
    rows = near.shape[0]
    total = top[i * rows : (i + 1) * rows, :].astype(F32) + normal_back(normed, scale[...], grad * gain[...])
    grad_after[...] = total
    mine, others = two_halves(total.astype(BF), me)
    branch_own[...] = mine
    branch_other[...] = others
    send_pieces(half_back(mine, others, out_own, out_other, 0).astype(BF), me, first, second, rest)


def self_back_kernel(at, own, near, far, plain, scale, before, wide_own, wide_other,
                     grad_after, query_mine, query_others, branch_own, branch_other, first, second, rest):
    me = at[0]
    mine, others = two_halves(received(own, near, far, me), me)
    query_mine[...] = mine
    query_others[...] = others
    total = before[...] + normal_back(plain[...], scale[...], half_back(mine, others, wide_own, wide_other, wide_own.shape[0] // 2))
    grad_after[...] = total
    mine, others = two_halves(total.astype(BF), me)
    branch_own[...] = mine
    branch_other[...] = others
    send_pieces(half_back(mine, others, wide_own, wide_other, 0).astype(BF), me, first, second, rest)


def half_grads_kernel(names, at, *refs):
    own, other = refs[-2:]
    half = own.shape[1] // names
    for n in range(names):
        parts = [ref[...] for ref in refs[6 * n : 6 * n + 6]]
        low, mine, others = (jnp.concatenate(parts[k : k + 2], axis=0) for k in (0, 2, 4))
        span = slice(n * half, (n + 1) * half)
        other[:, span] = dot_tn(low, others).astype(BF)
        own[:, span] = dot_tn(low, mine)


def qkv_back_kernel(at, dq, dkv, dkv_prev, weight, keep, send, keep_prev, send_prev):
    rows = dq.shape[0] // 4
    width = dq.shape[1]
    for parity, out, out_prev in ((1, send, send_prev), (0, keep, keep_prev)):
        for b in range(2):
            block = slice((2 * b + parity) * rows, (2 * b + parity + 1) * rows)
            place = slice(b * rows, (b + 1) * rows)
            grad = dot_nt(dq[block, :], weight[:, 0:width]) + dot_nt(dkv[block, :], weight[:, width:])
            out[place, :] = grad.astype(BF)
            out_prev[place, :] = dot_nt(dkv_prev[block, :], weight[:, width:]).astype(BF)


def lay_own(i, refs, low_all, before_all):
    rows = low_all.shape[0] // 4
    own = slice(i * rows, (i + 1) * rows)
    for out, pieces in ((low_all, refs[0:4]), (before_all, refs[4:8])):
        for k, ref in enumerate(pieces):
            out[k * rows : (k + 1) * rows, :] = ref[own, :]


def qkv_grads_kernel(i, at, *refs):
    dq, dkv, dkv_prev, out, low, before, own = refs[8:]
    width = dq.shape[1]
    lay_own(i, refs, low, before)
    out[:, 0:width] = dot_tn(low[...], dq[...])
    own[...] = dot_tn(low[...], dkv[...])
    out[:, width:] = own[...] + dot_tn(before[...], dkv_prev[...])


def last_qkv_grads_kernel(i, offsets, at, *refs):
    dq, dkv, dkv_prev, earlier, keep, send, low, before, total = refs[8:]
    width = dq.shape[1]
    lay_own(i, refs, low, before)
    total[:, 0:width] = earlier[:, 0:width] + dot_tn(low[...], dq[...])
    total[:, width:] = earlier[:, width:] + dot_tn(low[...], dkv[...])
    total[:, width:] += dot_tn(before[...], dkv_prev[...])
    half = len(offsets) // 2
    rows = total.shape[0] // len(offsets)
    for n, offset in enumerate(offsets):
        out = keep if n < half else send
        start = pl.multiple_of((at[0] ^ offset) * rows, rows)
        out[(n % half) * rows : (n % half + 1) * rows, :] = total[pl.ds(start, rows), :].astype(out.dtype)


def shape(rows, columns, dtype=BF):
    return jax.ShapeDtypeStruct((rows, columns), dtype)


D = 1024
MICRO = 2


def flip(block, axis, bit):
    return lax.ppermute(block, axis, [(i, i ^ bit) for i in range(lax.axis_size(axis))])


def shifted(block, distance):
    devices = range(lax.axis_size("seq"))
    route = [(i - distance, i) for i in devices if i - distance in devices]
    return lax.ppermute(block, "seq", route)


def far_slots(part):
    rows = part.shape[0] // 4
    return part[:rows], part[rows : 2 * rows], flip(part[2 * rows :], "mem", 2)


def near_slots(own, side, far):
    rows = own.shape[0]
    return own, flip(jnp.concatenate([side, far[rows:]], axis=0), "mem", 1), far


def near_sum(place, keep, send):
    rows, columns = keep.shape
    outs = [shape(rows // 2, columns, F32), shape(rows // 2, columns)]
    return call(near_kernel, place, (keep, flip(send, "mem", 1)), outs, time=1)


def seq_bits():
    count = lax.axis_size("seq")
    return [1 << i for i in reversed(range(count.bit_length() - 1))]


def seq_offsets(bits):
    offsets = [0]
    for bit in bits:
        offsets = offsets + [o ^ bit for o in offsets]
    return offsets


def seq_stage(block, bit):
    return jnp.concatenate([block, flip(block, "seq", bit)], axis=0)


def assemble_kernel(rows, offsets, at, first, second, *outs):
    half = len(offsets) // 2
    for i, offset in enumerate(offsets):
        ref = first if i < half else second
        start = pl.multiple_of((at[0] ^ offset) * rows, rows)
        column = 0
        for out in outs:
            columns = out.shape[1]
            place = slice((i % half) * rows, (i % half + 1) * rows)
            out[pl.ds(start, rows), :] = ref[place, column : column + columns]
            column += columns


def assemble(first, second, seq, bits, split):
    offsets = seq_offsets(bits)
    size = 2 * first.shape[0]
    outs = [shape(size, columns) for columns in split]
    return call(functools.partial(assemble_kernel, size // len(offsets), offsets), seq.reshape(1), (first, second), outs)


def reorder_kernel(rows, offsets, groups, at, *refs):
    keep, send = refs[-2:]
    half = len(offsets) // 2
    for i, offset in enumerate(offsets):
        start = pl.multiple_of((at[0] ^ offset) * rows, rows)
        out = keep if i < half else send
        place = slice((i % half) * rows, (i % half + 1) * rows)
        for column, terms in groups:
            total = None
            for term, first, columns in terms:
                part = refs[term][pl.ds(start, rows), first : first + columns].astype(F32)
                total = part if total is None else total + part
            out[place, column : column + columns] = total.astype(out.dtype)


def reorder(arrays, groups, seq, bits):
    offsets = seq_offsets(bits)
    size = arrays[0].shape[0]
    placed, column = [], 0
    for terms in groups:
        placed.append((column, terms))
        column += terms[0][2]
    kernel = functools.partial(reorder_kernel, size // len(offsets), offsets, placed)
    return call(kernel, seq.reshape(1), arrays, [shape(size // 2, column, F32), shape(size // 2, column)], time=column // 300)


def pack_kernel(width, half, at, *refs):
    me = at[0]
    (gain_self, gain_cross, gain_mlp), weights, (kept, message) = refs[:3], refs[3:11], refs[11:]
    query, key, value, out_w, cross_q, cross_k, cross_v, cross_o = weights

    def scaled(weight, gain):
        return (weight.astype(F32) * gain[...].astype(F32)).astype(BF)

    def piece(k):
        at_k = pl.ds(pl.multiple_of((me ^ k) * width, width), width)
        gained = [scaled(w[:, at_k], gain_self) for w in (query, key, value)]
        return jnp.concatenate(gained + [w[:, at_k] for w in (cross_k, cross_v)], axis=1)

    def side(k):
        at_k = pl.ds(pl.multiple_of(((me & 1) ^ k) * half, half), half)
        rows = gain_mlp.shape[0]
        lanes = lax.broadcasted_iota(jnp.int32, (rows, 128), 1)
        extra = jnp.where(lanes == 0, gain_mlp[...].astype(F32), 0.0).astype(BF)
        return jnp.concatenate([out_w[:, at_k], scaled(cross_q[:, at_k], gain_cross), cross_o[:, at_k], extra], axis=1)

    kept[...] = jnp.concatenate([piece(0), piece(1)], axis=1)
    message[...] = jnp.concatenate([piece(2), piece(3), side(0), side(1)], axis=1)


def repack_kernel(narrow, broad, at, kept, message, far, out):
    sides = 2 * narrow + broad
    out[:, 0:narrow] = kept[:, narrow:]
    out[:, narrow : 2 * narrow] = far[:, narrow : 2 * narrow]
    out[:, 2 * narrow : 2 * narrow + broad] = message[:, sides:]
    out[:, 2 * narrow + broad :] = far[:, sides:]


def unpack_kernel(width, narrow, broad, at, kept, message, far, near, qkv, first):
    me = at[0]
    start = 2 * narrow
    heads = [kept[:, 0:narrow], near[:, 0:narrow], far[:, 0:narrow], near[:, narrow:start]]
    sides = [message, near, far, near]
    sides = [ref[:, at_k : at_k + broad] for ref, at_k in zip(sides, (start, start, start, start + broad))]
    heads = join_pieces(heads, me, 0)
    sides = join_pieces(sides, me, 0)
    qkv[...] = heads[:, 0 : 3 * width]
    pair = broad - 128 - (broad - 128) // 3
    first[...] = jnp.concatenate([sides[:, 0:pair], heads[:, 3 * width :], sides[:, pair:]], axis=1)


class Stay:
    def __init__(self, value):
        self.value = value


def interleave(streams, sides):
    held = [next(s) for s in streams]
    results = [None] * len(streams)
    waiting = [(side, *next(side)) for side in sides]
    turn = 0
    ticks = 0

    def serve(arrays):
        nonlocal ticks, waiting
        ticks += 1
        due = [w for w in waiting if w[1] == ticks]
        waiting = [w for w in waiting if w[1] != ticks]
        arrays, taken = lax.optimization_barrier((arrays, [w[2]() for w in due]))
        for (side, _, _), got in zip(due, taken):
            try:
                waiting.append((side, *side.send(got)))
            except StopIteration:
                pass
        return arrays

    while True:
        other = (turn + 1) % len(streams)
        try:
            mark = streams[turn].send(held[turn])
            while isinstance(mark, Stay):
                mark = streams[turn].send(serve(mark.value))
            if results[other] is None:
                held[other], mark = serve((held[other], mark))
            else:
                mark = serve(mark)
            held[turn] = streams[turn].send(mark)
        except StopIteration as end:
            results[turn] = end.value
        if results[other] is None:
            turn = other
        elif results[turn] is not None:
            assert not waiting
            return results


def shards(
    inputs,
    memory,
    page_ids,
    memory_length,
    cotangent,
    gain_self,
    self_query,
    self_key,
    self_value,
    self_out,
    gain_cross,
    cross_query,
    cross_key,
    cross_value,
    cross_out,
    gain_mlp,
    mlp_in,
    mlp_out,
):
    seq = lax.axis_index("seq")
    me = lax.axis_index("mem")
    odd = me & 1
    blocks = lax.axis_size("mem")
    tok = inputs.shape[1]
    group = tok * blocks
    real = memory.shape[2]
    padded = -(-real // 16) * 16
    wrows = self_query.shape[0]
    bits = seq_bits()
    turned = bits[:-2] + [bits[-1], bits[-2]]
    half = D // 2

    def join_halves(own, other):
        return jnp.concatenate([jnp.where(odd == 0, own, other), jnp.where(odd == 0, other, own)], axis=1)

    width = self_query.shape[1] // blocks
    narrow, broad = 5 * width, 3 * half + 128
    place = me.reshape(1)
    weights = (self_query, self_key, self_value, self_out, cross_query, cross_key, cross_value, cross_out)
    gains = [g[:, None] for g in (gain_self, gain_cross, gain_mlp)]
    kept, message = call(
        functools.partial(pack_kernel, width, half), place, (*gains, *weights),
        [shape(wrows, 2 * narrow), shape(wrows, 2 * (narrow + broad))],
    )
    far = flip(message, "mem", 2)
    x_rows, tops = inputs.reshape(MICRO * tok, D), cotangent.reshape(MICRO * tok, D)
    lows = call(norm_kernel, place, (x_rows,), shape(MICRO * tok, D))
    befores = shifted(lows, 1)
    far_lows, near_lows = flip(lows, "mem", 2), flip(lows, "mem", 1)
    smem = pl.BlockSpec(memory_space=pltpu.SMEM)
    ids = page_ids.reshape(MICRO, -1, 128)
    places = pl.pallas_call(
        functools.partial(place_kernel, group),
        out_shape=[jax.ShapeDtypeStruct((8,), jnp.int32)] * MICRO,
        in_specs=[smem, smem, pl.BlockSpec(memory_space=pltpu.VMEM)],
        out_specs=[smem] * MICRO,
    )(jnp.stack([seq, me]), memory_length, ids)
    near = call(
        functools.partial(repack_kernel, narrow, broad), place, (kept, message, far),
        shape(*message.shape),
    )
    near = flip(near, "mem", 1)
    qkv_part, first_part = call(
        functools.partial(unpack_kernel, width, narrow, broad), place, (kept, message, far, near),
        [shape(blocks * wrows, columns) for columns in (3 * width, 3 * half + 128 + 2 * width)],
    )

    state = {}
    hidden = mlp_in.shape[0]
    stage = seq_stage(qkv_part, bits[0])
    stage, first_part, befores, memory_here = lax.optimization_barrier((stage, first_part, befores, memory))
    far_befores, near_befores = flip(befores, "mem", 2), flip(befores, "mem", 1)
    first_stage = first_part
    for bit in bits[:-3]:
        first_stage = seq_stage(first_stage, bit)
    first_pair = first_stage, flip(first_stage, "seq", bits[-3])
    memory_own = jnp.pad(memory_here.reshape(MICRO, real, D), ((0, 0), (0, padded - real), (0, 0)))
    memory_own = memory_own.reshape(MICRO * padded, D)
    hidden_part = jnp.concatenate([mlp_in, mlp_out], axis=0)
    for bit in bits[1:-1]:
        stage = seq_stage(stage, bit)
    stage, far_lows, memory_own, hidden_part, places = lax.optimization_barrier(
        (stage, far_lows, memory_own, hidden_part, places)
    )
    last_lows = flip(far_lows, "mem", 1)
    last_stage, first_pair, far_befores, memory_own, tops = lax.optimization_barrier(
        (flip(stage, "seq", bits[-1]), first_pair, far_befores, memory_own, tops)
    )
    first_stage = seq_stage(jnp.concatenate(first_pair, axis=0), bits[-2])
    memory_before = shifted(memory_own, 1)
    memory_far = flip(memory_own, "mem", 2)
    far_tops, near_tops = flip(tops, "mem", 2), flip(tops, "mem", 1)
    (qkv_full,) = assemble(stage, last_stage, seq, bits, [3 * width])
    gathered = [lows, near_lows, far_lows, last_lows, befores, near_befores, far_befores, flip(far_befores, "mem", 1)]

    def first_side():
        (first,) = yield 2, lambda: (first_stage,)
        cut = 2 * half + 2 * width
        first, last = first[:, :cut], first[:, cut:]
        first = first, flip(first, "seq", bits[-1])
        *first, last = yield 3, lambda: (*first, last)
        state["wide_own"], state["ckv"] = assemble(*first, seq, bits, [2 * half, 2 * width])
        state["wide_other"] = flip(state["wide_own"], "mem", 1)
        last = last, flip(last, "seq", bits[-1])
        last = yield 6, lambda: last
        state["cout_own"], gain = assemble(*last, seq, bits, [half, 128])
        state["gain"] = gain[:, 0].astype(F32)[None, :]
        state["cout_other"] = flip(state["cout_own"], "mem", 1)

    def memory_side():
        before, near_own = yield 2, lambda: (memory_before, flip(memory_own, "mem", 1))
        far_prev, near_prev = flip(before, "mem", 2), flip(before, "mem", 1)
        *gone, far_own = yield 3, lambda: (before, near_own, far_prev, near_prev, memory_far)
        before, near_own, far_prev, near_prev = gone
        last_own, last_prev = flip(far_own, "mem", 1), flip(far_prev, "mem", 1)
        pieces = memory_own, near_own, far_own, last_own, before, near_prev, far_prev, last_prev
        pieces = yield 4, lambda: pieces
        whole = blocks * padded
        outs = [shape(whole, D)] * (2 * MICRO) + [shape(whole, 2 * width)] * (2 * MICRO)
        got = call(functools.partial(memory_kernel, padded), place, (*pieces, state["ckv"]), outs, time=6)
        state["rows"], state["rows_prev"], state["mem_kv"], state["mem_prev"] = (
            got[k * MICRO : (k + 1) * MICRO] for k in range(4)
        )

    def top_side():
        far, near = yield 2, lambda: (far_tops, near_tops)
        state["top"] = tops, near, far, flip(far, "mem", 1)

    def hidden_side():
        (part,) = yield 2, lambda: (hidden_part,)
        whole = lax.all_gather(part, "seq", axis=0, tiled=True)
        (whole,) = yield 8, lambda: (whole,)
        both = [shape(whole.shape[0] // 2, D)] * 2
        both = call(functools.partial(hidden_kernel, hidden), place, (whole,), both)
        state["inner"], state["outer"] = yield 9, lambda: both
        kernel = functools.partial(hidden_grads_kernel, hidden)
        arrays = yield 11, lambda: state["grad_hidden"][0]
        grads = call(kernel, place, arrays, shape(2 * D, D), time=9)
        arrays = yield 12, lambda: (*state["grad_hidden"][1], grads)
        grads = call(kernel, place, arrays, shape(2 * D, D), time=9)
        (grads,) = yield 13, lambda: (grads,)
        grads = lax.psum_scatter(grads, "seq", scatter_dimension=0, tiled=True)
        (grads,) = yield 19, lambda: (grads,)
        state["hidden_grads"] = grads[:hidden].astype(F32), grads[hidden:].astype(F32)

    order = turned[::-1]

    def seq_next(kept, received, bit):
        rows, columns = kept.shape[0] // 2, kept.shape[1]
        kept, sent = call(tree_kernel, place, (kept, received), [shape(rows, columns, F32), shape(rows, columns)])
        return kept, flip(sent, "seq", bit)

    def half_grads(names):
        arrays = [part for low, mine, others in names for part in (*low, *mine, *others)]
        outs = [shape(D, len(names) * half, F32), shape(D, len(names) * half)]
        return call(functools.partial(half_grads_kernel, len(names)), place, arrays, outs, time=2 * len(names))

    def tree_side(name, arrays, groups, ticks):
        arrays = yield ticks[0], lambda: arrays
        kept, sent = reorder(arrays, groups, seq, turned)
        pair = kept, flip(sent, "seq", order[0])
        for bit, tick in zip(order[1:], ticks[1:]):
            pair = yield tick, lambda: pair
            pair = seq_next(*pair, bit)
        state[name] = pair

    def cout_side():
        names, gains = yield 15, lambda: (state["grad_cout"], state["grad_gain_three"])
        own, other = half_grads([list(zip(*names))])
        gains = jnp.pad((gains[0] + gains[1]).reshape(D, 1), ((0, 0), (0, 127)))
        groups = [[(0, 0, half), (1, 0, half)], [(2, 0, 128)]]
        yield from tree_side("cout", (own, flip(other, "mem", 1), gains), groups, (16, 20))

    def wide_side():
        out, query, dmem = yield 17, lambda: (state["grad_out"], state["grad_cquery"], state["dmem"])
        own, other = half_grads([list(zip(*out)), list(zip(*query))])
        other = flip(other, "mem", 1)
        mem_rows = shape(8 * padded, D)
        arrays = (*(part for pair in zip(*dmem) for part in pair), *state["rows"], *state["rows_prev"], state["ckv"])
        ckv, mem_keep, mem_send = call(
            memory_back_kernel, place, arrays, [shape(D, 2 * width, F32), mem_rows, mem_rows], time=10
        )
        state["memory_parts"] = mem_keep, flip(mem_send, "mem", 1)
        groups = [[(0, 0, 2 * half), (1, 0, 2 * half)], [(2, 0, 2 * width)]]
        yield from tree_side("wide", (own, other, ckv), groups, (18, 19, 20))

    def memory_grads_side():
        parts = yield 18, lambda: state["memory_parts"]
        rows = 4 * padded
        near, far = call(near_kernel, place, parts, [shape(rows, D, F32), shape(rows, D)], time=1)
        near, far = yield 20, lambda: (near, far)
        state["memory_sums"] = near, flip(far, "mem", 2)

    for name in ("hidden", "gain_three", "cout", "out", "cquery", "qkv"):
        state["grad_" + name] = []
    state["dmem"] = []
    quarter = [shape(tok, width), shape(tok, width), shape(2 * tok, width)]
    rounded, exact, column = shape(tok, D), shape(tok, D, F32), shape(tok, 1, F32)
    half_rows, whole, pair_rows = shape(tok, half), shape(group, D), shape(2 * tok, D)

    def far_pieces(pieces):
        return pieces[0], pieces[1], flip(pieces[2], "mem", 2)

    def stream(i):
        at = places[i]
        pieces = yield gathered
        qkv, kv_prev = call(
            functools.partial(qkv_kernel, i, tok), place, (*pieces, qkv_full),
            [shape(group, 3 * width), shape(group, 2 * width)], time=5,
        )
        if i == 0:
            qkv, kv_prev = yield Stay((qkv, kv_prev))
        self_o, self_lse = self_forward(at, qkv, kv_prev, blocks)
        self_lse = yield self_lse

        pieces = yield far_slots(self_o)
        self_low, after_self, plain_two, low_two, scale_two, *pieces = call(
            functools.partial(self_out_kernel, i), place,
            (*near_slots(*pieces), x_rows, state["wide_own"], state["wide_other"]),
            [rounded, exact, exact, rounded, column, *quarter], time=4,
        )
        scale_two = yield scale_two

        pieces = yield far_pieces(pieces)
        mem_kv, mem_prev = state["mem_kv"][i], state["mem_prev"][i]
        cross_o, cross_lse, cross_q = cross_forward(at, near_slots(*pieces), mem_prev, mem_kv, blocks, real)
        cross_lse = yield cross_lse

        pieces = yield far_slots(cross_o)
        cross_low, after_cross, plain_three, scale_three, low_three = call(
            cross_out_kernel, place,
            (*near_slots(*pieces), after_self, state["cout_own"], state["cout_other"], state["gain"]),
            [rounded, exact, exact, column, rounded], time=3,
        )
        scale_three = yield scale_three

        low_three, near, far = yield low_three, flip(low_three, "mem", 1), flip(low_three, "mem", 2)
        low_all, top_all, act, pre_low, grad_keep, grad_send, out_keep, out_send = call(
            functools.partial(mlp_kernel, i), place,
            (low_three, near, far, flip(far, "mem", 1), *state["top"], state["inner"], state["outer"]),
            [whole, whole, whole, whole, pair_rows, pair_rows, pair_rows, pair_rows], time=15,
        )
        state["grad_hidden"].append((pre_low, low_all, act, top_all))
        grad_keep, grad_send = yield grad_keep, grad_send

        near, far = near_sum(place, grad_keep, grad_send)
        far, out_send = yield flip(far, "mem", 2), out_send
        grad_after_cross, mine, others, gain_three, *pieces = call(
            functools.partial(cross_back_kernel, i), place,
            (near, far, plain_three, scale_three, state["gain"], tops, state["cout_own"], state["cout_other"]),
            [exact, half_rows, half_rows, shape(1, D, F32), *quarter], time=3,
        )
        state["grad_gain_three"].append(gain_three)
        state["grad_cout"].append((cross_low, mine, others))
        grad_after_cross = yield grad_after_cross

        pieces, out_send = yield far_pieces(pieces), out_send
        dcq, dmem_prev, dmem = cross_backward(
            at, cross_q, mem_prev, mem_kv, cross_o, near_slots(*pieces), cross_lse, blocks, real
        )
        out_near, out_far = near_sum(place, out_keep, out_send)
        dmem = yield dmem

        pieces, out_far = yield far_slots(dcq), out_far
        out_far = flip(out_far, "mem", 2)
        grad_after_self, query_mine, query_others, mine, others, *pieces = call(
            self_back_kernel, place,
            (*near_slots(*pieces), plain_two, scale_two, grad_after_cross, state["wide_own"], state["wide_other"]),
            [exact, half_rows, half_rows, half_rows, half_rows, *quarter], time=4,
        )
        state["grad_cquery"].append((low_two, query_mine, query_others))
        state["grad_out"].append((self_low, mine, others))
        state["dmem"].append((dmem, dmem_prev))
        grad_after_self = yield grad_after_self

        pieces, out_far = yield far_pieces(pieces), out_far
        pieces = near_slots(*pieces)
        if i == 0:
            pieces = yield Stay(pieces)
        dq, dkv, dkv_prev = self_backward(at, qkv, kv_prev, self_o, pieces, self_lse, blocks)
        grads = (*gathered, dq, dkv, dkv_prev)
        lows_scratch = [pltpu.VMEM((group, D), BF)] * 2
        if i == 0:
            grads = call(
                functools.partial(qkv_grads_kernel, i), place, grads, shape(D, 3 * width, F32),
                [*lows_scratch, pltpu.VMEM((D, 2 * width), F32)], time=6,
            )
            state["grad_qkv"].append(grads)
        else:
            grads = call(
                functools.partial(last_qkv_grads_kernel, i, seq_offsets(turned)), seq.reshape(1),
                (*grads, state["grad_qkv"][0]), [shape(D // 2, 3 * width, F32), shape(D // 2, 3 * width)],
                [*lows_scratch, pltpu.VMEM((D, 3 * width), F32)], time=7,
            )
        output = call(output_kernel, place, (after_cross, out_near, out_far), rounded)
        if i < MICRO - 1:
            back = call(qkv_back_kernel, place, (dq, dkv, dkv_prev, qkv_full), [pair_rows] * 4, time=5)
            back, state["grad_qkv"][0] = yield last_near(*back), grads
            back = yield last_far(*back)
        else:
            state["last_qkv"], dq, dkv, dkv_prev = yield grads, dq, dkv, dkv_prev
            back = call(qkv_back_kernel, place, (dq, dkv, dkv_prev, qkv_full), [pair_rows] * 4, time=5)
            yield ()
        return output, grad_after_self, back

    def last_near(keep, send, keep_prev, send_prev):
        return [near_sum(place, *pair) for pair in ((keep_prev, send_prev), (keep, send))]

    def last_far(*pairs):
        return [part for near, far in pairs for part in (near, flip(far, "mem", 2))]

    def back_rows(near_prev, far_prev, near, far):
        return shifted(call(far_sum_kernel, place, (near_prev, far_prev), rounded), -1)

    def final_rows(i, sums, back):
        grads = x_rows, done[i][1], sums[2], sums[3], back
        return call(functools.partial(grad_x_kernel, i), place, grads, exact)

    sides = [first_side(), memory_side(), top_side(), hidden_side(), cout_side(), wide_side(), memory_grads_side()]
    done = interleave([stream(i) for i in range(MICRO)], sides)

    def wide_finish(own):
        high = me >> 1
        rows_two = own.reshape(2, 2 * wrows, own.shape[1])
        theirs = lax.dynamic_index_in_dim(rows_two, 1 - high, 0, keepdims=False).astype(BF)
        own = lax.dynamic_index_in_dim(rows_two, high, 0, keepdims=False) + flip(theirs, "mem", 2).astype(F32)
        rows_two = own.reshape(2, wrows, own.shape[1])
        theirs = lax.dynamic_index_in_dim(rows_two, 1 - odd, 0, keepdims=False)
        own = lax.dynamic_index_in_dim(rows_two, odd, 0, keepdims=False)
        return own, flip(theirs.astype(BF), "mem", 1).astype(F32)

    def head_finish(summed, count):
        slots = summed.astype(BF).reshape(blocks, wrows, -1)
        first, second, *rest = [lax.dynamic_index_in_dim(slots, me ^ k, 0, keepdims=False) for k in range(4)]
        far = flip(jnp.concatenate(rest, axis=0), "mem", 2)
        own, near, far = near_slots(first, second, far)
        whole = join_pieces([own, near[:wrows], far[:wrows], near[wrows:]], me, 1).astype(F32)
        whole = whole.reshape(wrows, blocks, count, -1)
        return [whole[:, :, k].reshape(wrows, D) for k in range(count)]

    def seq_finish(pair, left):
        for bit in left:
            pair = seq_next(*pair, bit)
        return pair[0] + pair[1].astype(F32)

    tie = lax.optimization_barrier
    kept, sent = state["last_qkv"]
    qkv_pair = kept, flip(sent, "seq", order[0])
    sums = [done[0][2]]
    backs = [back_rows(*sums[0])]
    nears, memory_sums = tie((last_near(*done[1][2]), state["memory_sums"]))
    sums.append(last_far(*nears))
    qkv_pair, sums, backs, memory_sums, cout_pair = tie((qkv_pair, sums, backs, memory_sums, state["cout"]))
    qkv_pair = seq_next(*qkv_pair, order[1])
    backs.append(back_rows(*sums[1]))
    memory_near, memory_far = memory_sums
    both = call(far_sum_kernel, place, (memory_near, memory_far), shape(4 * padded, D))
    mem_own, mem_back = both[: 2 * padded], shifted(both[2 * padded :], -1)
    wide_pair, cout_pair = state["wide"], seq_next(*cout_pair, order[2])
    for bit in order[3:]:
        wide_pair, cout_pair = seq_next(*wide_pair, bit), seq_next(*cout_pair, bit)
    qkv_pair, wide_pair, cout_pair = tie((qkv_pair, wide_pair, cout_pair))
    qkv_pair = seq_next(*qkv_pair, order[2])
    for bit in order[3:]:
        qkv_pair = seq_next(*qkv_pair, bit)
    grad_rows = [final_rows(i, sums[i], backs[i]) for i in range(MICRO)]
    grad_mem = mem_own.reshape(MICRO, 1, padded, D).astype(F32) + mem_back.reshape(MICRO, 1, padded, D).astype(F32)
    grad_inner, grad_outer = state["hidden_grads"]
    own, near = wide_finish(seq_finish(cout_pair, []))
    grad_cout = join_halves(own[:, :half], near[:, :half])
    grad_gain_mlp = own[:, half] + near[:, half]
    last = seq_finish(wide_pair, [])
    grad_ckey, grad_cvalue = head_finish(last[:, 2 * half :], 2)
    own, near = wide_finish(last[:, : 2 * half])
    grad_out, plain_cquery = [
        join_halves(own[:, k * half : (k + 1) * half], near[:, k * half : (k + 1) * half]) for k in range(2)
    ]
    plain_qkv = head_finish(seq_finish(qkv_pair, []), 3)

    def gained(gain, weights, plains):
        scale = gain.astype(F32)[:, None]
        grad_gain = sum(jnp.sum(w.astype(F32) * p, axis=1) for w, p in zip(weights, plains))
        return grad_gain, [p * scale for p in plains]

    grad_gain_self, (grad_query, grad_key, grad_value) = gained(
        gain_self, (self_query, self_key, self_value), plain_qkv
    )
    grad_gain_cross, (grad_cquery,) = gained(gain_cross, (cross_query,), (plain_cquery,))
    return (
        jnp.stack([d[0] for d in done]),
        jnp.stack(grad_rows),
        grad_mem[:, :, :real],
        grad_gain_self,
        grad_query,
        grad_key,
        grad_value,
        grad_out,
        grad_gain_cross,
        grad_cquery,
        grad_ckey,
        grad_cvalue,
        grad_cout,
        grad_gain_mlp,
        grad_inner,
        grad_outer,
    )


def solution(mesh):
    rows = P(("seq", "mem"), None)
    tokens = P(None, ("seq", "mem"), None)
    pages = P(None, "seq", "mem", None)
    gains = P(("seq", "mem"))
    return jax.shard_map(
        shards,
        mesh=mesh,
        in_specs=(tokens, pages, P(), P(), tokens, gains, rows, rows, rows, rows, gains, rows, rows, rows, rows,
                  gains, rows, rows),
        out_specs=(tokens, tokens, pages, gains, rows, rows, rows, rows, gains, rows, rows, rows, rows, gains,
                   rows, rows),
        check_vma=False,
    )
```

```python
import functools
import math
import jax
import jax.numpy as jnp
import numpy as np
from jax import lax
from jax.experimental import pallas as pl
from jax.experimental.pallas import tpu as pltpu
from jax.sharding import PartitionSpec as P

HEAD = 64
BF = jnp.bfloat16
F32 = jnp.float32
LOWEST = -1e30


def head_lanes(rows, width):
    return lax.broadcasted_iota(jnp.int32, (rows, width), 1) // HEAD


def one_head(block, lanes, head):
    return jnp.where(lanes == head, block, jnp.zeros_like(block))


def dot_nt(left, right):
    return lax.dot_general(left, right, (((1,), (1,)), ((), ())), preferred_element_type=F32)


def dot_nn(left, right):
    return lax.dot_general(left, right, (((1,), (0,)), ((), ())), preferred_element_type=F32)


def dot_tn(left, right):
    return lax.dot_general(left, right, (((0,), (0,)), ((), ())), preferred_element_type=F32)


def self_range(p, rows, blocks, spill, prev_spill):
    first = jnp.where(p * rows < spill, prev_spill // rows, blocks + spill // rows)
    return first, blocks + p + 1


def self_allowed(query, key, extent, spill, prev_spill):
    first = jnp.where(query < spill, prev_spill, extent + spill)
    return (key >= first) & (key <= extent + query)


def cross_allowed(query, place, side, spill, length, me, padded, real):
    part = place // padded
    inner = place - part * padded
    row = (part ^ me) * real + inner
    return (inner < real) & (row < length) & ((query < spill) == (side == 0))


def fold(block, combine):
    total = block[0:8]
    for r in range(8, block.shape[0], 8):
        total = combine(total, block[r : r + 8])
    return total


def lay_heads(out, block, lanes, heads):
    rows = block.shape[0]
    for h in range(heads):
        out[h * rows : (h + 1) * rows, :] = one_head(block, lanes, h)


def score_block(kb, k, allowed, q_cat, s_scr, tops):
    rows = s_scr.shape[3]
    found = []
    for h, top in enumerate(tops):
        s = jnp.where(allowed, dot_nt(k, q_cat[h * rows : (h + 1) * rows, :]), LOWEST)
        s_scr[kb, h] = s
        found.append(jnp.maximum(top, fold(s, jnp.maximum)))
    return tuple(found)


def weigh_block(kb, tops, totals, s_scr, p_scr, v_cat):
    count = s_scr.shape[2]
    summed = []
    for h, (top, total) in enumerate(zip(tops, totals)):
        e = jnp.exp(s_scr[kb, h] - top)
        p_scr[h * count : (h + 1) * count, :] = e.astype(BF)
        summed.append(total + fold(e, jnp.add))
    return tuple(summed), dot_tn(p_scr[...], v_cat)


def attend(first, last, heads, scores, values, s_scr, p_scr, width):
    rows = s_scr.shape[3]
    lowest = jnp.full((8, rows), LOWEST, F32)
    tops = lax.fori_loop(first, last, scores, (lowest,) * heads)
    tops = tuple(jnp.max(top, axis=0, keepdims=True) for top in tops)

    def step(kb, carry):
        totals, acc = carry
        totals, more = weigh_block(kb, tops, totals, s_scr, p_scr, values(kb))
        return totals, acc + more

    start = (jnp.zeros((8, rows), F32),) * heads, jnp.zeros((rows, width), F32)
    totals, acc = lax.fori_loop(first, last, step, start)
    return tops, tuple(jnp.sum(total, axis=0, keepdims=True) for total in totals), acc


def finish(p, start, tops, totals, acc, lanes, o_ref, lse_ref):
    rows = acc.shape[0]
    heads = len(tops)
    inverse = jnp.concatenate([1.0 / total for total in totals] + [jnp.zeros((8 - heads, rows), F32)], axis=0).T
    spread_out = jnp.zeros(acc.shape, F32)
    for h in range(heads):
        spread_out = jnp.where(lanes == h, inverse[:, h : h + 1], spread_out)
    o_ref[pl.ds(start, rows), :] = (acc * spread_out).astype(BF)
    place = pl.ds(pl.multiple_of(p * rows, rows), rows)
    for h in range(heads):
        lse_ref[h : h + 1, place] = tops[h] + jnp.log(totals[h])


def self_forward_kernel(rows, blocks, heads, sc, qkv, kvp, o_ref, lse_ref, k_scr, v_scr, s_scr, q_cat, p_scr):
    width = heads * HEAD
    extent = rows * blocks
    me, spill, prev_spill = sc[0], sc[1], sc[4]
    lanes = head_lanes(rows, width)

    def place(b):
        return pl.multiple_of((b ^ me) * rows, rows)

    first_used, _ = self_range(0, rows, blocks, spill, prev_spill)

    @pl.loop(first_used, 2 * blocks)
    def _(kb):
        def fill(keys, values):
            k_scr[kb] = keys
            lay_heads(v_scr.at[kb], values, lanes, heads)

        @pl.when(kb < blocks)
        def _():
            at = pl.ds(place(kb), rows)
            fill(kvp[at, 0:width], kvp[at, width : 2 * width])

        @pl.when(kb >= blocks)
        def _():
            at = pl.ds(place(kb - blocks), rows)
            fill(qkv[at, width : 2 * width], qkv[at, 2 * width : 3 * width])

    @pl.loop(0, blocks)
    def _(p):
        lay_heads(q_cat, qkv[pl.ds(place(p), rows), 0:width] * jnp.asarray(0.125, BF), lanes, heads)
        first, last = self_range(p, rows, blocks, spill, prev_spill)
        query = p * rows + lax.broadcasted_iota(jnp.int32, (1, rows), 1)

        def scores(kb, tops):
            key = kb * rows + lax.broadcasted_iota(jnp.int32, (rows, rows), 0)
            return score_block(kb, k_scr[kb], self_allowed(query, key, extent, spill, prev_spill), q_cat, s_scr, tops)

        tops, totals, acc = attend(first, last, heads, scores, lambda kb: v_scr[kb], s_scr, p_scr, width)
        finish(p, place(p), tops, totals, acc, lanes, o_ref, lse_ref)


def lay(out, own, near, far):
    rows = own.shape[0]
    out[0:rows, :] = own[...]
    out[rows : 2 * rows, :] = near[0:rows, :]
    out[2 * rows : 3 * rows, :] = far[0:rows, :]
    out[3 * rows :, :] = near[rows:, :]


def cross_forward_kernel(rows, blocks, heads, padded, real, sc, own, near, far, kv0, kv1, o_ref, lse_ref, q_ref,
                         v_scr, s_scr, q_cat, p_scr):
    lay(q_ref, own, near, far)
    width = heads * HEAD
    keys = kv0.shape[0]
    me, spill = sc[0], sc[1]
    lanes = head_lanes(rows, width)
    key_lanes = head_lanes(keys, width)
    kvs = (kv0, kv1)

    def place(b):
        return pl.multiple_of((b ^ me) * rows, rows)

    for side in range(2):
        lay_heads(v_scr.at[side], kvs[side][:, width : 2 * width], key_lanes, heads)

    @pl.loop(0, blocks)
    def _(p):
        lay_heads(q_cat, q_ref[pl.ds(place(p), rows), :] * jnp.asarray(0.125, BF), lanes, heads)
        query = p * rows + lax.broadcasted_iota(jnp.int32, (1, rows), 1)

        def scores(side, tops):
            spot = lax.broadcasted_iota(jnp.int32, (keys, 1), 0)
            length = jnp.where(side == 0, sc[2], sc[3])
            allowed = cross_allowed(query, spot, side, spill, length, me, padded, real)
            k = jnp.where(side == 0, kv0[:, 0:width], kv1[:, 0:width])
            return score_block(side, k, allowed, q_cat, s_scr, tops)

        first = jnp.where(p * rows < spill, 0, 1)
        last = jnp.where((p + 1) * rows > spill, 2, 1)
        tops, totals, acc = attend(first, last, heads, scores, lambda side: v_scr[side], s_scr, p_scr, width)
        finish(p, place(p), tops, totals, acc, lanes, o_ref, lse_ref)


def spread(p, at, rows, heads, q, g, o_ref, lse_ref, lanes, q_cat, g_cat, stat):
    weighted = (g.astype(F32) * o_ref[at, :].astype(F32)).T
    for h in range(heads):
        q_cat[h * rows : (h + 1) * rows, :] = one_head(q, lanes, h)
        g_cat[h * rows : (h + 1) * rows, :] = one_head(g, lanes, h)
        stat[heads + h : heads + h + 1, :] = jnp.sum(weighted[h * HEAD : (h + 1) * HEAD, :], axis=0, keepdims=True)
    stat[0:heads, :] = lse_ref[0:heads, pl.ds(pl.multiple_of(p * rows, rows), rows)]


def back_block(rows, heads, k, v, allowed, q_cat, g_cat, stat, w_scr, ds_wide, ds_tall):
    count = k.shape[0]
    for h in range(heads):
        span = slice(h * rows, (h + 1) * rows)
        s = dot_nt(k, q_cat[span, :])
        e = jnp.where(allowed, jnp.exp(s - stat[h : h + 1, :]), 0.0)
        de = dot_nt(v, g_cat[span, :])
        ds = (e * (de - stat[heads + h : heads + h + 1, :])).astype(BF)
        w_scr[:, span] = e.astype(BF)
        ds_wide[:, span] = ds
        ds_tall[h * count : (h + 1) * count, :] = ds


def self_backward_kernel(rows, blocks, heads, sc, qkv, kvp, o_ref, own, near, far, lse_ref, dq_ref, dkv_ref,
                         dprev_ref, g_ref, kv_scr, k_cat, dkv_scr, q_cat, g_cat, stat, w_scr, ds_wide, ds_tall):
    lay(g_ref, own, near, far)
    width = heads * HEAD
    extent = rows * blocks
    me, spill, prev_spill = sc[0], sc[1], sc[4]
    lanes = head_lanes(rows, width)

    def place(b):
        return pl.multiple_of((b ^ me) * rows, rows)

    first_used, _ = self_range(0, rows, blocks, spill, prev_spill)

    @pl.loop(0, 2 * blocks)
    def _(kb):
        dkv_scr[kb] = jnp.zeros(dkv_scr.shape[1:], F32)

    @pl.loop(first_used, 2 * blocks)
    def _(kb):
        def fill(pair):
            kv_scr[kb] = pair
            scaled = pair[:, 0:width] * jnp.asarray(0.125, BF)
            for h in range(heads):
                k_cat[kb, h * rows : (h + 1) * rows, :] = one_head(scaled, lanes, h)

        @pl.when(kb < blocks)
        def _():
            fill(kvp[pl.ds(place(kb), rows), :])

        @pl.when(kb >= blocks)
        def _():
            fill(qkv[pl.ds(place(kb - blocks), rows), width : 3 * width])

    @pl.loop(0, blocks)
    def _(p):
        at = pl.ds(place(p), rows)
        q = qkv[at, 0:width] * jnp.asarray(0.125, BF)
        g = g_ref[at, :]
        spread(p, at, rows, heads, q, g, o_ref, lse_ref, lanes, q_cat, g_cat, stat)
        first, last = self_range(p, rows, blocks, spill, prev_spill)
        query = p * rows + lax.broadcasted_iota(jnp.int32, (1, rows), 1)

        def step(kb, dq):
            key = kb * rows + lax.broadcasted_iota(jnp.int32, (rows, 1), 0)
            allowed = self_allowed(query, key, extent, spill, prev_spill)
            back_block(rows, heads, kv_scr[kb, :, 0:width], kv_scr[kb, :, width : 2 * width], allowed,
                       q_cat, g_cat, stat, w_scr, ds_wide, ds_tall)
            dkv_scr[kb, :, 0:width] += dot_nn(ds_wide[...], q_cat[...])
            dkv_scr[kb, :, width : 2 * width] += dot_nn(w_scr[...], g_cat[...])
            return dq + dot_tn(ds_tall[...], k_cat[kb])

        dq = lax.fori_loop(first, last, step, jnp.zeros((rows, width), F32))
        dq_ref[at, :] = dq.astype(BF)

    @pl.loop(0, blocks)
    def _(b):
        at = pl.ds(place(b), rows)
        dprev_ref[at, :] = dkv_scr[b].astype(BF)
        dkv_ref[at, :] = dkv_scr[blocks + b].astype(BF)


def cross_backward_kernel(rows, blocks, heads, padded, real, pieces, sc, q_ref, kv0, kv1, o_ref, own, near, far,
                          lse_ref, dq_ref, dkv0_ref, dkv1_ref, g_ref, k_cat, dkv_scr, q_cat, g_cat, stat, w_scr, ds_wide, ds_tall):
    lay(g_ref, own, near, far)
    width = heads * HEAD
    keys = kv0.shape[0]
    step_keys = keys // pieces
    me, spill = sc[0], sc[1]
    lanes = head_lanes(rows, width)
    key_lanes = head_lanes(step_keys, width)
    kvs = (kv0, kv1)

    def place(b):
        return pl.multiple_of((b ^ me) * rows, rows)

    dkv_scr[...] = jnp.zeros(dkv_scr.shape, F32)
    for side in range(2):
        for piece in range(pieces):
            scaled = kvs[side][piece * step_keys : (piece + 1) * step_keys, 0:width] * jnp.asarray(0.125, BF)
            for h in range(heads):
                k_cat[side * pieces + piece, h * step_keys : (h + 1) * step_keys, :] = one_head(scaled, key_lanes, h)

    @pl.loop(0, blocks)
    def _(p):
        at = pl.ds(place(p), rows)
        q = q_ref[at, :] * jnp.asarray(0.125, BF)
        spread(p, at, rows, heads, q, g_ref[at, :], o_ref, lse_ref, lanes, q_cat, g_cat, stat)
        query = p * rows + lax.broadcasted_iota(jnp.int32, (1, rows), 1)
        reads = (p * rows < spill, (p + 1) * rows > spill)
        first = jnp.where(reads[0], 0, pieces)
        last = jnp.where(reads[1], 2 * pieces, pieces)

        def step(kb, dq):
            side = kb // pieces
            at_key = pl.ds(pl.multiple_of((kb - side * pieces) * step_keys, step_keys), step_keys)
            spot = (kb - side * pieces) * step_keys + lax.broadcasted_iota(jnp.int32, (step_keys, 1), 0)
            length = jnp.where(side == 0, sc[2], sc[3])
            allowed = cross_allowed(query, spot, side, spill, length, me, padded, real)
            is_prev = side == 0
            pair = jnp.where(is_prev, kv0[at_key, :], kv1[at_key, :])
            back_block(rows, heads, pair[:, 0:width], pair[:, width : 2 * width], allowed,
                       q_cat, g_cat, stat, w_scr, ds_wide, ds_tall)
            dkv_scr[kb, :, 0:width] += dot_nn(ds_wide[...], q_cat[...])
            dkv_scr[kb, :, width : 2 * width] += dot_nn(w_scr[...], g_cat[...])
            return dq + dot_tn(ds_tall[...], k_cat[kb])

        dq = lax.fori_loop(first, last, step, jnp.zeros((rows, width), F32))
        dq_ref[at, :] = dq.astype(BF)

    for piece in range(pieces):
        span = slice(piece * step_keys, (piece + 1) * step_keys)
        dkv0_ref[span, :] = dkv_scr[piece].astype(BF)
        dkv1_ref[span, :] = dkv_scr[pieces + piece].astype(BF)


def call(kernel, scalars, arrays, outs, scratch=(), time=2):
    vmem = pl.BlockSpec(memory_space=pltpu.VMEM)
    held = (*arrays, *jax.tree.leaves(outs), *scratch)
    room = sum(math.prod(a.shape) * jnp.dtype(a.dtype).itemsize for a in held) + 12 * 2**20
    return pl.pallas_call(
        kernel,
        out_shape=outs,
        in_specs=[pl.BlockSpec(memory_space=pltpu.SMEM)] + [vmem] * len(arrays),
        out_specs=jax.tree.map(lambda _: vmem, outs),
        scratch_shapes=scratch,
        compiler_params=pltpu.CompilerParams(vmem_limit_bytes=min(room, 48 * 2**20)),
        cost_estimate=pl.CostEstimate(flops=1024, bytes_accessed=int(time * 640000), transcendentals=0),
    )(scalars, *arrays)


def self_forward(scalars, qkv, kvp, blocks):
    extent = qkv.shape[0]
    rows = extent // blocks
    width = qkv.shape[1] // 3
    heads = width // HEAD
    return call(
        functools.partial(self_forward_kernel, rows, blocks, heads),
        scalars,
        (qkv, kvp),
        [jax.ShapeDtypeStruct((extent, width), BF), jax.ShapeDtypeStruct((8, extent), F32)],
        [
            pltpu.VMEM((2 * blocks, rows, width), BF),
            pltpu.VMEM((2 * blocks, heads * rows, width), BF),
            pltpu.VMEM((2 * blocks, heads, rows, rows), F32),
            pltpu.VMEM((heads * rows, width), BF),
            pltpu.VMEM((heads * rows, rows), BF),
        ],
        time=18,
    )


def cross_forward(scalars, pieces, kv0, kv1, blocks, real):
    rows, width = pieces[0].shape
    extent = rows * blocks
    heads = width // HEAD
    keys = kv0.shape[0]
    return call(
        functools.partial(cross_forward_kernel, rows, blocks, heads, keys // blocks, real),
        scalars,
        (*pieces, kv0, kv1),
        [
            jax.ShapeDtypeStruct((extent, width), BF),
            jax.ShapeDtypeStruct((8, extent), F32),
            jax.ShapeDtypeStruct((extent, width), BF),
        ],
        [
            pltpu.VMEM((2, heads * keys, width), BF),
            pltpu.VMEM((2, heads, keys, rows), F32),
            pltpu.VMEM((heads * rows, width), BF),
            pltpu.VMEM((heads * keys, rows), BF),
        ],
        time=9,
    )


def back_scratch(rows, heads, width, keys):
    return [
        pltpu.VMEM((heads * rows, width), BF),
        pltpu.VMEM((heads * rows, width), BF),
        pltpu.VMEM((8, rows), F32),
        pltpu.VMEM((keys, heads * rows), BF),
        pltpu.VMEM((keys, heads * rows), BF),
        pltpu.VMEM((heads * keys, rows), BF),
    ]


def self_backward(scalars, qkv, kvp, o, g, lse, blocks):
    extent = qkv.shape[0]
    rows = extent // blocks
    width = qkv.shape[1] // 3
    heads = width // HEAD
    return call(
        functools.partial(self_backward_kernel, rows, blocks, heads),
        scalars,
        (qkv, kvp, o, *g, lse),
        [
            jax.ShapeDtypeStruct((extent, width), BF),
            jax.ShapeDtypeStruct((extent, 2 * width), BF),
            jax.ShapeDtypeStruct((extent, 2 * width), BF),
        ],
        [
            pltpu.VMEM((extent, width), BF),
            pltpu.VMEM((2 * blocks, rows, 2 * width), BF),
            pltpu.VMEM((2 * blocks, heads * rows, width), BF),
            pltpu.VMEM((2 * blocks, rows, 2 * width), F32),
        ]
        + back_scratch(rows, heads, width, rows),
        time=22,
    )


def cross_backward(scalars, q, kv0, kv1, o, g, lse, blocks, real, pieces=1):
    extent, width = q.shape
    rows = extent // blocks
    heads = width // HEAD
    keys = kv0.shape[0]
    step_keys = keys // pieces
    return call(
        functools.partial(cross_backward_kernel, rows, blocks, heads, keys // blocks, real, pieces),
        scalars,
        (q, kv0, kv1, o, *g, lse),
        [
            jax.ShapeDtypeStruct((extent, width), BF),
            jax.ShapeDtypeStruct((keys, 2 * width), BF),
            jax.ShapeDtypeStruct((keys, 2 * width), BF),
        ],
        [
            pltpu.VMEM((extent, width), BF),
            pltpu.VMEM((2 * pieces, heads * step_keys, width), BF),
            pltpu.VMEM((2 * pieces, step_keys, 2 * width), F32),
        ]
        + back_scratch(rows, heads, width, step_keys),
        time=14,
    )


def ordered_pieces(pieces, me):
    odd = (me & 1) == 1
    high = (me & 2) == 2
    low_pair = [jnp.where(odd, pieces[1 - i], pieces[i]) for i in range(2)]
    high_pair = [jnp.where(odd, pieces[3 - i], pieces[2 + i]) for i in range(2)]
    ordered = [jnp.where(high, high_pair[i], low_pair[i]) for i in range(2)]
    return ordered + [jnp.where(high, low_pair[i], high_pair[i]) for i in range(2)]


def join_pieces(pieces, me, axis):
    return jnp.concatenate(ordered_pieces(pieces, me), axis=axis)


def received(own, near, far, me):
    rows = own.shape[0]
    return join_pieces([own[...], near[0:rows, :], far[0:rows, :], near[rows:, :]], me, 1)


def send_pieces(tensor, me, first, second, rest):
    width = tensor.shape[1] // 4
    rows = tensor.shape[0]
    pieces = ordered_pieces([tensor[:, k * width : (k + 1) * width] for k in range(4)], me)
    first[...] = pieces[0]
    second[...] = pieces[1]
    rest[0:rows, :] = pieces[2]
    rest[rows:, :] = pieces[3]


def half_product(tensor, own, other, me, first):
    span = slice(first, first + own.shape[0] // 2)
    left, right = dot_nn(tensor, own[:, span]), dot_nn(tensor, other[:, span])
    odd = (me & 1) == 1
    return jnp.concatenate([jnp.where(odd, right, left), jnp.where(odd, left, right)], axis=1)


def two_halves(tensor, me):
    half = tensor.shape[1] // 2
    odd = (me & 1) == 1
    left, right = tensor[:, 0:half], tensor[:, half:]
    return jnp.where(odd, right, left), jnp.where(odd, left, right)


def half_back(mine, others, own, other, first):
    span = slice(first, first + own.shape[0] // 2)
    return dot_nt(mine, own[:, span]) + dot_nt(others, other[:, span])


def normal_parts(tensor):
    average = jnp.mean(tensor, axis=-1, keepdims=True)
    centered = tensor - average
    scale = lax.rsqrt(jnp.mean(centered * centered, axis=-1, keepdims=True) + 1e-05)
    return centered * scale, scale


def normal_back(plain, scale, grad):
    inner = jnp.mean(grad * plain, axis=-1, keepdims=True)
    return scale * (grad - jnp.mean(grad, axis=-1, keepdims=True) - plain * inner)


def gelu_parts(pre):
    size = jnp.abs(pre)
    t = 1.0 / (1.0 + (0.3275911 * 0.7071067811865476) * size)
    poly = ((((1.061405429 * t - 1.453152027) * t + 1.421413741) * t - 0.284496736) * t + 0.254829592) * t
    bell = jnp.exp(-0.5 * pre * pre)
    tail = 0.5 * poly * bell
    cdf = jnp.where(pre < 0.0, tail, 1.0 - tail)
    return pre * cdf, cdf + pre * bell * 0.3989422804014327


def place_kernel(group, at, lengths, ids, *outs):
    seq, me = at[0], at[1]
    before = jnp.maximum(seq - 1, 0)
    for i, out in enumerate(outs):
        out[0] = me
        out[2] = lengths[i, before]
        out[3] = lengths[i, seq]
        for slot, block, number in ((1, seq, seq), (4, before, seq - 1)):
            rows = group // 128
            part = ids[i, pl.ds(pl.multiple_of(block * rows, rows), rows), :]
            out[slot] = jnp.sum(jnp.where(part < number, 1.0, 0.0)).astype(jnp.int32)
        for slot in (5, 6, 7):
            out[slot] = 0


def norm_kernel(at, x, low):
    rows = 256
    for start in range(0, low.shape[0], rows):
        span = slice(start, min(start + rows, low.shape[0]))
        low[span, :] = normal_parts(x[span, :].astype(F32))[0].astype(BF)


def lay_four(out, own, near, far, last):
    rows = own.shape[0]
    for k, ref in enumerate((own, near, far, last)):
        out[k * rows : (k + 1) * rows, :] = ref[...]


def qkv_kernel(i, rows, at, *refs):
    weight, qkv, kvp = refs[8:]
    width = weight.shape[1] // 3
    own = slice(i * rows, (i + 1) * rows)
    for k in range(4):
        block = slice(k * rows, (k + 1) * rows)
        qkv[block, :] = dot_nn(refs[k][own, :], weight[...]).astype(BF)
        kvp[block, :] = dot_nn(refs[4 + k][own, :], weight[:, width:]).astype(BF)


def memory_kernel(size, at, *refs):
    weight, outs = refs[8], refs[9:]
    count = len(outs) // 2
    rows, keys = outs[:count], outs[count:]
    for i in range(count):
        span = slice((i % (count // 2)) * size, (i % (count // 2) + 1) * size)
        pieces = refs[0:4] if i < count // 2 else refs[4:8]
        block = jnp.concatenate([ref[span, :] for ref in pieces], axis=0)
        rows[i][...] = block
        keys[i][...] = dot_nn(block, weight[...]).astype(BF)


def hidden_kernel(rows, at, whole, inner, outer):
    slot = 2 * rows
    for i in range(inner.shape[0] // rows):
        inner[i * rows : (i + 1) * rows, :] = whole[i * slot : i * slot + rows, :]
        outer[i * rows : (i + 1) * rows, :] = whole[i * slot + rows : i * slot + 2 * rows, :]


def hidden_grads_kernel(rows, at, pre_low, low, act, top, *refs):
    before, out = (refs[0], refs[1]) if len(refs) == 2 else (None, refs[0])
    step, slot = 256, 2 * rows
    for i in range(pre_low.shape[1] // step):
        for k, (left, right) in enumerate(((pre_low, low), (act, top))):
            grad = dot_tn(left[:, i * step : (i + 1) * step], right[...])
            for part in range(step // rows):
                start = (i * step // rows + part) * slot + k * rows
                block = grad[part * rows : (part + 1) * rows]
                if before is not None:
                    block = block + before[start : start + rows, :].astype(F32)
                out[start : start + rows, :] = block.astype(BF)


def near_kernel(at, keep, received, near, far):
    rows = near.shape[0]
    near[...] = keep[0:rows, :].astype(F32) + received[0:rows, :].astype(F32)
    far[...] = (keep[rows:, :].astype(F32) + received[rows:, :].astype(F32)).astype(BF)


def tree_kernel(at, keep, received, kept, sent):
    rows = kept.shape[0]
    kept[...] = keep[0:rows, :] + received[0:rows, :].astype(F32)
    sent[...] = (keep[rows:, :] + received[rows:, :].astype(F32)).astype(BF)


def output_kernel(at, after, near, far, out):
    out[...] = (after[...] + near[...] + far[...].astype(F32)).astype(BF)


def grad_x_kernel(i, at, x, before, near, far, back, out):
    rows = out.shape[0]
    plain, scale = normal_parts(x[i * rows : (i + 1) * rows, :].astype(F32))
    grad = near[...] + far[...].astype(F32) + back[...].astype(F32)
    out[...] = before[...] + normal_back(plain, scale, grad)


def far_sum_kernel(at, near, far, out):
    out[...] = (near[...] + far[...].astype(F32)).astype(BF)


def memory_back_kernel(at, own_a, own_b, prev_a, prev_b, rows_a, rows_b, rows_prev_a, rows_prev_b, weight,
                       grad, keep, send):
    rows = own_a.shape[0] // 4
    total = None
    grads, places = (own_a, own_b, prev_a, prev_b), (rows_a, rows_b, rows_prev_a, rows_prev_b)
    for k, (part, memory) in enumerate(zip(grads, places)):
        term = dot_tn(memory[...], part[...])
        total = term if total is None else total + term
        part = dot_nt(part[...], weight[...]).astype(BF)
        for slot, out, place in ((0, keep, 0), (1, send, 0), (2, keep, 4), (3, send, 4)):
            out[(place + k) * rows : (place + k + 1) * rows, :] = part[slot * rows : (slot + 1) * rows]
    grad[...] = total


def self_out_kernel(i, at, own, near, far, x, wide_own, wide_other,
                    low, after, plain, low_next, scale, first, second, rest):
    me = at[0]
    joined = received(own, near, far, me)
    low[...] = joined
    rows = low.shape[0]
    total = x[i * rows : (i + 1) * rows, :].astype(F32) + half_product(joined, wide_own, wide_other, me, 0)
    after[...] = total
    normed, scaled = normal_parts(total)
    plain[...] = normed
    scale[...] = scaled
    rounded = normed.astype(BF)
    low_next[...] = rounded
    send_pieces(half_product(rounded, wide_own, wide_other, me, wide_own.shape[0] // 2).astype(BF), me, first, second, rest)


def cross_out_kernel(at, own, near, far, before, out_own, out_other, gain, low, after, plain, scale, low_next):
    me = at[0]
    joined = received(own, near, far, me)
    low[...] = joined
    total = before[...] + half_product(joined, out_own, out_other, me, 0)
    after[...] = total
    normed, scaled = normal_parts(total)
    plain[...] = normed
    scale[...] = scaled
    low_next[...] = (normed * gain[...]).astype(BF)


def mlp_kernel(i, at, low, near_low, far_low, last_low, top, near_top, far_top, last_top, inner, outer,
               low_all, top_all, act, pre_low, grad_keep, grad_send, out_keep, out_send):
    rows = low.shape[0]
    lay_four(low_all, low, near_low, far_low, last_low)
    lay_four(top_all, *(ref.at[i * rows : (i + 1) * rows, :] for ref in (top, near_top, far_top, last_top)))
    for parity, grad, out in ((1, grad_send, out_send), (0, grad_keep, out_keep)):

        @pl.loop(0, 2)
        def _(b):
            block = pl.ds(pl.multiple_of((2 * b + parity) * rows, rows), rows)
            place = pl.ds(pl.multiple_of(b * rows, rows), rows)
            value, slope = gelu_parts(dot_nt(low_all[block, :], inner[...]))
            act_block = value.astype(BF)
            act[block, :] = act_block
            pre_block = (dot_nt(top_all[block, :], outer[...]) * slope).astype(BF)
            pre_low[block, :] = pre_block
            grad[place, :] = dot_nn(pre_block, inner[...]).astype(BF)
            out[place, :] = dot_nn(act_block, outer[...]).astype(BF)


def cross_back_kernel(i, at, near, far, plain, scale, gain, top, out_own, out_other,
                      grad_after, branch_own, branch_other, grad_gain, first, second, rest):
    me = at[0]
    grad = near[...] + far[...].astype(F32)
    normed = plain[...]
    grad_gain[...] = jnp.sum(grad * normed, axis=0, keepdims=True)
    rows = near.shape[0]
    total = top[i * rows : (i + 1) * rows, :].astype(F32) + normal_back(normed, scale[...], grad * gain[...])
    grad_after[...] = total
    mine, others = two_halves(total.astype(BF), me)
    branch_own[...] = mine
    branch_other[...] = others
    send_pieces(half_back(mine, others, out_own, out_other, 0).astype(BF), me, first, second, rest)


def self_back_kernel(at, own, near, far, plain, scale, before, wide_own, wide_other,
                     grad_after, query_mine, query_others, branch_own, branch_other, first, second, rest):
    me = at[0]
    mine, others = two_halves(received(own, near, far, me), me)
    query_mine[...] = mine
    query_others[...] = others
    total = before[...] + normal_back(plain[...], scale[...], half_back(mine, others, wide_own, wide_other, wide_own.shape[0] // 2))
    grad_after[...] = total
    mine, others = two_halves(total.astype(BF), me)
    branch_own[...] = mine
    branch_other[...] = others
    send_pieces(half_back(mine, others, wide_own, wide_other, 0).astype(BF), me, first, second, rest)


def half_grads_kernel(names, at, *refs):
    own, other = refs[-2:]
    half = own.shape[1] // names
    for n in range(names):
        parts = [ref[...] for ref in refs[6 * n : 6 * n + 6]]
        low, mine, others = (jnp.concatenate(parts[k : k + 2], axis=0) for k in (0, 2, 4))
        span = slice(n * half, (n + 1) * half)
        other[:, span] = dot_tn(low, others).astype(BF)
        own[:, span] = dot_tn(low, mine)


def qkv_back_kernel(at, dq, dkv, dkv_prev, weight, keep, send, keep_prev, send_prev):
    rows = dq.shape[0] // 4
    width = dq.shape[1]
    for parity, out, out_prev in ((1, send, send_prev), (0, keep, keep_prev)):
        for b in range(2):
            block = slice((2 * b + parity) * rows, (2 * b + parity + 1) * rows)
            place = slice(b * rows, (b + 1) * rows)
            grad = dot_nt(dq[block, :], weight[:, 0:width]) + dot_nt(dkv[block, :], weight[:, width:])
            out[place, :] = grad.astype(BF)
            out_prev[place, :] = dot_nt(dkv_prev[block, :], weight[:, width:]).astype(BF)


def lay_own(i, refs, low_all, before_all):
    rows = low_all.shape[0] // 4
    own = slice(i * rows, (i + 1) * rows)
    for out, pieces in ((low_all, refs[0:4]), (before_all, refs[4:8])):
        for k, ref in enumerate(pieces):
            out[k * rows : (k + 1) * rows, :] = ref[own, :]


def qkv_grads_kernel(i, at, *refs):
    dq, dkv, dkv_prev, out, low, before, own = refs[8:]
    width = dq.shape[1]
    lay_own(i, refs, low, before)
    out[:, 0:width] = dot_tn(low[...], dq[...])
    own[...] = dot_tn(low[...], dkv[...])
    out[:, width:] = own[...] + dot_tn(before[...], dkv_prev[...])


def last_qkv_grads_kernel(i, offsets, at, *refs):
    dq, dkv, dkv_prev, earlier, keep, send, low, before, total = refs[8:]
    width = dq.shape[1]
    lay_own(i, refs, low, before)
    total[:, 0:width] = earlier[:, 0:width] + dot_tn(low[...], dq[...])
    total[:, width:] = earlier[:, width:] + dot_tn(low[...], dkv[...])
    total[:, width:] += dot_tn(before[...], dkv_prev[...])
    half = len(offsets) // 2
    rows = total.shape[0] // len(offsets)
    for n, offset in enumerate(offsets):
        out = keep if n < half else send
        start = pl.multiple_of((at[0] ^ offset) * rows, rows)
        out[(n % half) * rows : (n % half + 1) * rows, :] = total[pl.ds(start, rows), :].astype(out.dtype)


def shape(rows, columns, dtype=BF):
    return jax.ShapeDtypeStruct((rows, columns), dtype)


D = 1024
MICRO = 2


def flip(block, axis, bit):
    return lax.ppermute(block, axis, [(i, i ^ bit) for i in range(lax.axis_size(axis))])


def shifted(block, distance):
    devices = range(lax.axis_size("seq"))
    route = [(i - distance, i) for i in devices if i - distance in devices]
    return lax.ppermute(block, "seq", route)


def far_slots(part):
    rows = part.shape[0] // 4
    return part[:rows], part[rows : 2 * rows], flip(part[2 * rows :], "mem", 2)


def near_slots(own, side, far):
    rows = own.shape[0]
    return own, flip(jnp.concatenate([side, far[rows:]], axis=0), "mem", 1), far


def near_sum(place, keep, send):
    rows, columns = keep.shape
    outs = [shape(rows // 2, columns, F32), shape(rows // 2, columns)]
    return call(near_kernel, place, (keep, flip(send, "mem", 1)), outs, time=1)


def seq_bits():
    count = lax.axis_size("seq")
    return [1 << i for i in reversed(range(count.bit_length() - 1))]


def seq_offsets(bits):
    offsets = [0]
    for bit in bits:
        offsets = offsets + [o ^ bit for o in offsets]
    return offsets


def seq_stage(block, bit):
    return jnp.concatenate([block, flip(block, "seq", bit)], axis=0)


def assemble_kernel(rows, offsets, at, first, second, *outs):
    half = len(offsets) // 2
    for i, offset in enumerate(offsets):
        ref = first if i < half else second
        start = pl.multiple_of((at[0] ^ offset) * rows, rows)
        column = 0
        for out in outs:
            columns = out.shape[1]
            place = slice((i % half) * rows, (i % half + 1) * rows)
            out[pl.ds(start, rows), :] = ref[place, column : column + columns]
            column += columns


def assemble(first, second, seq, bits, split):
    offsets = seq_offsets(bits)
    size = 2 * first.shape[0]
    outs = [shape(size, columns) for columns in split]
    return call(functools.partial(assemble_kernel, size // len(offsets), offsets), seq.reshape(1), (first, second), outs)


def reorder_kernel(rows, offsets, groups, at, *refs):
    keep, send = refs[-2:]
    half = len(offsets) // 2
    for i, offset in enumerate(offsets):
        start = pl.multiple_of((at[0] ^ offset) * rows, rows)
        out = keep if i < half else send
        place = slice((i % half) * rows, (i % half + 1) * rows)
        for column, terms in groups:
            total = None
            for term, first, columns in terms:
                part = refs[term][pl.ds(start, rows), first : first + columns].astype(F32)
                total = part if total is None else total + part
            out[place, column : column + columns] = total.astype(out.dtype)


def reorder(arrays, groups, seq, bits):
    offsets = seq_offsets(bits)
    size = arrays[0].shape[0]
    placed, column = [], 0
    for terms in groups:
        placed.append((column, terms))
        column += terms[0][2]
    kernel = functools.partial(reorder_kernel, size // len(offsets), offsets, placed)
    return call(kernel, seq.reshape(1), arrays, [shape(size // 2, column, F32), shape(size // 2, column)], time=column // 300)


def pack_kernel(width, half, at, *refs):
    me = at[0]
    (gain_self, gain_cross, gain_mlp), weights, (kept, message) = refs[:3], refs[3:11], refs[11:]
    query, key, value, out_w, cross_q, cross_k, cross_v, cross_o = weights

    def scaled(weight, gain):
        return (weight.astype(F32) * gain[...].astype(F32)).astype(BF)

    def piece(k):
        at_k = pl.ds(pl.multiple_of((me ^ k) * width, width), width)
        gained = [scaled(w[:, at_k], gain_self) for w in (query, key, value)]
        return jnp.concatenate(gained + [w[:, at_k] for w in (cross_k, cross_v)], axis=1)

    def side(k):
        at_k = pl.ds(pl.multiple_of(((me & 1) ^ k) * half, half), half)
        rows = gain_mlp.shape[0]
        lanes = lax.broadcasted_iota(jnp.int32, (rows, 128), 1)
        extra = jnp.where(lanes == 0, gain_mlp[...].astype(F32), 0.0).astype(BF)
        return jnp.concatenate([out_w[:, at_k], scaled(cross_q[:, at_k], gain_cross), cross_o[:, at_k], extra], axis=1)

    kept[...] = jnp.concatenate([piece(0), piece(1)], axis=1)
    message[...] = jnp.concatenate([piece(2), piece(3), side(0), side(1)], axis=1)


def repack_kernel(narrow, broad, at, kept, message, far, out):
    sides = 2 * narrow + broad
    out[:, 0:narrow] = kept[:, narrow:]
    out[:, narrow : 2 * narrow] = far[:, narrow : 2 * narrow]
    out[:, 2 * narrow : 2 * narrow + broad] = message[:, sides:]
    out[:, 2 * narrow + broad :] = far[:, sides:]


def unpack_kernel(width, narrow, broad, at, kept, message, far, near, qkv, first):
    me = at[0]
    start = 2 * narrow
    heads = [kept[:, 0:narrow], near[:, 0:narrow], far[:, 0:narrow], near[:, narrow:start]]
    sides = [message, near, far, near]
    sides = [ref[:, at_k : at_k + broad] for ref, at_k in zip(sides, (start, start, start, start + broad))]
    heads = join_pieces(heads, me, 0)
    sides = join_pieces(sides, me, 0)
    qkv[...] = heads[:, 0 : 3 * width]
    pair = broad - 128 - (broad - 128) // 3
    first[...] = jnp.concatenate([sides[:, 0:pair], heads[:, 3 * width :], sides[:, pair:]], axis=1)


class Stay:
    def __init__(self, value):
        self.value = value


def interleave(streams, sides):
    held = [next(s) for s in streams]
    results = [None] * len(streams)
    waiting = [(side, *next(side)) for side in sides]
    turn = 0
    ticks = 0

    def serve(arrays):
        nonlocal ticks, waiting
        ticks += 1
        due = [w for w in waiting if w[1] == ticks]
        waiting = [w for w in waiting if w[1] != ticks]
        arrays, taken = lax.optimization_barrier((arrays, [w[2]() for w in due]))
        for (side, _, _), got in zip(due, taken):
            try:
                waiting.append((side, *side.send(got)))
            except StopIteration:
                pass
        return arrays

    while True:
        other = (turn + 1) % len(streams)
        try:
            mark = streams[turn].send(held[turn])
            while isinstance(mark, Stay):
                mark = streams[turn].send(serve(mark.value))
            if results[other] is None:
                held[other], mark = serve((held[other], mark))
            else:
                mark = serve(mark)
            held[turn] = streams[turn].send(mark)
        except StopIteration as end:
            results[turn] = end.value
        if results[other] is None:
            turn = other
        elif results[turn] is not None:
            assert not waiting
            return results


def shards(
    inputs,
    memory,
    page_ids,
    memory_length,
    cotangent,
    gain_self,
    self_query,
    self_key,
    self_value,
    self_out,
    gain_cross,
    cross_query,
    cross_key,
    cross_value,
    cross_out,
    gain_mlp,
    mlp_in,
    mlp_out,
):
    seq = lax.axis_index("seq")
    me = lax.axis_index("mem")
    odd = me & 1
    blocks = lax.axis_size("mem")
    tok = inputs.shape[1]
    group = tok * blocks
    real = memory.shape[2]
    padded = -(-real // 16) * 16
    wrows = self_query.shape[0]
    bits = seq_bits()
    turned = bits[:-2] + [bits[-1], bits[-2]]
    half = D // 2

    def join_halves(own, other):
        return jnp.concatenate([jnp.where(odd == 0, own, other), jnp.where(odd == 0, other, own)], axis=1)

    width = self_query.shape[1] // blocks
    narrow, broad = 5 * width, 3 * half + 128
    place = me.reshape(1)
    weights = (self_query, self_key, self_value, self_out, cross_query, cross_key, cross_value, cross_out)
    gains = [g[:, None] for g in (gain_self, gain_cross, gain_mlp)]
    kept, message = call(
        functools.partial(pack_kernel, width, half), place, (*gains, *weights),
        [shape(wrows, 2 * narrow), shape(wrows, 2 * (narrow + broad))],
    )
    far = flip(message, "mem", 2)
    x_rows, tops = inputs.reshape(MICRO * tok, D), cotangent.reshape(MICRO * tok, D)
    lows = call(norm_kernel, place, (x_rows,), shape(MICRO * tok, D))
    befores = shifted(lows, 1)
    far_lows, near_lows = flip(lows, "mem", 2), flip(lows, "mem", 1)
    smem = pl.BlockSpec(memory_space=pltpu.SMEM)
    ids = page_ids.reshape(MICRO, -1, 128)
    places = pl.pallas_call(
        functools.partial(place_kernel, group),
        out_shape=[jax.ShapeDtypeStruct((8,), jnp.int32)] * MICRO,
        in_specs=[smem, smem, pl.BlockSpec(memory_space=pltpu.VMEM)],
        out_specs=[smem] * MICRO,
    )(jnp.stack([seq, me]), memory_length, ids)
    near = call(
        functools.partial(repack_kernel, narrow, broad), place, (kept, message, far),
        shape(*message.shape),
    )
    near = flip(near, "mem", 1)
    qkv_part, first_part = call(
        functools.partial(unpack_kernel, width, narrow, broad), place, (kept, message, far, near),
        [shape(blocks * wrows, columns) for columns in (3 * width, 3 * half + 128 + 2 * width)],
    )

    state = {}
    hidden = mlp_in.shape[0]
    stage = seq_stage(qkv_part, bits[0])
    stage, first_part, befores, memory_here = lax.optimization_barrier((stage, first_part, befores, memory))
    far_befores, near_befores = flip(befores, "mem", 2), flip(befores, "mem", 1)
    first_stage = first_part
    for bit in bits[:-3]:
        first_stage = seq_stage(first_stage, bit)
    first_pair = first_stage, flip(first_stage, "seq", bits[-3])
    memory_own = jnp.pad(memory_here.reshape(MICRO, real, D), ((0, 0), (0, padded - real), (0, 0)))
    memory_own = memory_own.reshape(MICRO * padded, D)
    hidden_part = jnp.concatenate([mlp_in, mlp_out], axis=0)
    for bit in bits[1:-1]:
        stage = seq_stage(stage, bit)
    stage, far_lows, memory_own, hidden_part, places = lax.optimization_barrier(
        (stage, far_lows, memory_own, hidden_part, places)
    )
    last_lows = flip(far_lows, "mem", 1)
    last_stage, first_pair, far_befores, memory_own, tops = lax.optimization_barrier(
        (flip(stage, "seq", bits[-1]), first_pair, far_befores, memory_own, tops)
    )
    first_stage = seq_stage(jnp.concatenate(first_pair, axis=0), bits[-2])
    memory_before = shifted(memory_own, 1)
    memory_far = flip(memory_own, "mem", 2)
    far_tops, near_tops = flip(tops, "mem", 2), flip(tops, "mem", 1)
    (qkv_full,) = assemble(stage, last_stage, seq, bits, [3 * width])
    gathered = [lows, near_lows, far_lows, last_lows, befores, near_befores, far_befores, flip(far_befores, "mem", 1)]

    def first_side():
        (first,) = yield 2, lambda: (first_stage,)
        cut = 2 * half + 2 * width
        first, last = first[:, :cut], first[:, cut:]
        first = first, flip(first, "seq", bits[-1])
        *first, last = yield 3, lambda: (*first, last)
        state["wide_own"], state["ckv"] = assemble(*first, seq, bits, [2 * half, 2 * width])
        state["wide_other"] = flip(state["wide_own"], "mem", 1)
        last = last, flip(last, "seq", bits[-1])
        last = yield 6, lambda: last
        state["cout_own"], gain = assemble(*last, seq, bits, [half, 128])
        state["gain"] = gain[:, 0].astype(F32)[None, :]
        state["cout_other"] = flip(state["cout_own"], "mem", 1)

    def memory_side():
        before, near_own, far_own = yield 3, lambda: (memory_before, flip(memory_own, "mem", 1), memory_far)
        far_prev, near_prev = flip(before, "mem", 2), flip(before, "mem", 1)
        last_own = flip(far_own, "mem", 1)
        *gone, far_prev = yield 5, lambda: (before, near_own, far_own, last_own, near_prev, far_prev)
        before, near_own, far_own, last_own, near_prev = gone
        last_prev = flip(far_prev, "mem", 1)
        pieces = memory_own, near_own, far_own, last_own, before, near_prev, far_prev, last_prev
        whole = blocks * padded
        outs = [shape(whole, D)] * (2 * MICRO) + [shape(whole, 2 * width)] * (2 * MICRO)
        got = call(functools.partial(memory_kernel, padded), place, (*pieces, state["ckv"]), outs, time=6)
        state["rows"], state["rows_prev"], state["mem_kv"], state["mem_prev"] = (
            got[k * MICRO : (k + 1) * MICRO] for k in range(4)
        )

    def top_side():
        far, near = yield 2, lambda: (far_tops, near_tops)
        state["top"] = tops, near, far, flip(far, "mem", 1)

    def hidden_side():
        (part,) = yield 2, lambda: (hidden_part,)
        whole = lax.all_gather(part, "seq", axis=0, tiled=True)
        (whole,) = yield 8, lambda: (whole,)
        both = [shape(whole.shape[0] // 2, D)] * 2
        both = call(functools.partial(hidden_kernel, hidden), place, (whole,), both)
        state["inner"], state["outer"] = yield 9, lambda: both
        kernel = functools.partial(hidden_grads_kernel, hidden)
        arrays = yield 11, lambda: state["grad_hidden"][0]
        grads = call(kernel, place, arrays, shape(2 * D, D), time=9)
        arrays = yield 12, lambda: (*state["grad_hidden"][1], grads)
        grads = call(kernel, place, arrays, shape(2 * D, D), time=9)
        (grads,) = yield 13, lambda: (grads,)
        grads = lax.psum_scatter(grads, "seq", scatter_dimension=0, tiled=True)
        (grads,) = yield 19, lambda: (grads,)
        state["hidden_grads"] = grads[:hidden].astype(F32), grads[hidden:].astype(F32)

    order = turned[::-1]

    def seq_next(kept, received, bit):
        rows, columns = kept.shape[0] // 2, kept.shape[1]
        kept, sent = call(tree_kernel, place, (kept, received), [shape(rows, columns, F32), shape(rows, columns)])
        return kept, flip(sent, "seq", bit)

    def half_grads(names):
        arrays = [part for low, mine, others in names for part in (*low, *mine, *others)]
        outs = [shape(D, len(names) * half, F32), shape(D, len(names) * half)]
        return call(functools.partial(half_grads_kernel, len(names)), place, arrays, outs, time=2 * len(names))

    def tree_side(name, arrays, groups, ticks):
        arrays = yield ticks[0], lambda: arrays
        kept, sent = reorder(arrays, groups, seq, turned)
        pair = kept, flip(sent, "seq", order[0])
        for bit, tick in zip(order[1:], ticks[1:]):
            pair = yield tick, lambda: pair
            pair = seq_next(*pair, bit)
        state[name] = pair

    def cout_side():
        names, gains = yield 15, lambda: (state["grad_cout"], state["grad_gain_three"])
        own, other = half_grads([list(zip(*names))])
        gains = jnp.pad((gains[0] + gains[1]).reshape(D, 1), ((0, 0), (0, 127)))
        groups = [[(0, 0, half), (1, 0, half)], [(2, 0, 128)]]
        yield from tree_side("cout", (own, flip(other, "mem", 1), gains), groups, (16, 20))

    def wide_side():
        out, query, dmem = yield 17, lambda: (state["grad_out"], state["grad_cquery"], state["dmem"])
        own, other = half_grads([list(zip(*out)), list(zip(*query))])
        other = flip(other, "mem", 1)
        mem_rows = shape(8 * padded, D)
        arrays = (*(part for pair in zip(*dmem) for part in pair), *state["rows"], *state["rows_prev"], state["ckv"])
        ckv, mem_keep, mem_send = call(
            memory_back_kernel, place, arrays, [shape(D, 2 * width, F32), mem_rows, mem_rows], time=10
        )
        state["memory_parts"] = mem_keep, flip(mem_send, "mem", 1)
        groups = [[(0, 0, 2 * half), (1, 0, 2 * half)], [(2, 0, 2 * width)]]
        yield from tree_side("wide", (own, other, ckv), groups, (18, 19, 20))

    def memory_grads_side():
        parts = yield 18, lambda: state["memory_parts"]
        rows = 4 * padded
        near, far = call(near_kernel, place, parts, [shape(rows, D, F32), shape(rows, D)], time=1)
        near, far = yield 20, lambda: (near, far)
        state["memory_sums"] = near, flip(far, "mem", 2)

    for name in ("hidden", "gain_three", "cout", "out", "cquery", "qkv"):
        state["grad_" + name] = []
    state["dmem"] = []
    quarter = [shape(tok, width), shape(tok, width), shape(2 * tok, width)]
    rounded, exact, column = shape(tok, D), shape(tok, D, F32), shape(tok, 1, F32)
    half_rows, whole, pair_rows = shape(tok, half), shape(group, D), shape(2 * tok, D)

    def far_pieces(pieces):
        return pieces[0], pieces[1], flip(pieces[2], "mem", 2)

    def stream(i):
        at = places[i]
        pieces = yield gathered
        qkv, kv_prev = call(
            functools.partial(qkv_kernel, i, tok), place, (*pieces, qkv_full),
            [shape(group, 3 * width), shape(group, 2 * width)], time=5,
        )
        if i == 0:
            qkv, kv_prev = yield Stay((qkv, kv_prev))
        self_o, self_lse = self_forward(at, qkv, kv_prev, blocks)
        self_lse = yield self_lse

        pieces = yield far_slots(self_o)
        self_low, after_self, plain_two, low_two, scale_two, *pieces = call(
            functools.partial(self_out_kernel, i), place,
            (*near_slots(*pieces), x_rows, state["wide_own"], state["wide_other"]),
            [rounded, exact, exact, rounded, column, *quarter], time=4,
        )
        scale_two = yield scale_two

        pieces = yield far_pieces(pieces)
        mem_kv, mem_prev = state["mem_kv"][i], state["mem_prev"][i]
        cross_o, cross_lse, cross_q = cross_forward(at, near_slots(*pieces), mem_prev, mem_kv, blocks, real)
        cross_lse = yield cross_lse

        pieces = yield far_slots(cross_o)
        cross_low, after_cross, plain_three, scale_three, low_three = call(
            cross_out_kernel, place,
            (*near_slots(*pieces), after_self, state["cout_own"], state["cout_other"], state["gain"]),
            [rounded, exact, exact, column, rounded], time=3,
        )
        scale_three = yield scale_three

        low_three, near, far = yield low_three, flip(low_three, "mem", 1), flip(low_three, "mem", 2)
        low_all, top_all, act, pre_low, grad_keep, grad_send, out_keep, out_send = call(
            functools.partial(mlp_kernel, i), place,
            (low_three, near, far, flip(far, "mem", 1), *state["top"], state["inner"], state["outer"]),
            [whole, whole, whole, whole, pair_rows, pair_rows, pair_rows, pair_rows], time=15,
        )
        state["grad_hidden"].append((pre_low, low_all, act, top_all))
        grad_keep, grad_send = yield grad_keep, grad_send

        near, far = near_sum(place, grad_keep, grad_send)
        far, out_send = yield flip(far, "mem", 2), out_send
        grad_after_cross, mine, others, gain_three, *pieces = call(
            functools.partial(cross_back_kernel, i), place,
            (near, far, plain_three, scale_three, state["gain"], tops, state["cout_own"], state["cout_other"]),
            [exact, half_rows, half_rows, shape(1, D, F32), *quarter], time=3,
        )
        state["grad_gain_three"].append(gain_three)
        state["grad_cout"].append((cross_low, mine, others))
        grad_after_cross = yield grad_after_cross

        pieces, out_send = yield far_pieces(pieces), out_send
        dcq, dmem_prev, dmem = cross_backward(
            at, cross_q, mem_prev, mem_kv, cross_o, near_slots(*pieces), cross_lse, blocks, real
        )
        out_near, out_far = near_sum(place, out_keep, out_send)
        dmem = yield dmem

        pieces, out_far = yield far_slots(dcq), out_far
        out_far = flip(out_far, "mem", 2)
        grad_after_self, query_mine, query_others, mine, others, *pieces = call(
            self_back_kernel, place,
            (*near_slots(*pieces), plain_two, scale_two, grad_after_cross, state["wide_own"], state["wide_other"]),
            [exact, half_rows, half_rows, half_rows, half_rows, *quarter], time=4,
        )
        state["grad_cquery"].append((low_two, query_mine, query_others))
        state["grad_out"].append((self_low, mine, others))
        state["dmem"].append((dmem, dmem_prev))
        grad_after_self = yield grad_after_self

        pieces, out_far = yield far_pieces(pieces), out_far
        pieces = near_slots(*pieces)
        if i == 0:
            pieces = yield Stay(pieces)
        dq, dkv, dkv_prev = self_backward(at, qkv, kv_prev, self_o, pieces, self_lse, blocks)
        grads = (*gathered, dq, dkv, dkv_prev)
        lows_scratch = [pltpu.VMEM((group, D), BF)] * 2
        if i == 0:
            grads = call(
                functools.partial(qkv_grads_kernel, i), place, grads, shape(D, 3 * width, F32),
                [*lows_scratch, pltpu.VMEM((D, 2 * width), F32)], time=6,
            )
            state["grad_qkv"].append(grads)
        else:
            grads = call(
                functools.partial(last_qkv_grads_kernel, i, seq_offsets(turned)), seq.reshape(1),
                (*grads, state["grad_qkv"][0]), [shape(D // 2, 3 * width, F32), shape(D // 2, 3 * width)],
                [*lows_scratch, pltpu.VMEM((D, 3 * width), F32)], time=7,
            )
        output = call(output_kernel, place, (after_cross, out_near, out_far), rounded)
        if i < MICRO - 1:
            back = call(qkv_back_kernel, place, (dq, dkv, dkv_prev, qkv_full), [pair_rows] * 4, time=5)
            back, state["grad_qkv"][0] = yield last_near(*back), grads
            back = yield last_far(*back)
        else:
            state["last_qkv"], dq, dkv, dkv_prev = yield grads, dq, dkv, dkv_prev
            back = call(qkv_back_kernel, place, (dq, dkv, dkv_prev, qkv_full), [pair_rows] * 4, time=5)
            yield ()
        return output, grad_after_self, back

    def last_near(keep, send, keep_prev, send_prev):
        return [near_sum(place, *pair) for pair in ((keep_prev, send_prev), (keep, send))]

    def last_far(*pairs):
        return [part for near, far in pairs for part in (near, flip(far, "mem", 2))]

    def back_rows(near_prev, far_prev, near, far):
        return shifted(call(far_sum_kernel, place, (near_prev, far_prev), rounded), -1)

    def final_rows(i, sums, back):
        grads = x_rows, done[i][1], sums[2], sums[3], back
        return call(functools.partial(grad_x_kernel, i), place, grads, exact)

    sides = [first_side(), memory_side(), top_side(), hidden_side(), cout_side(), wide_side(), memory_grads_side()]
    done = interleave([stream(i) for i in range(MICRO)], sides)

    def wide_finish(own):
        high = me >> 1
        rows_two = own.reshape(2, 2 * wrows, own.shape[1])
        theirs = lax.dynamic_index_in_dim(rows_two, 1 - high, 0, keepdims=False).astype(BF)
        own = lax.dynamic_index_in_dim(rows_two, high, 0, keepdims=False) + flip(theirs, "mem", 2).astype(F32)
        rows_two = own.reshape(2, wrows, own.shape[1])
        theirs = lax.dynamic_index_in_dim(rows_two, 1 - odd, 0, keepdims=False)
        own = lax.dynamic_index_in_dim(rows_two, odd, 0, keepdims=False)
        return own, flip(theirs.astype(BF), "mem", 1).astype(F32)

    def head_finish(summed, count):
        slots = summed.astype(BF).reshape(blocks, wrows, -1)
        first, second, *rest = [lax.dynamic_index_in_dim(slots, me ^ k, 0, keepdims=False) for k in range(4)]
        far = flip(jnp.concatenate(rest, axis=0), "mem", 2)
        own, near, far = near_slots(first, second, far)
        whole = join_pieces([own, near[:wrows], far[:wrows], near[wrows:]], me, 1).astype(F32)
        whole = whole.reshape(wrows, blocks, count, -1)
        return [whole[:, :, k].reshape(wrows, D) for k in range(count)]

    def seq_finish(pair, left):
        for bit in left:
            pair = seq_next(*pair, bit)
        return pair[0] + pair[1].astype(F32)

    tie = lax.optimization_barrier
    kept, sent = state["last_qkv"]
    qkv_pair = kept, flip(sent, "seq", order[0])
    sums = [done[0][2]]
    backs = [back_rows(*sums[0])]
    nears, memory_sums = tie((last_near(*done[1][2]), state["memory_sums"]))
    sums.append(last_far(*nears))
    qkv_pair, sums, backs, memory_sums, cout_pair = tie((qkv_pair, sums, backs, memory_sums, state["cout"]))
    qkv_pair = seq_next(*qkv_pair, order[1])
    backs.append(back_rows(*sums[1]))
    memory_near, memory_far = memory_sums
    both = call(far_sum_kernel, place, (memory_near, memory_far), shape(4 * padded, D))
    mem_own, mem_back = both[: 2 * padded], shifted(both[2 * padded :], -1)
    wide_pair, cout_pair = state["wide"], seq_next(*cout_pair, order[2])
    for bit in order[3:]:
        wide_pair, cout_pair = seq_next(*wide_pair, bit), seq_next(*cout_pair, bit)
    qkv_pair, wide_pair, cout_pair = tie((qkv_pair, wide_pair, cout_pair))
    qkv_pair = seq_next(*qkv_pair, order[2])
    for bit in order[3:]:
        qkv_pair = seq_next(*qkv_pair, bit)
    grad_rows = [final_rows(i, sums[i], backs[i]) for i in range(MICRO)]
    grad_mem = mem_own.reshape(MICRO, 1, padded, D).astype(F32) + mem_back.reshape(MICRO, 1, padded, D).astype(F32)
    grad_inner, grad_outer = state["hidden_grads"]
    own, near = wide_finish(seq_finish(cout_pair, []))
    grad_cout = join_halves(own[:, :half], near[:, :half])
    grad_gain_mlp = own[:, half] + near[:, half]
    last = seq_finish(wide_pair, [])
    grad_ckey, grad_cvalue = head_finish(last[:, 2 * half :], 2)
    own, near = wide_finish(last[:, : 2 * half])
    grad_out, plain_cquery = [
        join_halves(own[:, k * half : (k + 1) * half], near[:, k * half : (k + 1) * half]) for k in range(2)
    ]
    plain_qkv = head_finish(seq_finish(qkv_pair, []), 3)

    def gained(gain, weights, plains):
        scale = gain.astype(F32)[:, None]
        grad_gain = sum(jnp.sum(w.astype(F32) * p, axis=1) for w, p in zip(weights, plains))
        return grad_gain, [p * scale for p in plains]

    grad_gain_self, (grad_query, grad_key, grad_value) = gained(
        gain_self, (self_query, self_key, self_value), plain_qkv
    )
    grad_gain_cross, (grad_cquery,) = gained(gain_cross, (cross_query,), (plain_cquery,))
    return (
        jnp.stack([d[0] for d in done]),
        jnp.stack(grad_rows),
        grad_mem[:, :, :real],
        grad_gain_self,
        grad_query,
        grad_key,
        grad_value,
        grad_out,
        grad_gain_cross,
        grad_cquery,
        grad_ckey,
        grad_cvalue,
        grad_cout,
        grad_gain_mlp,
        grad_inner,
        grad_outer,
    )


def solution(mesh):
    rows = P(("seq", "mem"), None)
    tokens = P(None, ("seq", "mem"), None)
    pages = P(None, "seq", "mem", None)
    gains = P(("seq", "mem"))
    return jax.shard_map(
        shards,
        mesh=mesh,
        in_specs=(tokens, pages, P(), P(), tokens, gains, rows, rows, rows, rows, gains, rows, rows, rows, rows,
                  gains, rows, rows),
        out_specs=(tokens, tokens, pages, gains, rows, rows, rows, rows, gains, rows, rows, rows, rows, gains,
                   rows, rows),
        check_vma=False,
    )
```

```python
import functools
import math
import jax
import jax.numpy as jnp
import numpy as np
from jax import lax
from jax.experimental import pallas as pl
from jax.experimental.pallas import tpu as pltpu
from jax.sharding import PartitionSpec as P

HEAD = 64
BF = jnp.bfloat16
F32 = jnp.float32
LOWEST = -1e30


def head_lanes(rows, width):
    return lax.broadcasted_iota(jnp.int32, (rows, width), 1) // HEAD


def one_head(block, lanes, head):
    return jnp.where(lanes == head, block, jnp.zeros_like(block))


def dot_nt(left, right):
    return lax.dot_general(left, right, (((1,), (1,)), ((), ())), preferred_element_type=F32)


def dot_nn(left, right):
    return lax.dot_general(left, right, (((1,), (0,)), ((), ())), preferred_element_type=F32)


def dot_tn(left, right):
    return lax.dot_general(left, right, (((0,), (0,)), ((), ())), preferred_element_type=F32)


def self_range(p, rows, blocks, spill, prev_spill):
    first = jnp.where(p * rows < spill, prev_spill // rows, blocks + spill // rows)
    return first, blocks + p + 1


def self_allowed(query, key, extent, spill, prev_spill):
    first = jnp.where(query < spill, prev_spill, extent + spill)
    return (key >= first) & (key <= extent + query)


def cross_allowed(query, place, side, spill, length, me, padded, real):
    part = place // padded
    inner = place - part * padded
    row = (part ^ me) * real + inner
    return (inner < real) & (row < length) & ((query < spill) == (side == 0))


def fold(block, combine):
    total = block[0:8]
    for r in range(8, block.shape[0], 8):
        total = combine(total, block[r : r + 8])
    return total


def lay_heads(out, block, lanes, heads):
    rows = block.shape[0]
    for h in range(heads):
        out[h * rows : (h + 1) * rows, :] = one_head(block, lanes, h)


def score_block(kb, k, allowed, q_cat, s_scr, tops):
    rows = s_scr.shape[3]
    found = []
    for h, top in enumerate(tops):
        s = jnp.where(allowed, dot_nt(k, q_cat[h * rows : (h + 1) * rows, :]), LOWEST)
        s_scr[kb, h] = s
        found.append(jnp.maximum(top, fold(s, jnp.maximum)))
    return tuple(found)


def weigh_block(kb, tops, totals, s_scr, p_scr, v_cat):
    count = s_scr.shape[2]
    summed = []
    for h, (top, total) in enumerate(zip(tops, totals)):
        e = jnp.exp(s_scr[kb, h] - top)
        p_scr[h * count : (h + 1) * count, :] = e.astype(BF)
        summed.append(total + fold(e, jnp.add))
    return tuple(summed), dot_tn(p_scr[...], v_cat)


def attend(first, last, heads, scores, values, s_scr, p_scr, width):
    rows = s_scr.shape[3]
    lowest = jnp.full((8, rows), LOWEST, F32)
    tops = lax.fori_loop(first, last, scores, (lowest,) * heads)
    tops = tuple(jnp.max(top, axis=0, keepdims=True) for top in tops)

    def step(kb, carry):
        totals, acc = carry
        totals, more = weigh_block(kb, tops, totals, s_scr, p_scr, values(kb))
        return totals, acc + more

    start = (jnp.zeros((8, rows), F32),) * heads, jnp.zeros((rows, width), F32)
    totals, acc = lax.fori_loop(first, last, step, start)
    return tops, tuple(jnp.sum(total, axis=0, keepdims=True) for total in totals), acc


def finish(p, start, tops, totals, acc, lanes, o_ref, lse_ref):
    rows = acc.shape[0]
    heads = len(tops)
    inverse = jnp.concatenate([1.0 / total for total in totals] + [jnp.zeros((8 - heads, rows), F32)], axis=0).T
    spread_out = jnp.zeros(acc.shape, F32)
    for h in range(heads):
        spread_out = jnp.where(lanes == h, inverse[:, h : h + 1], spread_out)
    o_ref[pl.ds(start, rows), :] = (acc * spread_out).astype(BF)
    place = pl.ds(pl.multiple_of(p * rows, rows), rows)
    for h in range(heads):
        lse_ref[h : h + 1, place] = tops[h] + jnp.log(totals[h])


def self_forward_kernel(rows, blocks, heads, sc, qkv, kvp, o_ref, lse_ref, k_scr, v_scr, s_scr, q_cat, p_scr):
    width = heads * HEAD
    extent = rows * blocks
    me, spill, prev_spill = sc[0], sc[1], sc[4]
    lanes = head_lanes(rows, width)

    def place(b):
        return pl.multiple_of((b ^ me) * rows, rows)

    first_used, _ = self_range(0, rows, blocks, spill, prev_spill)

    @pl.loop(first_used, 2 * blocks)
    def _(kb):
        def fill(keys, values):
            k_scr[kb] = keys
            lay_heads(v_scr.at[kb], values, lanes, heads)

        @pl.when(kb < blocks)
        def _():
            at = pl.ds(place(kb), rows)
            fill(kvp[at, 0:width], kvp[at, width : 2 * width])

        @pl.when(kb >= blocks)
        def _():
            at = pl.ds(place(kb - blocks), rows)
            fill(qkv[at, width : 2 * width], qkv[at, 2 * width : 3 * width])

    @pl.loop(0, blocks)
    def _(p):
        lay_heads(q_cat, qkv[pl.ds(place(p), rows), 0:width] * jnp.asarray(0.125, BF), lanes, heads)
        first, last = self_range(p, rows, blocks, spill, prev_spill)
        query = p * rows + lax.broadcasted_iota(jnp.int32, (1, rows), 1)

        def scores(kb, tops):
            key = kb * rows + lax.broadcasted_iota(jnp.int32, (rows, rows), 0)
            return score_block(kb, k_scr[kb], self_allowed(query, key, extent, spill, prev_spill), q_cat, s_scr, tops)

        tops, totals, acc = attend(first, last, heads, scores, lambda kb: v_scr[kb], s_scr, p_scr, width)
        finish(p, place(p), tops, totals, acc, lanes, o_ref, lse_ref)


def lay(out, own, near, far):
    rows = own.shape[0]
    out[0:rows, :] = own[...]
    out[rows : 2 * rows, :] = near[0:rows, :]
    out[2 * rows : 3 * rows, :] = far[0:rows, :]
    out[3 * rows :, :] = near[rows:, :]


def cross_forward_kernel(rows, blocks, heads, padded, real, sc, own, near, far, kv0, kv1, o_ref, lse_ref, q_ref,
                         v_scr, s_scr, q_cat, p_scr):
    lay(q_ref, own, near, far)
    width = heads * HEAD
    keys = kv0.shape[0]
    me, spill = sc[0], sc[1]
    lanes = head_lanes(rows, width)
    key_lanes = head_lanes(keys, width)
    kvs = (kv0, kv1)

    def place(b):
        return pl.multiple_of((b ^ me) * rows, rows)

    for side in range(2):
        lay_heads(v_scr.at[side], kvs[side][:, width : 2 * width], key_lanes, heads)

    @pl.loop(0, blocks)
    def _(p):
        lay_heads(q_cat, q_ref[pl.ds(place(p), rows), :] * jnp.asarray(0.125, BF), lanes, heads)
        query = p * rows + lax.broadcasted_iota(jnp.int32, (1, rows), 1)

        def scores(side, tops):
            spot = lax.broadcasted_iota(jnp.int32, (keys, 1), 0)
            length = jnp.where(side == 0, sc[2], sc[3])
            allowed = cross_allowed(query, spot, side, spill, length, me, padded, real)
            k = jnp.where(side == 0, kv0[:, 0:width], kv1[:, 0:width])
            return score_block(side, k, allowed, q_cat, s_scr, tops)

        first = jnp.where(p * rows < spill, 0, 1)
        last = jnp.where((p + 1) * rows > spill, 2, 1)
        tops, totals, acc = attend(first, last, heads, scores, lambda side: v_scr[side], s_scr, p_scr, width)
        finish(p, place(p), tops, totals, acc, lanes, o_ref, lse_ref)


def spread(p, at, rows, heads, q, g, o_ref, lse_ref, lanes, q_cat, g_cat, stat):
    weighted = (g.astype(F32) * o_ref[at, :].astype(F32)).T
    for h in range(heads):
        q_cat[h * rows : (h + 1) * rows, :] = one_head(q, lanes, h)
        g_cat[h * rows : (h + 1) * rows, :] = one_head(g, lanes, h)
        stat[heads + h : heads + h + 1, :] = jnp.sum(weighted[h * HEAD : (h + 1) * HEAD, :], axis=0, keepdims=True)
    stat[0:heads, :] = lse_ref[0:heads, pl.ds(pl.multiple_of(p * rows, rows), rows)]


def back_block(rows, heads, k, v, allowed, q_cat, g_cat, stat, w_scr, ds_wide, ds_tall):
    count = k.shape[0]
    for h in range(heads):
        span = slice(h * rows, (h + 1) * rows)
        s = dot_nt(k, q_cat[span, :])
        e = jnp.where(allowed, jnp.exp(s - stat[h : h + 1, :]), 0.0)
        de = dot_nt(v, g_cat[span, :])
        ds = (e * (de - stat[heads + h : heads + h + 1, :])).astype(BF)
        w_scr[:, span] = e.astype(BF)
        ds_wide[:, span] = ds
        ds_tall[h * count : (h + 1) * count, :] = ds


def self_backward_kernel(rows, blocks, heads, sc, qkv, kvp, o_ref, own, near, far, lse_ref, dq_ref, dkv_ref,
                         dprev_ref, g_ref, kv_scr, k_cat, dkv_scr, q_cat, g_cat, stat, w_scr, ds_wide, ds_tall):
    lay(g_ref, own, near, far)
    width = heads * HEAD
    extent = rows * blocks
    me, spill, prev_spill = sc[0], sc[1], sc[4]
    lanes = head_lanes(rows, width)

    def place(b):
        return pl.multiple_of((b ^ me) * rows, rows)

    first_used, _ = self_range(0, rows, blocks, spill, prev_spill)

    @pl.loop(0, 2 * blocks)
    def _(kb):
        dkv_scr[kb] = jnp.zeros(dkv_scr.shape[1:], F32)

    @pl.loop(first_used, 2 * blocks)
    def _(kb):
        def fill(pair):
            kv_scr[kb] = pair
            scaled = pair[:, 0:width] * jnp.asarray(0.125, BF)
            for h in range(heads):
                k_cat[kb, h * rows : (h + 1) * rows, :] = one_head(scaled, lanes, h)

        @pl.when(kb < blocks)
        def _():
            fill(kvp[pl.ds(place(kb), rows), :])

        @pl.when(kb >= blocks)
        def _():
            fill(qkv[pl.ds(place(kb - blocks), rows), width : 3 * width])

    @pl.loop(0, blocks)
    def _(p):
        at = pl.ds(place(p), rows)
        q = qkv[at, 0:width] * jnp.asarray(0.125, BF)
        g = g_ref[at, :]
        spread(p, at, rows, heads, q, g, o_ref, lse_ref, lanes, q_cat, g_cat, stat)
        first, last = self_range(p, rows, blocks, spill, prev_spill)
        query = p * rows + lax.broadcasted_iota(jnp.int32, (1, rows), 1)

        def step(kb, dq):
            key = kb * rows + lax.broadcasted_iota(jnp.int32, (rows, 1), 0)
            allowed = self_allowed(query, key, extent, spill, prev_spill)
            back_block(rows, heads, kv_scr[kb, :, 0:width], kv_scr[kb, :, width : 2 * width], allowed,
                       q_cat, g_cat, stat, w_scr, ds_wide, ds_tall)
            dkv_scr[kb, :, 0:width] += dot_nn(ds_wide[...], q_cat[...])
            dkv_scr[kb, :, width : 2 * width] += dot_nn(w_scr[...], g_cat[...])
            return dq + dot_tn(ds_tall[...], k_cat[kb])

        dq = lax.fori_loop(first, last, step, jnp.zeros((rows, width), F32))
        dq_ref[at, :] = dq.astype(BF)

    @pl.loop(0, blocks)
    def _(b):
        at = pl.ds(place(b), rows)
        dprev_ref[at, :] = dkv_scr[b].astype(BF)
        dkv_ref[at, :] = dkv_scr[blocks + b].astype(BF)


def cross_backward_kernel(rows, blocks, heads, padded, real, pieces, sc, q_ref, kv0, kv1, o_ref, own, near, far,
                          lse_ref, dq_ref, dkv0_ref, dkv1_ref, g_ref, k_cat, dkv_scr, q_cat, g_cat, stat, w_scr, ds_wide, ds_tall):
    lay(g_ref, own, near, far)
    width = heads * HEAD
    keys = kv0.shape[0]
    step_keys = keys // pieces
    me, spill = sc[0], sc[1]
    lanes = head_lanes(rows, width)
    key_lanes = head_lanes(step_keys, width)
    kvs = (kv0, kv1)

    def place(b):
        return pl.multiple_of((b ^ me) * rows, rows)

    dkv_scr[...] = jnp.zeros(dkv_scr.shape, F32)
    for side in range(2):
        for piece in range(pieces):
            scaled = kvs[side][piece * step_keys : (piece + 1) * step_keys, 0:width] * jnp.asarray(0.125, BF)
            for h in range(heads):
                k_cat[side * pieces + piece, h * step_keys : (h + 1) * step_keys, :] = one_head(scaled, key_lanes, h)

    @pl.loop(0, blocks)
    def _(p):
        at = pl.ds(place(p), rows)
        q = q_ref[at, :] * jnp.asarray(0.125, BF)
        spread(p, at, rows, heads, q, g_ref[at, :], o_ref, lse_ref, lanes, q_cat, g_cat, stat)
        query = p * rows + lax.broadcasted_iota(jnp.int32, (1, rows), 1)
        reads = (p * rows < spill, (p + 1) * rows > spill)
        first = jnp.where(reads[0], 0, pieces)
        last = jnp.where(reads[1], 2 * pieces, pieces)

        def step(kb, dq):
            side = kb // pieces
            at_key = pl.ds(pl.multiple_of((kb - side * pieces) * step_keys, step_keys), step_keys)
            spot = (kb - side * pieces) * step_keys + lax.broadcasted_iota(jnp.int32, (step_keys, 1), 0)
            length = jnp.where(side == 0, sc[2], sc[3])
            allowed = cross_allowed(query, spot, side, spill, length, me, padded, real)
            is_prev = side == 0
            pair = jnp.where(is_prev, kv0[at_key, :], kv1[at_key, :])
            back_block(rows, heads, pair[:, 0:width], pair[:, width : 2 * width], allowed,
                       q_cat, g_cat, stat, w_scr, ds_wide, ds_tall)
            dkv_scr[kb, :, 0:width] += dot_nn(ds_wide[...], q_cat[...])
            dkv_scr[kb, :, width : 2 * width] += dot_nn(w_scr[...], g_cat[...])
            return dq + dot_tn(ds_tall[...], k_cat[kb])

        dq = lax.fori_loop(first, last, step, jnp.zeros((rows, width), F32))
        dq_ref[at, :] = dq.astype(BF)

    for piece in range(pieces):
        span = slice(piece * step_keys, (piece + 1) * step_keys)
        dkv0_ref[span, :] = dkv_scr[piece].astype(BF)
        dkv1_ref[span, :] = dkv_scr[pieces + piece].astype(BF)


def call(kernel, scalars, arrays, outs, scratch=(), time=2):
    vmem = pl.BlockSpec(memory_space=pltpu.VMEM)
    held = (*arrays, *jax.tree.leaves(outs), *scratch)
    room = sum(math.prod(a.shape) * jnp.dtype(a.dtype).itemsize for a in held) + 7 * 2**20
    return pl.pallas_call(
        kernel,
        out_shape=outs,
        in_specs=[pl.BlockSpec(memory_space=pltpu.SMEM)] + [vmem] * len(arrays),
        out_specs=jax.tree.map(lambda _: vmem, outs),
        scratch_shapes=scratch,
        compiler_params=pltpu.CompilerParams(vmem_limit_bytes=min(room, 48 * 2**20)),
        cost_estimate=pl.CostEstimate(flops=1024, bytes_accessed=int(time * 640000), transcendentals=0),
    )(scalars, *arrays)


def self_forward(scalars, qkv, kvp, blocks):
    extent = qkv.shape[0]
    rows = extent // blocks
    width = qkv.shape[1] // 3
    heads = width // HEAD
    return call(
        functools.partial(self_forward_kernel, rows, blocks, heads),
        scalars,
        (qkv, kvp),
        [jax.ShapeDtypeStruct((extent, width), BF), jax.ShapeDtypeStruct((8, extent), F32)],
        [
            pltpu.VMEM((2 * blocks, rows, width), BF),
            pltpu.VMEM((2 * blocks, heads * rows, width), BF),
            pltpu.VMEM((2 * blocks, heads, rows, rows), F32),
            pltpu.VMEM((heads * rows, width), BF),
            pltpu.VMEM((heads * rows, rows), BF),
        ],
        time=18,
    )


def cross_forward(scalars, pieces, kv0, kv1, blocks, real):
    rows, width = pieces[0].shape
    extent = rows * blocks
    heads = width // HEAD
    keys = kv0.shape[0]
    return call(
        functools.partial(cross_forward_kernel, rows, blocks, heads, keys // blocks, real),
        scalars,
        (*pieces, kv0, kv1),
        [
            jax.ShapeDtypeStruct((extent, width), BF),
            jax.ShapeDtypeStruct((8, extent), F32),
            jax.ShapeDtypeStruct((extent, width), BF),
        ],
        [
            pltpu.VMEM((2, heads * keys, width), BF),
            pltpu.VMEM((2, heads, keys, rows), F32),
            pltpu.VMEM((heads * rows, width), BF),
            pltpu.VMEM((heads * keys, rows), BF),
        ],
        time=9,
    )


def back_scratch(rows, heads, width, keys):
    return [
        pltpu.VMEM((heads * rows, width), BF),
        pltpu.VMEM((heads * rows, width), BF),
        pltpu.VMEM((8, rows), F32),
        pltpu.VMEM((keys, heads * rows), BF),
        pltpu.VMEM((keys, heads * rows), BF),
        pltpu.VMEM((heads * keys, rows), BF),
    ]


def self_backward(scalars, qkv, kvp, o, g, lse, blocks):
    extent = qkv.shape[0]
    rows = extent // blocks
    width = qkv.shape[1] // 3
    heads = width // HEAD
    return call(
        functools.partial(self_backward_kernel, rows, blocks, heads),
        scalars,
        (qkv, kvp, o, *g, lse),
        [
            jax.ShapeDtypeStruct((extent, width), BF),
            jax.ShapeDtypeStruct((extent, 2 * width), BF),
            jax.ShapeDtypeStruct((extent, 2 * width), BF),
        ],
        [
            pltpu.VMEM((extent, width), BF),
            pltpu.VMEM((2 * blocks, rows, 2 * width), BF),
            pltpu.VMEM((2 * blocks, heads * rows, width), BF),
            pltpu.VMEM((2 * blocks, rows, 2 * width), F32),
        ]
        + back_scratch(rows, heads, width, rows),
        time=22,
    )


def cross_backward(scalars, q, kv0, kv1, o, g, lse, blocks, real, pieces=1):
    extent, width = q.shape
    rows = extent // blocks
    heads = width // HEAD
    keys = kv0.shape[0]
    step_keys = keys // pieces
    return call(
        functools.partial(cross_backward_kernel, rows, blocks, heads, keys // blocks, real, pieces),
        scalars,
        (q, kv0, kv1, o, *g, lse),
        [
            jax.ShapeDtypeStruct((extent, width), BF),
            jax.ShapeDtypeStruct((keys, 2 * width), BF),
            jax.ShapeDtypeStruct((keys, 2 * width), BF),
        ],
        [
            pltpu.VMEM((extent, width), BF),
            pltpu.VMEM((2 * pieces, heads * step_keys, width), BF),
            pltpu.VMEM((2 * pieces, step_keys, 2 * width), F32),
        ]
        + back_scratch(rows, heads, width, step_keys),
        time=14,
    )


def ordered_pieces(pieces, me):
    odd = (me & 1) == 1
    high = (me & 2) == 2
    low_pair = [jnp.where(odd, pieces[1 - i], pieces[i]) for i in range(2)]
    high_pair = [jnp.where(odd, pieces[3 - i], pieces[2 + i]) for i in range(2)]
    ordered = [jnp.where(high, high_pair[i], low_pair[i]) for i in range(2)]
    return ordered + [jnp.where(high, low_pair[i], high_pair[i]) for i in range(2)]


def join_pieces(pieces, me, axis):
    return jnp.concatenate(ordered_pieces(pieces, me), axis=axis)


def received(own, near, far, me):
    rows = own.shape[0]
    return join_pieces([own[...], near[0:rows, :], far[0:rows, :], near[rows:, :]], me, 1)


def send_pieces(tensor, me, first, second, rest):
    width = tensor.shape[1] // 4
    rows = tensor.shape[0]
    pieces = ordered_pieces([tensor[:, k * width : (k + 1) * width] for k in range(4)], me)
    first[...] = pieces[0]
    second[...] = pieces[1]
    rest[0:rows, :] = pieces[2]
    rest[rows:, :] = pieces[3]


def half_product(tensor, own, other, me, first):
    span = slice(first, first + own.shape[0] // 2)
    left, right = dot_nn(tensor, own[:, span]), dot_nn(tensor, other[:, span])
    odd = (me & 1) == 1
    return jnp.concatenate([jnp.where(odd, right, left), jnp.where(odd, left, right)], axis=1)


def two_halves(tensor, me):
    half = tensor.shape[1] // 2
    odd = (me & 1) == 1
    left, right = tensor[:, 0:half], tensor[:, half:]
    return jnp.where(odd, right, left), jnp.where(odd, left, right)


def half_back(mine, others, own, other, first):
    span = slice(first, first + own.shape[0] // 2)
    return dot_nt(mine, own[:, span]) + dot_nt(others, other[:, span])


def normal_parts(tensor):
    average = jnp.mean(tensor, axis=-1, keepdims=True)
    centered = tensor - average
    scale = lax.rsqrt(jnp.mean(centered * centered, axis=-1, keepdims=True) + 1e-05)
    return centered * scale, scale


def normal_back(plain, scale, grad):
    inner = jnp.mean(grad * plain, axis=-1, keepdims=True)
    return scale * (grad - jnp.mean(grad, axis=-1, keepdims=True) - plain * inner)


def gelu_parts(pre):
    size = jnp.abs(pre)
    t = 1.0 / (1.0 + (0.3275911 * 0.7071067811865476) * size)
    poly = ((((1.061405429 * t - 1.453152027) * t + 1.421413741) * t - 0.284496736) * t + 0.254829592) * t
    bell = jnp.exp(-0.5 * pre * pre)
    tail = 0.5 * poly * bell
    cdf = jnp.where(pre < 0.0, tail, 1.0 - tail)
    return pre * cdf, cdf + pre * bell * 0.3989422804014327


def place_kernel(group, at, lengths, ids, *outs):
    seq, me = at[0], at[1]
    before = jnp.maximum(seq - 1, 0)
    for i, out in enumerate(outs):
        out[0] = me
        out[2] = lengths[i, before]
        out[3] = lengths[i, seq]
        for slot, block, number in ((1, seq, seq), (4, before, seq - 1)):
            rows = group // 128
            part = ids[i, pl.ds(pl.multiple_of(block * rows, rows), rows), :]
            out[slot] = jnp.sum(jnp.where(part < number, 1.0, 0.0)).astype(jnp.int32)
        for slot in (5, 6, 7):
            out[slot] = 0


def norm_kernel(at, x, low):
    rows = 256
    for start in range(0, low.shape[0], rows):
        span = slice(start, min(start + rows, low.shape[0]))
        low[span, :] = normal_parts(x[span, :].astype(F32))[0].astype(BF)


def lay_four(out, own, near, far, last):
    rows = own.shape[0]
    for k, ref in enumerate((own, near, far, last)):
        out[k * rows : (k + 1) * rows, :] = ref[...]


def qkv_kernel(i, rows, at, *refs):
    weight, qkv, kvp = refs[8:]
    width = weight.shape[1] // 3
    own = slice(i * rows, (i + 1) * rows)
    for k in range(4):
        block = slice(k * rows, (k + 1) * rows)
        qkv[block, :] = dot_nn(refs[k][own, :], weight[...]).astype(BF)
        kvp[block, :] = dot_nn(refs[4 + k][own, :], weight[:, width:]).astype(BF)


def memory_kernel(size, at, *refs):
    weight, outs = refs[8], refs[9:]
    count = len(outs) // 2
    rows, keys = outs[:count], outs[count:]
    for i in range(count):
        span = slice((i % (count // 2)) * size, (i % (count // 2) + 1) * size)
        pieces = refs[0:4] if i < count // 2 else refs[4:8]
        block = jnp.concatenate([ref[span, :] for ref in pieces], axis=0)
        rows[i][...] = block
        keys[i][...] = dot_nn(block, weight[...]).astype(BF)


def hidden_kernel(rows, at, whole, inner, outer):
    slot = 2 * rows
    for i in range(inner.shape[0] // rows):
        inner[i * rows : (i + 1) * rows, :] = whole[i * slot : i * slot + rows, :]
        outer[i * rows : (i + 1) * rows, :] = whole[i * slot + rows : i * slot + 2 * rows, :]


def hidden_grads_kernel(rows, at, pre_low, low, act, top, *refs):
    before, out = (refs[0], refs[1]) if len(refs) == 2 else (None, refs[0])
    step, slot = 256, 2 * rows
    for i in range(pre_low.shape[1] // step):
        for k, (left, right) in enumerate(((pre_low, low), (act, top))):
            grad = dot_tn(left[:, i * step : (i + 1) * step], right[...])
            for part in range(step // rows):
                start = (i * step // rows + part) * slot + k * rows
                block = grad[part * rows : (part + 1) * rows]
                if before is not None:
                    block = block + before[start : start + rows, :].astype(F32)
                out[start : start + rows, :] = block.astype(BF)


def near_kernel(at, keep, received, near, far):
    rows = near.shape[0]
    near[...] = keep[0:rows, :].astype(F32) + received[0:rows, :].astype(F32)
    far[...] = (keep[rows:, :].astype(F32) + received[rows:, :].astype(F32)).astype(BF)


def tree_kernel(at, keep, received, kept, sent):
    rows = kept.shape[0]
    kept[...] = keep[0:rows, :] + received[0:rows, :].astype(F32)
    sent[...] = (keep[rows:, :] + received[rows:, :].astype(F32)).astype(BF)


def output_kernel(at, after, near, far, out):
    out[...] = (after[...] + near[...] + far[...].astype(F32)).astype(BF)


def grad_x_kernel(i, at, x, before, near, far, back, out):
    rows = out.shape[0]
    plain, scale = normal_parts(x[i * rows : (i + 1) * rows, :].astype(F32))
    grad = near[...] + far[...].astype(F32) + back[...].astype(F32)
    out[...] = before[...] + normal_back(plain, scale, grad)


def far_sum_kernel(at, near, far, out):
    out[...] = (near[...] + far[...].astype(F32)).astype(BF)


def memory_back_kernel(at, own_a, own_b, prev_a, prev_b, rows_a, rows_b, rows_prev_a, rows_prev_b, weight,
                       grad, keep, send):
    rows = own_a.shape[0] // 4
    total = None
    grads, places = (own_a, own_b, prev_a, prev_b), (rows_a, rows_b, rows_prev_a, rows_prev_b)
    for k, (part, memory) in enumerate(zip(grads, places)):
        term = dot_tn(memory[...], part[...])
        total = term if total is None else total + term
        part = dot_nt(part[...], weight[...]).astype(BF)
        for slot, out, place in ((0, keep, 0), (1, send, 0), (2, keep, 4), (3, send, 4)):
            out[(place + k) * rows : (place + k + 1) * rows, :] = part[slot * rows : (slot + 1) * rows]
    grad[...] = total


def self_out_kernel(i, at, own, near, far, x, wide_own, wide_other,
                    low, after, plain, low_next, scale, first, second, rest):
    me = at[0]
    joined = received(own, near, far, me)
    low[...] = joined
    rows = low.shape[0]
    total = x[i * rows : (i + 1) * rows, :].astype(F32) + half_product(joined, wide_own, wide_other, me, 0)
    after[...] = total
    normed, scaled = normal_parts(total)
    plain[...] = normed
    scale[...] = scaled
    rounded = normed.astype(BF)
    low_next[...] = rounded
    send_pieces(half_product(rounded, wide_own, wide_other, me, wide_own.shape[0] // 2).astype(BF), me, first, second, rest)


def cross_out_kernel(at, own, near, far, before, out_own, out_other, gain, low, after, plain, scale, low_next):
    me = at[0]
    joined = received(own, near, far, me)
    low[...] = joined
    total = before[...] + half_product(joined, out_own, out_other, me, 0)
    after[...] = total
    normed, scaled = normal_parts(total)
    plain[...] = normed
    scale[...] = scaled
    low_next[...] = (normed * gain[...]).astype(BF)


def mlp_kernel(i, at, low, near_low, far_low, last_low, top, near_top, far_top, last_top, inner, outer,
               low_all, top_all, act, pre_low, grad_keep, grad_send, out_keep, out_send):
    rows = low.shape[0]
    lay_four(low_all, low, near_low, far_low, last_low)
    lay_four(top_all, *(ref.at[i * rows : (i + 1) * rows, :] for ref in (top, near_top, far_top, last_top)))
    for parity, grad, out in ((1, grad_send, out_send), (0, grad_keep, out_keep)):

        @pl.loop(0, 2)
        def _(b):
            block = pl.ds(pl.multiple_of((2 * b + parity) * rows, rows), rows)
            place = pl.ds(pl.multiple_of(b * rows, rows), rows)
            value, slope = gelu_parts(dot_nt(low_all[block, :], inner[...]))
            act_block = value.astype(BF)
            act[block, :] = act_block
            pre_block = (dot_nt(top_all[block, :], outer[...]) * slope).astype(BF)
            pre_low[block, :] = pre_block
            grad[place, :] = dot_nn(pre_block, inner[...]).astype(BF)
            out[place, :] = dot_nn(act_block, outer[...]).astype(BF)


def cross_back_kernel(i, at, near, far, plain, scale, gain, top, out_own, out_other,
                      grad_after, branch_own, branch_other, grad_gain, first, second, rest):
    me = at[0]
    grad = near[...] + far[...].astype(F32)
    normed = plain[...]
    grad_gain[...] = jnp.sum(grad * normed, axis=0, keepdims=True)
    rows = near.shape[0]
    total = top[i * rows : (i + 1) * rows, :].astype(F32) + normal_back(normed, scale[...], grad * gain[...])
    grad_after[...] = total
    mine, others = two_halves(total.astype(BF), me)
    branch_own[...] = mine
    branch_other[...] = others
    send_pieces(half_back(mine, others, out_own, out_other, 0).astype(BF), me, first, second, rest)


def self_back_kernel(at, own, near, far, plain, scale, before, wide_own, wide_other,
                     grad_after, query_mine, query_others, branch_own, branch_other, first, second, rest):
    me = at[0]
    mine, others = two_halves(received(own, near, far, me), me)
    query_mine[...] = mine
    query_others[...] = others
    total = before[...] + normal_back(plain[...], scale[...], half_back(mine, others, wide_own, wide_other, wide_own.shape[0] // 2))
    grad_after[...] = total
    mine, others = two_halves(total.astype(BF), me)
    branch_own[...] = mine
    branch_other[...] = others
    send_pieces(half_back(mine, others, wide_own, wide_other, 0).astype(BF), me, first, second, rest)


def half_grads_kernel(names, at, *refs):
    own, other = refs[-2:]
    half = own.shape[1] // names
    for n in range(names):
        parts = [ref[...] for ref in refs[6 * n : 6 * n + 6]]
        low, mine, others = (jnp.concatenate(parts[k : k + 2], axis=0) for k in (0, 2, 4))
        span = slice(n * half, (n + 1) * half)
        other[:, span] = dot_tn(low, others).astype(BF)
        own[:, span] = dot_tn(low, mine)


def qkv_back_kernel(at, dq, dkv, dkv_prev, weight, keep, send, keep_prev, send_prev):
    rows = dq.shape[0] // 4
    width = dq.shape[1]
    for parity, out, out_prev in ((1, send, send_prev), (0, keep, keep_prev)):
        for b in range(2):
            block = slice((2 * b + parity) * rows, (2 * b + parity + 1) * rows)
            place = slice(b * rows, (b + 1) * rows)
            grad = dot_nt(dq[block, :], weight[:, 0:width]) + dot_nt(dkv[block, :], weight[:, width:])
            out[place, :] = grad.astype(BF)
            out_prev[place, :] = dot_nt(dkv_prev[block, :], weight[:, width:]).astype(BF)


def lay_own(i, refs, low_all, before_all):
    rows = low_all.shape[0] // 4
    own = slice(i * rows, (i + 1) * rows)
    for out, pieces in ((low_all, refs[0:4]), (before_all, refs[4:8])):
        for k, ref in enumerate(pieces):
            out[k * rows : (k + 1) * rows, :] = ref[own, :]


def qkv_grads_kernel(i, at, *refs):
    dq, dkv, dkv_prev, out, low, before, own = refs[8:]
    width = dq.shape[1]
    lay_own(i, refs, low, before)
    out[:, 0:width] = dot_tn(low[...], dq[...])
    own[...] = dot_tn(low[...], dkv[...])
    out[:, width:] = own[...] + dot_tn(before[...], dkv_prev[...])


def last_qkv_grads_kernel(i, offsets, at, *refs):
    dq, dkv, dkv_prev, earlier, keep, send, low, before, total = refs[8:]
    width = dq.shape[1]
    lay_own(i, refs, low, before)
    total[:, 0:width] = earlier[:, 0:width] + dot_tn(low[...], dq[...])
    total[:, width:] = earlier[:, width:] + dot_tn(low[...], dkv[...])
    total[:, width:] += dot_tn(before[...], dkv_prev[...])
    half = len(offsets) // 2
    rows = total.shape[0] // len(offsets)
    for n, offset in enumerate(offsets):
        out = keep if n < half else send
        start = pl.multiple_of((at[0] ^ offset) * rows, rows)
        out[(n % half) * rows : (n % half + 1) * rows, :] = total[pl.ds(start, rows), :].astype(out.dtype)


def shape(rows, columns, dtype=BF):
    return jax.ShapeDtypeStruct((rows, columns), dtype)


D = 1024
MICRO = 2


def flip(block, axis, bit):
    return lax.ppermute(block, axis, [(i, i ^ bit) for i in range(lax.axis_size(axis))])


def shifted(block, distance):
    devices = range(lax.axis_size("seq"))
    route = [(i - distance, i) for i in devices if i - distance in devices]
    return lax.ppermute(block, "seq", route)


def far_slots(part):
    rows = part.shape[0] // 4
    return part[:rows], part[rows : 2 * rows], flip(part[2 * rows :], "mem", 2)


def near_slots(own, side, far):
    rows = own.shape[0]
    return own, flip(jnp.concatenate([side, far[rows:]], axis=0), "mem", 1), far


def near_sum(place, keep, send):
    rows, columns = keep.shape
    outs = [shape(rows // 2, columns, F32), shape(rows // 2, columns)]
    return call(near_kernel, place, (keep, flip(send, "mem", 1)), outs, time=1)


def seq_bits():
    count = lax.axis_size("seq")
    return [1 << i for i in reversed(range(count.bit_length() - 1))]


def seq_offsets(bits):
    offsets = [0]
    for bit in bits:
        offsets = offsets + [o ^ bit for o in offsets]
    return offsets


def seq_stage(block, bit):
    return jnp.concatenate([block, flip(block, "seq", bit)], axis=0)


def assemble_kernel(rows, offsets, at, first, second, *outs):
    half = len(offsets) // 2
    for i, offset in enumerate(offsets):
        ref = first if i < half else second
        start = pl.multiple_of((at[0] ^ offset) * rows, rows)
        column = 0
        for out in outs:
            columns = out.shape[1]
            place = slice((i % half) * rows, (i % half + 1) * rows)
            out[pl.ds(start, rows), :] = ref[place, column : column + columns]
            column += columns


def assemble(first, second, seq, bits, split):
    offsets = seq_offsets(bits)
    size = 2 * first.shape[0]
    outs = [shape(size, columns) for columns in split]
    return call(functools.partial(assemble_kernel, size // len(offsets), offsets), seq.reshape(1), (first, second), outs)


def reorder_kernel(rows, offsets, groups, at, *refs):
    keep, send = refs[-2:]
    half = len(offsets) // 2
    for i, offset in enumerate(offsets):
        start = pl.multiple_of((at[0] ^ offset) * rows, rows)
        out = keep if i < half else send
        place = slice((i % half) * rows, (i % half + 1) * rows)
        for column, terms in groups:
            total = None
            for term, first, columns in terms:
                part = refs[term][pl.ds(start, rows), first : first + columns].astype(F32)
                total = part if total is None else total + part
            out[place, column : column + columns] = total.astype(out.dtype)


def reorder(arrays, groups, seq, bits):
    offsets = seq_offsets(bits)
    size = arrays[0].shape[0]
    placed, column = [], 0
    for terms in groups:
        placed.append((column, terms))
        column += terms[0][2]
    kernel = functools.partial(reorder_kernel, size // len(offsets), offsets, placed)
    return call(kernel, seq.reshape(1), arrays, [shape(size // 2, column, F32), shape(size // 2, column)], time=column // 300)


def pack_kernel(width, half, at, *refs):
    me = at[0]
    (gain_self, gain_cross, gain_mlp), weights, (kept, message) = refs[:3], refs[3:11], refs[11:]
    query, key, value, out_w, cross_q, cross_k, cross_v, cross_o = weights

    def scaled(weight, gain):
        return (weight.astype(F32) * gain[...].astype(F32)).astype(BF)

    def piece(k):
        at_k = pl.ds(pl.multiple_of((me ^ k) * width, width), width)
        gained = [scaled(w[:, at_k], gain_self) for w in (query, key, value)]
        return jnp.concatenate(gained + [w[:, at_k] for w in (cross_k, cross_v)], axis=1)

    def side(k):
        at_k = pl.ds(pl.multiple_of(((me & 1) ^ k) * half, half), half)
        rows = gain_mlp.shape[0]
        lanes = lax.broadcasted_iota(jnp.int32, (rows, 128), 1)
        extra = jnp.where(lanes == 0, gain_mlp[...].astype(F32), 0.0).astype(BF)
        return jnp.concatenate([out_w[:, at_k], scaled(cross_q[:, at_k], gain_cross), cross_o[:, at_k], extra], axis=1)

    kept[...] = jnp.concatenate([piece(0), piece(1)], axis=1)
    message[...] = jnp.concatenate([piece(2), piece(3), side(0), side(1)], axis=1)


def repack_kernel(narrow, broad, at, kept, message, far, out):
    sides = 2 * narrow + broad
    out[:, 0:narrow] = kept[:, narrow:]
    out[:, narrow : 2 * narrow] = far[:, narrow : 2 * narrow]
    out[:, 2 * narrow : 2 * narrow + broad] = message[:, sides:]
    out[:, 2 * narrow + broad :] = far[:, sides:]


def unpack_kernel(width, narrow, broad, at, kept, message, far, near, qkv, first):
    me = at[0]
    start = 2 * narrow
    heads = [kept[:, 0:narrow], near[:, 0:narrow], far[:, 0:narrow], near[:, narrow:start]]
    sides = [message, near, far, near]
    sides = [ref[:, at_k : at_k + broad] for ref, at_k in zip(sides, (start, start, start, start + broad))]
    heads = join_pieces(heads, me, 0)
    sides = join_pieces(sides, me, 0)
    qkv[...] = heads[:, 0 : 3 * width]
    pair = broad - 128 - (broad - 128) // 3
    first[...] = jnp.concatenate([sides[:, 0:pair], heads[:, 3 * width :], sides[:, pair:]], axis=1)


class Stay:
    def __init__(self, value):
        self.value = value


def interleave(streams, sides):
    held = [next(s) for s in streams]
    results = [None] * len(streams)
    waiting = [(side, *next(side)) for side in sides]
    turn = 0
    ticks = 0

    def serve(arrays):
        nonlocal ticks, waiting
        ticks += 1
        due = [w for w in waiting if w[1] == ticks]
        waiting = [w for w in waiting if w[1] != ticks]
        arrays, taken = lax.optimization_barrier((arrays, [w[2]() for w in due]))
        for (side, _, _), got in zip(due, taken):
            try:
                waiting.append((side, *side.send(got)))
            except StopIteration:
                pass
        return arrays

    while True:
        other = (turn + 1) % len(streams)
        try:
            mark = streams[turn].send(held[turn])
            while isinstance(mark, Stay):
                mark = streams[turn].send(serve(mark.value))
            if results[other] is None:
                held[other], mark = serve((held[other], mark))
            else:
                mark = serve(mark)
            held[turn] = streams[turn].send(mark)
        except StopIteration as end:
            results[turn] = end.value
        if results[other] is None:
            turn = other
        elif results[turn] is not None:
            assert not waiting
            return results


def shards(
    inputs,
    memory,
    page_ids,
    memory_length,
    cotangent,
    gain_self,
    self_query,
    self_key,
    self_value,
    self_out,
    gain_cross,
    cross_query,
    cross_key,
    cross_value,
    cross_out,
    gain_mlp,
    mlp_in,
    mlp_out,
):
    seq = lax.axis_index("seq")
    me = lax.axis_index("mem")
    odd = me & 1
    blocks = lax.axis_size("mem")
    tok = inputs.shape[1]
    group = tok * blocks
    real = memory.shape[2]
    padded = -(-real // 16) * 16
    wrows = self_query.shape[0]
    bits = seq_bits()
    turned = bits[:-2] + [bits[-1], bits[-2]]
    half = D // 2

    def join_halves(own, other):
        return jnp.concatenate([jnp.where(odd == 0, own, other), jnp.where(odd == 0, other, own)], axis=1)

    width = self_query.shape[1] // blocks
    narrow, broad = 5 * width, 3 * half + 128
    place = me.reshape(1)
    weights = (self_query, self_key, self_value, self_out, cross_query, cross_key, cross_value, cross_out)
    gains = [g[:, None] for g in (gain_self, gain_cross, gain_mlp)]
    kept, message = call(
        functools.partial(pack_kernel, width, half), place, (*gains, *weights),
        [shape(wrows, 2 * narrow), shape(wrows, 2 * (narrow + broad))],
    )
    far = flip(message, "mem", 2)
    x_rows, tops = inputs.reshape(MICRO * tok, D), cotangent.reshape(MICRO * tok, D)
    lows = call(norm_kernel, place, (x_rows,), shape(MICRO * tok, D))
    befores = shifted(lows, 1)
    far_lows, near_lows = flip(lows, "mem", 2), flip(lows, "mem", 1)
    smem = pl.BlockSpec(memory_space=pltpu.SMEM)
    ids = page_ids.reshape(MICRO, -1, 128)
    places = pl.pallas_call(
        functools.partial(place_kernel, group),
        out_shape=[jax.ShapeDtypeStruct((8,), jnp.int32)] * MICRO,
        in_specs=[smem, smem, pl.BlockSpec(memory_space=pltpu.VMEM)],
        out_specs=[smem] * MICRO,
    )(jnp.stack([seq, me]), memory_length, ids)
    near = call(
        functools.partial(repack_kernel, narrow, broad), place, (kept, message, far),
        shape(*message.shape),
    )
    near = flip(near, "mem", 1)
    qkv_part, first_part = call(
        functools.partial(unpack_kernel, width, narrow, broad), place, (kept, message, far, near),
        [shape(blocks * wrows, columns) for columns in (3 * width, 3 * half + 128 + 2 * width)],
    )

    state = {}
    hidden = mlp_in.shape[0]
    stage = seq_stage(qkv_part, bits[0])
    stage, first_part, befores, memory_here = lax.optimization_barrier((stage, first_part, befores, memory))
    far_befores, near_befores = flip(befores, "mem", 2), flip(befores, "mem", 1)
    first_stage = first_part
    for bit in bits[:-3]:
        first_stage = seq_stage(first_stage, bit)
    first_pair = first_stage, flip(first_stage, "seq", bits[-3])
    memory_own = jnp.pad(memory_here.reshape(MICRO, real, D), ((0, 0), (0, padded - real), (0, 0)))
    memory_own = memory_own.reshape(MICRO * padded, D)
    hidden_part = jnp.concatenate([mlp_in, mlp_out], axis=0)
    for bit in bits[1:-1]:
        stage = seq_stage(stage, bit)
    stage, far_lows, memory_own, hidden_part, places = lax.optimization_barrier(
        (stage, far_lows, memory_own, hidden_part, places)
    )
    last_lows = flip(far_lows, "mem", 1)
    last_stage, first_pair, far_befores, memory_own, tops = lax.optimization_barrier(
        (flip(stage, "seq", bits[-1]), first_pair, far_befores, memory_own, tops)
    )
    first_stage = seq_stage(jnp.concatenate(first_pair, axis=0), bits[-2])
    memory_before = shifted(memory_own, 1)
    memory_far = flip(memory_own, "mem", 2)
    far_tops, near_tops = flip(tops, "mem", 2), flip(tops, "mem", 1)
    (qkv_full,) = assemble(stage, last_stage, seq, bits, [3 * width])
    gathered = [lows, near_lows, far_lows, last_lows, befores, near_befores, far_befores, flip(far_befores, "mem", 1)]

    def first_side():
        (first,) = yield 2, lambda: (first_stage,)
        cut = 2 * half + 2 * width
        first, last = first[:, :cut], first[:, cut:]
        first = first, flip(first, "seq", bits[-1])
        *first, last = yield 3, lambda: (*first, last)
        state["wide_own"], state["ckv"] = assemble(*first, seq, bits, [2 * half, 2 * width])
        state["wide_other"] = flip(state["wide_own"], "mem", 1)
        last = last, flip(last, "seq", bits[-1])
        last = yield 6, lambda: last
        state["cout_own"], gain = assemble(*last, seq, bits, [half, 128])
        state["gain"] = gain[:, 0].astype(F32)[None, :]
        state["cout_other"] = flip(state["cout_own"], "mem", 1)

    def memory_side():
        before, near_own = yield 2, lambda: (memory_before, flip(memory_own, "mem", 1))
        far_prev, near_prev = flip(before, "mem", 2), flip(before, "mem", 1)
        *gone, far_own = yield 3, lambda: (before, near_own, far_prev, near_prev, memory_far)
        before, near_own, far_prev, near_prev = gone
        last_own, last_prev = flip(far_own, "mem", 1), flip(far_prev, "mem", 1)
        pieces = memory_own, near_own, far_own, last_own, before, near_prev, far_prev, last_prev
        pieces = yield 4, lambda: pieces
        whole = blocks * padded
        outs = [shape(whole, D)] * (2 * MICRO) + [shape(whole, 2 * width)] * (2 * MICRO)
        got = call(functools.partial(memory_kernel, padded), place, (*pieces, state["ckv"]), outs, time=6)
        state["rows"], state["rows_prev"], state["mem_kv"], state["mem_prev"] = (
            got[k * MICRO : (k + 1) * MICRO] for k in range(4)
        )

    def top_side():
        far, near = yield 2, lambda: (far_tops, near_tops)
        state["top"] = tops, near, far, flip(far, "mem", 1)

    def hidden_side():
        (part,) = yield 2, lambda: (hidden_part,)
        whole = lax.all_gather(part, "seq", axis=0, tiled=True)
        (whole,) = yield 8, lambda: (whole,)
        both = [shape(whole.shape[0] // 2, D)] * 2
        both = call(functools.partial(hidden_kernel, hidden), place, (whole,), both)
        state["inner"], state["outer"] = yield 9, lambda: both
        kernel = functools.partial(hidden_grads_kernel, hidden)
        arrays = yield 11, lambda: state["grad_hidden"][0]
        grads = call(kernel, place, arrays, shape(2 * D, D), time=9)
        arrays = yield 12, lambda: (*state["grad_hidden"][1], grads)
        grads = call(kernel, place, arrays, shape(2 * D, D), time=9)
        (grads,) = yield 13, lambda: (grads,)
        grads = lax.psum_scatter(grads, "seq", scatter_dimension=0, tiled=True)
        (grads,) = yield 19, lambda: (grads,)
        state["hidden_grads"] = grads[:hidden].astype(F32), grads[hidden:].astype(F32)

    order = turned[::-1]

    def seq_next(kept, received, bit):
        rows, columns = kept.shape[0] // 2, kept.shape[1]
        kept, sent = call(tree_kernel, place, (kept, received), [shape(rows, columns, F32), shape(rows, columns)])
        return kept, flip(sent, "seq", bit)

    def half_grads(names):
        arrays = [part for low, mine, others in names for part in (*low, *mine, *others)]
        outs = [shape(D, len(names) * half, F32), shape(D, len(names) * half)]
        return call(functools.partial(half_grads_kernel, len(names)), place, arrays, outs, time=2 * len(names))

    def tree_side(name, arrays, groups, ticks):
        arrays = yield ticks[0], lambda: arrays
        kept, sent = reorder(arrays, groups, seq, turned)
        pair = kept, flip(sent, "seq", order[0])
        for bit, tick in zip(order[1:], ticks[1:]):
            pair = yield tick, lambda: pair
            pair = seq_next(*pair, bit)
        state[name] = pair

    def cout_side():
        names, gains = yield 15, lambda: (state["grad_cout"], state["grad_gain_three"])
        own, other = half_grads([list(zip(*names))])
        gains = jnp.pad((gains[0] + gains[1]).reshape(D, 1), ((0, 0), (0, 127)))
        groups = [[(0, 0, half), (1, 0, half)], [(2, 0, 128)]]
        yield from tree_side("cout", (own, flip(other, "mem", 1), gains), groups, (16, 20))

    def wide_side():
        out, query, dmem = yield 17, lambda: (state["grad_out"], state["grad_cquery"], state["dmem"])
        own, other = half_grads([list(zip(*out)), list(zip(*query))])
        other = flip(other, "mem", 1)
        mem_rows = shape(8 * padded, D)
        arrays = (*(part for pair in zip(*dmem) for part in pair), *state["rows"], *state["rows_prev"], state["ckv"])
        ckv, mem_keep, mem_send = call(
            memory_back_kernel, place, arrays, [shape(D, 2 * width, F32), mem_rows, mem_rows], time=10
        )
        state["memory_parts"] = mem_keep, flip(mem_send, "mem", 1)
        groups = [[(0, 0, 2 * half), (1, 0, 2 * half)], [(2, 0, 2 * width)]]
        yield from tree_side("wide", (own, other, ckv), groups, (18, 19, 20))

    def memory_grads_side():
        parts = yield 18, lambda: state["memory_parts"]
        rows = 4 * padded
        near, far = call(near_kernel, place, parts, [shape(rows, D, F32), shape(rows, D)], time=1)
        near, far = yield 20, lambda: (near, far)
        state["memory_sums"] = near, flip(far, "mem", 2)

    for name in ("hidden", "gain_three", "cout", "out", "cquery", "qkv"):
        state["grad_" + name] = []
    state["dmem"] = []
    quarter = [shape(tok, width), shape(tok, width), shape(2 * tok, width)]
    rounded, exact, column = shape(tok, D), shape(tok, D, F32), shape(tok, 1, F32)
    half_rows, whole, pair_rows = shape(tok, half), shape(group, D), shape(2 * tok, D)

    def far_pieces(pieces):
        return pieces[0], pieces[1], flip(pieces[2], "mem", 2)

    def stream(i):
        at = places[i]
        pieces = yield gathered
        qkv, kv_prev = call(
            functools.partial(qkv_kernel, i, tok), place, (*pieces, qkv_full),
            [shape(group, 3 * width), shape(group, 2 * width)], time=5,
        )
        if i == 0:
            qkv, kv_prev = yield Stay((qkv, kv_prev))
        self_o, self_lse = self_forward(at, qkv, kv_prev, blocks)
        self_lse = yield self_lse

        pieces = yield far_slots(self_o)
        self_low, after_self, plain_two, low_two, scale_two, *pieces = call(
            functools.partial(self_out_kernel, i), place,
            (*near_slots(*pieces), x_rows, state["wide_own"], state["wide_other"]),
            [rounded, exact, exact, rounded, column, *quarter], time=4,
        )
        scale_two = yield scale_two

        pieces = yield far_pieces(pieces)
        mem_kv, mem_prev = state["mem_kv"][i], state["mem_prev"][i]
        cross_o, cross_lse, cross_q = cross_forward(at, near_slots(*pieces), mem_prev, mem_kv, blocks, real)
        cross_lse = yield cross_lse

        pieces = yield far_slots(cross_o)
        cross_low, after_cross, plain_three, scale_three, low_three = call(
            cross_out_kernel, place,
            (*near_slots(*pieces), after_self, state["cout_own"], state["cout_other"], state["gain"]),
            [rounded, exact, exact, column, rounded], time=3,
        )
        scale_three = yield scale_three

        low_three, near, far = yield low_three, flip(low_three, "mem", 1), flip(low_three, "mem", 2)
        low_all, top_all, act, pre_low, grad_keep, grad_send, out_keep, out_send = call(
            functools.partial(mlp_kernel, i), place,
            (low_three, near, far, flip(far, "mem", 1), *state["top"], state["inner"], state["outer"]),
            [whole, whole, whole, whole, pair_rows, pair_rows, pair_rows, pair_rows], time=15,
        )
        state["grad_hidden"].append((pre_low, low_all, act, top_all))
        grad_keep, grad_send = yield grad_keep, grad_send

        near, far = near_sum(place, grad_keep, grad_send)
        far, out_send = yield flip(far, "mem", 2), out_send
        grad_after_cross, mine, others, gain_three, *pieces = call(
            functools.partial(cross_back_kernel, i), place,
            (near, far, plain_three, scale_three, state["gain"], tops, state["cout_own"], state["cout_other"]),
            [exact, half_rows, half_rows, shape(1, D, F32), *quarter], time=3,
        )
        state["grad_gain_three"].append(gain_three)
        state["grad_cout"].append((cross_low, mine, others))
        grad_after_cross = yield grad_after_cross

        pieces, out_send = yield far_pieces(pieces), out_send
        dcq, dmem_prev, dmem = cross_backward(
            at, cross_q, mem_prev, mem_kv, cross_o, near_slots(*pieces), cross_lse, blocks, real
        )
        out_near, out_far = near_sum(place, out_keep, out_send)
        dmem = yield dmem

        pieces, out_far = yield far_slots(dcq), out_far
        out_far = flip(out_far, "mem", 2)
        grad_after_self, query_mine, query_others, mine, others, *pieces = call(
            self_back_kernel, place,
            (*near_slots(*pieces), plain_two, scale_two, grad_after_cross, state["wide_own"], state["wide_other"]),
            [exact, half_rows, half_rows, half_rows, half_rows, *quarter], time=4,
        )
        state["grad_cquery"].append((low_two, query_mine, query_others))
        state["grad_out"].append((self_low, mine, others))
        state["dmem"].append((dmem, dmem_prev))
        grad_after_self = yield grad_after_self

        pieces, out_far = yield far_pieces(pieces), out_far
        pieces = near_slots(*pieces)
        if i == 0:
            pieces = yield Stay(pieces)
        dq, dkv, dkv_prev = self_backward(at, qkv, kv_prev, self_o, pieces, self_lse, blocks)
        grads = (*gathered, dq, dkv, dkv_prev)
        lows_scratch = [pltpu.VMEM((group, D), BF)] * 2
        if i == 0:
            grads = call(
                functools.partial(qkv_grads_kernel, i), place, grads, shape(D, 3 * width, F32),
                [*lows_scratch, pltpu.VMEM((D, 2 * width), F32)], time=6,
            )
            state["grad_qkv"].append(grads)
        else:
            grads = call(
                functools.partial(last_qkv_grads_kernel, i, seq_offsets(turned)), seq.reshape(1),
                (*grads, state["grad_qkv"][0]), [shape(D // 2, 3 * width, F32), shape(D // 2, 3 * width)],
                [*lows_scratch, pltpu.VMEM((D, 3 * width), F32)], time=7,
            )
        output = call(output_kernel, place, (after_cross, out_near, out_far), rounded)
        if i < MICRO - 1:
            back = call(qkv_back_kernel, place, (dq, dkv, dkv_prev, qkv_full), [pair_rows] * 4, time=5)
            back, state["grad_qkv"][0] = yield last_near(*back), grads
            back = yield last_far(*back)
        else:
            state["last_qkv"], dq, dkv, dkv_prev = yield grads, dq, dkv, dkv_prev
            back = call(qkv_back_kernel, place, (dq, dkv, dkv_prev, qkv_full), [pair_rows] * 4, time=5)
            yield ()
        return output, grad_after_self, back

    def last_near(keep, send, keep_prev, send_prev):
        return [near_sum(place, *pair) for pair in ((keep_prev, send_prev), (keep, send))]

    def last_far(*pairs):
        return [part for near, far in pairs for part in (near, flip(far, "mem", 2))]

    def back_rows(near_prev, far_prev, near, far):
        return shifted(call(far_sum_kernel, place, (near_prev, far_prev), rounded), -1)

    def final_rows(i, sums, back):
        grads = x_rows, done[i][1], sums[2], sums[3], back
        return call(functools.partial(grad_x_kernel, i), place, grads, exact)

    sides = [first_side(), memory_side(), top_side(), hidden_side(), cout_side(), wide_side(), memory_grads_side()]
    done = interleave([stream(i) for i in range(MICRO)], sides)

    def wide_finish(own):
        high = me >> 1
        rows_two = own.reshape(2, 2 * wrows, own.shape[1])
        theirs = lax.dynamic_index_in_dim(rows_two, 1 - high, 0, keepdims=False).astype(BF)
        own = lax.dynamic_index_in_dim(rows_two, high, 0, keepdims=False) + flip(theirs, "mem", 2).astype(F32)
        rows_two = own.reshape(2, wrows, own.shape[1])
        theirs = lax.dynamic_index_in_dim(rows_two, 1 - odd, 0, keepdims=False)
        own = lax.dynamic_index_in_dim(rows_two, odd, 0, keepdims=False)
        return own, flip(theirs.astype(BF), "mem", 1).astype(F32)

    def head_finish(summed, count):
        slots = summed.astype(BF).reshape(blocks, wrows, -1)
        first, second, *rest = [lax.dynamic_index_in_dim(slots, me ^ k, 0, keepdims=False) for k in range(4)]
        far = flip(jnp.concatenate(rest, axis=0), "mem", 2)
        own, near, far = near_slots(first, second, far)
        whole = join_pieces([own, near[:wrows], far[:wrows], near[wrows:]], me, 1).astype(F32)
        whole = whole.reshape(wrows, blocks, count, -1)
        return [whole[:, :, k].reshape(wrows, D) for k in range(count)]

    def seq_finish(pair, left):
        for bit in left:
            pair = seq_next(*pair, bit)
        return pair[0] + pair[1].astype(F32)

    tie = lax.optimization_barrier
    kept, sent = state["last_qkv"]
    qkv_pair = kept, flip(sent, "seq", order[0])
    sums = [done[0][2]]
    backs = [back_rows(*sums[0])]
    nears, memory_sums = tie((last_near(*done[1][2]), state["memory_sums"]))
    sums.append(last_far(*nears))
    qkv_pair, sums, backs, memory_sums, cout_pair = tie((qkv_pair, sums, backs, memory_sums, state["cout"]))
    qkv_pair = seq_next(*qkv_pair, order[1])
    backs.append(back_rows(*sums[1]))
    memory_near, memory_far = memory_sums
    both = call(far_sum_kernel, place, (memory_near, memory_far), shape(4 * padded, D))
    mem_own, mem_back = both[: 2 * padded], shifted(both[2 * padded :], -1)
    wide_pair, cout_pair = state["wide"], seq_next(*cout_pair, order[2])
    for bit in order[3:]:
        wide_pair, cout_pair = seq_next(*wide_pair, bit), seq_next(*cout_pair, bit)
    qkv_pair, wide_pair, cout_pair = tie((qkv_pair, wide_pair, cout_pair))
    qkv_pair = seq_next(*qkv_pair, order[2])
    for bit in order[3:]:
        qkv_pair = seq_next(*qkv_pair, bit)
    grad_rows = [final_rows(i, sums[i], backs[i]) for i in range(MICRO)]
    grad_mem = mem_own.reshape(MICRO, 1, padded, D).astype(F32) + mem_back.reshape(MICRO, 1, padded, D).astype(F32)
    grad_inner, grad_outer = state["hidden_grads"]
    own, near = wide_finish(seq_finish(cout_pair, []))
    grad_cout = join_halves(own[:, :half], near[:, :half])
    grad_gain_mlp = own[:, half] + near[:, half]
    last = seq_finish(wide_pair, [])
    grad_ckey, grad_cvalue = head_finish(last[:, 2 * half :], 2)
    own, near = wide_finish(last[:, : 2 * half])
    grad_out, plain_cquery = [
        join_halves(own[:, k * half : (k + 1) * half], near[:, k * half : (k + 1) * half]) for k in range(2)
    ]
    plain_qkv = head_finish(seq_finish(qkv_pair, []), 3)

    def gained(gain, weights, plains):
        scale = gain.astype(F32)[:, None]
        grad_gain = sum(jnp.sum(w.astype(F32) * p, axis=1) for w, p in zip(weights, plains))
        return grad_gain, [p * scale for p in plains]

    grad_gain_self, (grad_query, grad_key, grad_value) = gained(
        gain_self, (self_query, self_key, self_value), plain_qkv
    )
    grad_gain_cross, (grad_cquery,) = gained(gain_cross, (cross_query,), (plain_cquery,))
    return (
        jnp.stack([d[0] for d in done]),
        jnp.stack(grad_rows),
        grad_mem[:, :, :real],
        grad_gain_self,
        grad_query,
        grad_key,
        grad_value,
        grad_out,
        grad_gain_cross,
        grad_cquery,
        grad_ckey,
        grad_cvalue,
        grad_cout,
        grad_gain_mlp,
        grad_inner,
        grad_outer,
    )


def solution(mesh):
    rows = P(("seq", "mem"), None)
    tokens = P(None, ("seq", "mem"), None)
    pages = P(None, "seq", "mem", None)
    gains = P(("seq", "mem"))
    return jax.shard_map(
        shards,
        mesh=mesh,
        in_specs=(tokens, pages, P(), P(), tokens, gains, rows, rows, rows, rows, gains, rows, rows, rows, rows,
                  gains, rows, rows),
        out_specs=(tokens, tokens, pages, gains, rows, rows, rows, rows, gains, rows, rows, rows, rows, gains,
                   rows, rows),
        check_vma=False,
    )
```
